32 devices in a mesh: batch: 8 (over z, x), tensor: 4 (over y, core).
Axes of the slice: x: 2, y: 2, z: 4, core: 2. Of those that a mesh axis runs over, the one named last changes fastest.
Arguments:
- inputs: bfloat16 [16384, 1024], P('batch'), may hold values from -6 to 6
- buckets: int32 [16], P('batch'), may hold values from 0 to 1
- ln1_gain: float32 [1024], replicated, may hold values from 0.1 to 1.9
- ln1_bias: float32 [1024], replicated, may hold values from -2 to 2
- w_qkv: bfloat16 [1024, 3, 1024], P(None, None, 'tensor'), may hold values from -0.1875 to 0.1875
- w_out: bfloat16 [1024, 1024], P('tensor'), may hold values from -1 to 1
- ln2_gain: float32 [1024], replicated, may hold values from 0.1 to 1.9
- ln2_bias: float32 [1024], replicated, may hold values from -2 to 2
- w_up: bfloat16 [1024, 4096], P(None, 'tensor'), may hold values from -0.1875 to 0.1875
- w_down: bfloat16 [4096, 1024], P('tensor'), may hold values from -0.09375 to 0.09375
- prefix_embed: bfloat16 [10, 1024], replicated, may hold values from -6 to 6
- prefix_w1: bfloat16 [1024, 512], replicated, may hold values from -0.1875 to 0.1875
- prefix_b1: float32 [512], replicated, may hold values from -3 to 3
- prefix_w2: bfloat16 [512, 2, 1024], P(None, None, 'tensor'), may hold values from -0.25 to 0.25
- prefix_b2: float32 [2, 1024], P(None, 'tensor'), may hold values from -3 to 3
- cotangent: bfloat16 [16384, 1024], P('batch'), may hold values from -6 to 6
Outputs:
- output: bfloat16 [16384, 1024], P(('batch', 'tensor'))
- input_grad: float32 [16384, 1024], P(('batch', 'tensor'))
- embed_grad: float32 [10, 1024], replicated
- w1_grad: float32 [1024, 512], replicated
- b1_grad: float32 [512], replicated
- w2_grad: float32 [512, 2, 1024], P(None, None, 'tensor')
- b2_grad: float32 [2, 1024], P(None, 'tensor')
The draws below stay inside these ranges and needn't reach their ends.
Inputs may be any that keep to these rules, and one draw needn't show every extreme that they name: `buckets`: 0 marks a slot of short sequences, 1 a slot holding one long sequence.
All inputs are finite; a program needn't handle non-finite values.
Results may differ from the reference program's by a relative error of at most 0.017.
Values may be sent and summed in bfloat16 or wider, within the bound.
No kernel may reach another device: no remote copies, remote signals or barrier semaphores. Data moves between devices by JAX's collectives and lax.ppermute only.
A program may use at most 192 MiB of HBM per device.

```python
import jax
import jax.numpy as jnp
from jax import lax

D = 1024
H = 16
HD = 64
FF = 4096
P_SIZE = 10
R = 512
SEQ = 1024
SEG = 256
SLOTS = 16
TOKENS = 16384
N_TENSOR = 4


def place_ends(values, rng, smallest, top_value):
    shape = values.shape
    index_at = [jax.random.randint(jax.random.fold_in(rng, axis), (), 0, shape[axis]) for axis in range(len(shape))]
    values = values.at[tuple(index_at)].set(smallest)
    longest = shape.index(max(shape))
    index_at[longest] = (index_at[longest] + 1) % shape[longest]
    return values.at[tuple(index_at)].set(top_value)


def shard_levels(own_key, dims, shards, smallest, largest):
    factor_of = 1.0
    for dim, blocks in shards:
        heights = jax.random.uniform(jax.random.fold_in(jax.random.fold_in(own_key, 6), dim), (blocks,), jnp.float32, smallest / len(shards), largest / len(shards))
        factor_of = factor_of * jnp.repeat(jnp.exp(heights), dims[dim] // blocks).reshape((-1,) + (1,) * (len(dims) - 1 - dim))
    return factor_of


def bell_draw(rng, dims, spread, limit, split=(), kind=jnp.bfloat16):
    drawn = spread * jax.random.normal(rng, dims, jnp.float32)
    if split:
        drawn = drawn * shard_levels(rng, dims, split, -0.22, 0.18)
    return jnp.clip(drawn, -limit, limit).astype(kind)


def setup_inputs(seed: int = 0) -> dict:
    keys = jax.random.split(jax.random.key(seed), 17)
    inputs = bell_draw(keys[0], (TOKENS, D), 1.0, 6.0, ((0, 8),))
    buckets = place_ends(jax.random.randint(keys[1], (SLOTS,), 0, 2), jax.random.fold_in(keys[1], 1), 0, 1).astype(jnp.int32)
    ln1_gain = jnp.clip(1.0 + 0.18 * jax.random.normal(keys[2], (D,), jnp.float32), 0.1, 1.9)
    ln1_bias = bell_draw(keys[3], (D,), 0.3, 2.0, (), jnp.float32)
    w_qkv = bell_draw(keys[4], (D, 3, D), D ** -0.5, 0.1875, ((2, 4),))
    w_out = bell_draw(keys[5], (D, D), (D // 32) ** -0.5, 1.0, ((0, 4),))
    ln2_gain = jnp.clip(1.0 + 0.18 * jax.random.normal(keys[6], (D,), jnp.float32), 0.1, 1.9)
    ln2_bias = bell_draw(keys[7], (D,), 0.3, 2.0, (), jnp.float32)
    w_up = bell_draw(keys[8], (D, FF), D ** -0.5, 0.1875, ((1, 4),))
    w_down = bell_draw(keys[9], (FF, D), FF ** -0.5, 0.09375, ((0, 4),))
    prefix_embed = bell_draw(keys[10], (P_SIZE, D), 1.0, 6.0)
    prefix_w1 = bell_draw(keys[11], (D, R), D ** -0.5, 0.1875)
    prefix_b1 = bell_draw(keys[12], (R,), 0.5, 3.0, (), jnp.float32)
    prefix_w2 = bell_draw(keys[13], (R, 2, D), R ** -0.5, 0.25, ((2, 4),))
    prefix_b2 = bell_draw(keys[14], (2, D), 0.5, 3.0, ((1, 4),), jnp.float32)
    cotangent = bell_draw(keys[15], (TOKENS, D), 1.0, 6.0, ((0, 8),))
    return {"inputs": inputs, "buckets": buckets, "ln1_gain": ln1_gain, "ln1_bias": ln1_bias, "w_qkv": w_qkv, "w_out": w_out, "ln2_gain": ln2_gain, "ln2_bias": ln2_bias, "w_up": w_up, "w_down": w_down, "prefix_embed": prefix_embed, "prefix_w1": prefix_w1, "prefix_b1": prefix_b1, "prefix_w2": prefix_w2, "prefix_b2": prefix_b2, "cotangent": cotangent}


precise = lax.Precision.HIGHEST

@jax.custom_vjp
def low(v):
    return lax.optimization_barrier(v.astype(jnp.bfloat16)).astype(jnp.float32)

@jax.custom_vjp
def low_back(v):
    return v

def low_keep(v):
    return (low(v), None)

def low_pass(kept, grad):
    return (grad,)

def back_keep(v):
    return (v, None)

def back_low(kept, grad):
    return (low(grad),)
low.defvjp(low_keep, low_pass)
low_back.defvjp(back_keep, back_low)

def matmul(left_side, right_side):
    return jnp.dot(left_side, right_side, precision=precise)

def layer_norm(values, norm_gain, norm_bias):
    average = lax.optimization_barrier(jnp.mean(values, axis=-1, keepdims=True))
    centred = values - average
    variance = lax.optimization_barrier(jnp.mean(centred * centred, axis=-1, keepdims=True))
    return centred * lax.rsqrt(variance + 1e-05) * norm_gain + norm_bias

def slot_mask(bucket):
    positions = jnp.arange(SEQ, dtype=jnp.int32)
    seg_span = jnp.where(bucket == 1, SEQ, SEG).astype(jnp.int32)
    causal = positions[None, :] <= positions[:, None]
    return causal & (positions[:, None] // seg_span == positions[None, :] // seg_span)

def slot_block(slot_rows, bucket, prefix_keys, prefix_values, frozen):
    ln1_gain, ln1_bias, w_qkv, w_out, ln2_gain, ln2_bias, w_up, w_down = frozen
    normed_in = low(layer_norm(slot_rows, ln1_gain, ln1_bias))
    projected = matmul(normed_in, w_qkv.reshape(D, 3 * D)).reshape(SEQ, 3, H, HD)
    queries = low(low_back(projected[:, 0]))
    key_rows = low(low_back(projected[:, 1]))
    value_rows = low(low_back(projected[:, 2]))
    prefix_scores = jnp.einsum('ihd,phd->hip', queries, prefix_keys, precision=precise) / 8.0
    inner_scores = jnp.einsum('ihd,jhd->hij', queries, key_rows, precision=precise) / 8.0
    scores = low_back(jnp.concatenate([prefix_scores, inner_scores], axis=-1))
    allowed = jnp.concatenate([jnp.ones((SEQ, P_SIZE), jnp.bool_), slot_mask(bucket)], axis=-1)
    scores = jnp.where(allowed[None], scores, -1000000000.0)
    row_top = lax.optimization_barrier(jnp.max(scores, axis=-1, keepdims=True))
    weights = jnp.exp(scores - row_top)
    weights = low(weights / lax.optimization_barrier(jnp.sum(weights, axis=-1, keepdims=True)))
    all_values = jnp.concatenate([prefix_values, value_rows], axis=0)
    mixed_heads = jnp.einsum('hij,jhd->ihd', weights, all_values, precision=precise)
    mixed_heads = low(low_back(mixed_heads)).reshape(SEQ, N_TENSOR, D // N_TENSOR)
    attn_parts = jnp.einsum('sgc,gcd->gsd', mixed_heads, w_out.reshape(N_TENSOR, D // N_TENSOR, D), precision=precise)
    middle = slot_rows + low_back(lax.optimization_barrier(jnp.sum(low(attn_parts), axis=0)))
    normed_mid = low(layer_norm(middle, ln2_gain, ln2_bias))
    hidden_pre = low_back(matmul(normed_mid, w_up))
    activated = low(jax.nn.gelu(hidden_pre, approximate=True)).reshape(SEQ, N_TENSOR, FF // N_TENSOR)
    mlp_parts = jnp.einsum('sgc,gcd->gsd', activated, w_down.reshape(N_TENSOR, FF // N_TENSOR, D), precision=precise)
    return middle + low_back(lax.optimization_barrier(jnp.sum(low(mlp_parts), axis=0)))

def reference(inputs, buckets, ln1_gain, ln1_bias, w_qkv, w_out, ln2_gain, ln2_bias, w_up, w_down, prefix_embed, prefix_w1, prefix_b1, prefix_w2, prefix_b2, cotangent):
    frozen = tuple((weight_in.astype(jnp.float32) for weight_in in (ln1_gain, ln1_bias, w_qkv, w_out, ln2_gain, ln2_bias, w_up, w_down)))

    def forward(residual, embedding, reparam_w1, reparam_b1, reparam_w2, reparam_b2):
        hidden = jnp.tanh(matmul(embedding, reparam_w1) + reparam_b1)
        prefix_kv = low(matmul(hidden, reparam_w2.reshape(R, 2 * D)).reshape(P_SIZE, 2, D) + reparam_b2)
        prefix_pair = (prefix_kv[:, 0].reshape(P_SIZE, H, HD), prefix_kv[:, 1].reshape(P_SIZE, H, HD))

        def slot_step(prefix_state, slot_item):
            return (prefix_state, slot_block(slot_item[0], slot_item[1], prefix_state[0], prefix_state[1], frozen))
        _, blocks_out = lax.scan(jax.checkpoint(slot_step), prefix_pair, (residual.reshape(-1, SEQ, D), buckets))
        return blocks_out.reshape(-1, D)
    result, pull_back = jax.vjp(forward, inputs.astype(jnp.float32), prefix_embed.astype(jnp.float32), prefix_w1.astype(jnp.float32), prefix_b1, prefix_w2.astype(jnp.float32), prefix_b2)
    grads = pull_back(cotangent.astype(jnp.float32))
    return (result.astype(jnp.bfloat16), grads[0], grads[1], grads[2], grads[3], grads[4], grads[5])
```

```python
import functools

import jax
import jax.numpy as jnp
from jax import lax
from jax.experimental import pallas as pl
from jax.experimental.pallas import tpu as pltpu
from jax.sharding import PartitionSpec as P

D = 1024
HD = 64
SEQ = 1024
SEG = 256
HEADS = 4
COLS = HEADS * HD
BLK = 256
NBLK = SEQ // BLK
LANES = HEADS * BLK
PREFIX_ROWS = 16
LOG2E = 1.4426950408889634
SCALE = 0.125
FAR = -1e30
MASKED = -1e9
MIB = 1 << 20

f32 = jnp.float32
bf16 = jnp.bfloat16
precise = lax.Precision.HIGHEST


def dot_nn(a, b):
    return lax.dot_general(a, b, (((1,), (0,)), ((), ())), preferred_element_type=f32)


def dot_nt(a, b):
    return lax.dot_general(a, b, (((1,), (1,)), ((), ())), preferred_element_type=f32)


def exact(a, b, dims):
    return lax.dot_general(a, b, (dims, ((), ())), precision=precise, preferred_element_type=f32)


def norm_rows(values):
    average = jnp.mean(values, axis=-1, keepdims=True)
    centred = values - average
    inv = lax.rsqrt(jnp.mean(centred * centred, axis=-1, keepdims=True) + 1e-05)
    return centred * inv, inv


def norm_back(incoming, normed, inv, gain):
    scaled = incoming * gain
    return inv * (
        scaled
        - jnp.mean(scaled, axis=-1, keepdims=True)
        - normed * jnp.mean(scaled * normed, axis=-1, keepdims=True)
    )


def head_stack(rows):
    lane_head = lax.broadcasted_iota(jnp.int32, rows.shape, 1) // HD
    return jnp.concatenate(
        [jnp.where(lane_head == h, rows, jnp.zeros_like(rows)) for h in range(HEADS)], axis=0
    )


def head_lanes(h):
    return slice(h * BLK, (h + 1) * BLK)


def head_rows(h):
    return slice(h * HD, (h + 1) * HD)


def fetch(copies):
    for copy in copies:
        copy.start()
    for copy in copies:
        copy.wait()


def piece_copies(place, pieces, target, sems, first):
    rows = target.shape[0] // 4
    return [
        pltpu.make_async_copy(
            piece, target.at[pl.ds(pl.multiple_of((place ^ k) * rows, rows), rows)], sems.at[first + k]
        )
        for k, piece in enumerate(pieces)
    ]


def prefix_kernel(embed, w1, b1, w2, b2, hidden_out, kv_out):
    hidden = jnp.tanh(dot_nn(embed[...], w1[...]) + b1[...])
    kv = exact(hidden, w2[...].astype(f32), ((1,), (0,))) + b2[...]
    real = lax.broadcasted_iota(jnp.int32, kv.shape, 0) < 10
    kv = jnp.where(real, kv, 0.0)
    hidden_out[...] = hidden
    kv_out[...] = jnp.concatenate([kv[:, :COLS], kv[:, COLS:]], axis=0).astype(bf16)


def prefix_forward(embed, w1, b1, w2, b2):
    width = w1.shape[1]
    return pl.pallas_call(
        prefix_kernel,
        out_shape=(
            jax.ShapeDtypeStruct((PREFIX_ROWS, width), f32),
            jax.ShapeDtypeStruct((2 * PREFIX_ROWS, COLS), bf16),
        ),
        name="prefix_forward",
    )(embed, w1, b1, w2, b2)


def attend_kernel(
    peer, where, x, gain, bias, *rest
):
    if peer:
        q_pieces, o_pieces, rest = rest[:4], rest[4:8], rest[8:]
        kv, _, _, _, _, _ = rest[:6]
        rest = rest[6:]
    else:
        w_ref, wo_ref, kv = rest[:3]
        rest = rest[3:]
    proj_out, o_out, e_out, ep_out, inv_out, part_out = rest[:6]
    if peer:
        k_all, vt_all, w_ref, wo_ref, sems = rest[6:]
    else:
        k_all, vt_all = rest[6:]
    i = pl.program_id(0)
    bucket = where[1]
    if peer:

        @pl.when(i == 0)
        def _():
            fetch(
                piece_copies(where[2], q_pieces, w_ref, sems, 0)
                + piece_copies(where[2], o_pieces, wo_ref, sems, 4)
            )

    normed, _ = norm_rows(x[...].astype(f32))
    u1 = (normed * gain[...] + bias[...]).astype(bf16)
    proj = dot_nn(u1, w_ref[...])
    low = proj.astype(bf16)
    proj_out[0] = low
    here = pl.ds(pl.multiple_of(i * BLK, BLK), BLK)
    k_all[here, :] = low[:, COLS : 2 * COLS]
    vt_all[:, here] = proj[:, 2 * COLS :].T.astype(bf16)
    q_stack = head_stack(low[:, :COLS])
    keep = (lax.broadcasted_iota(jnp.int32, (BLK, LANES), 0)) <= (
        lax.broadcasted_iota(jnp.int32, (BLK, LANES), 1) % BLK
    )
    real = lax.broadcasted_iota(jnp.int32, (PREFIX_ROWS, LANES), 0) < 10

    def attend(start, count):
        scores = []
        for c in range(count):
            keys = k_all[pl.ds(start + c * BLK, BLK), :]
            block = dot_nt(keys, q_stack)
            if c == count - 1:
                block = jnp.where(keep, block, MASKED)
            scores.append(block)
        prefix = jnp.where(real, dot_nt(kv[:PREFIX_ROWS], q_stack), FAR)
        top = jnp.max(prefix, axis=0, keepdims=True)
        for block in scores:
            top = jnp.maximum(top, jnp.max(block, axis=0, keepdims=True))
        shift = top * (SCALE * LOG2E)
        e_prefix = jnp.exp2(prefix * (SCALE * LOG2E) - shift)
        total = jnp.sum(e_prefix, axis=0, keepdims=True)
        ep_low = e_prefix.astype(bf16)
        ep_out[0, 0] = ep_low
        mixed = [
            dot_nn(
                kv[PREFIX_ROWS:].astype(f32).T.astype(bf16)[head_rows(h)], ep_low[:, head_lanes(h)]
            )
            for h in range(HEADS)
        ]
        for c, block in enumerate(scores):
            e = jnp.exp2(block * (SCALE * LOG2E) - shift)
            total = total + jnp.sum(e, axis=0, keepdims=True)
            e_low = e.astype(bf16)
            e_out[0, 0, c * BLK : (c + 1) * BLK, :] = e_low
            for h in range(HEADS):
                mixed[h] = mixed[h] + dot_nn(
                    vt_all[head_rows(h), pl.ds(start + c * BLK, BLK)], e_low[:, head_lanes(h)]
                )
        inv = 1.0 / total
        inv_out[0, 0] = inv
        o = jnp.concatenate([mixed[h] * inv[:, head_lanes(h)] for h in range(HEADS)], axis=0)
        o_low = o.T.astype(bf16)
        o_out[0] = o_low
        part_out[...] = dot_nn(o_low, wo_ref[...]).astype(bf16)

    @pl.when(jnp.logical_or(bucket == 0, i == 0))
    def _():
        attend(pl.multiple_of(i * BLK, BLK), 1)

    for count in range(2, NBLK + 1):

        @pl.when(jnp.logical_and(bucket != 0, i == count - 1))
        def _():
            attend(0, count)


def attend(where, x, gain, bias, weights, kv, saved=None):
    peer = saved is not None
    group = 1 if peer else 0
    row = pl.BlockSpec((1, D), lambda i, s: (0, 0))
    any_spec = pl.BlockSpec(memory_space=pl.ANY)
    specs = [pl.BlockSpec((BLK, D), lambda i, s: (s[0] * NBLK + i, 0)), row, row]
    args = [x, gain, bias]
    scratch = [pltpu.VMEM((SEQ, COLS), bf16), pltpu.VMEM((COLS, SEQ), bf16)]
    aliases = {}
    if peer:
        q_pieces, o_pieces = weights
        args += [*q_pieces, *o_pieces, kv, *saved]
        specs += [any_spec] * 8 + [pl.BlockSpec(kv.shape, lambda i, s: (0, 0))] + [any_spec] * 5
        scratch += [
            pltpu.VMEM((D, 3 * COLS), bf16),
            pltpu.VMEM((COLS, D), bf16),
            pltpu.SemaphoreType.DMA((8,)),
        ]
        aliases = {1 + 3 + 8 + 1 + k: k for k in range(5)}
    else:
        w, wo = weights
        args += [w, wo, kv]
        specs += [pl.BlockSpec(a.shape, lambda i, s: (0, 0)) for a in (w, wo, kv)]
    out_shape = (
        jax.ShapeDtypeStruct((2, SEQ, 3 * COLS), bf16),
        jax.ShapeDtypeStruct((2, SEQ, COLS), bf16),
        jax.ShapeDtypeStruct((2, NBLK, SEQ, LANES), bf16),
        jax.ShapeDtypeStruct((2, NBLK, PREFIX_ROWS, LANES), bf16),
        jax.ShapeDtypeStruct((2, NBLK, 1, LANES), f32),
        jax.ShapeDtypeStruct((SEQ, D), bf16),
    )
    out_specs = (
        pl.BlockSpec((1, BLK, 3 * COLS), lambda i, s: (group, i, 0)),
        pl.BlockSpec((1, BLK, COLS), lambda i, s: (group, i, 0)),
        pl.BlockSpec((1, 1, SEQ, LANES), lambda i, s: (group, i, 0, 0)),
        pl.BlockSpec((1, 1, PREFIX_ROWS, LANES), lambda i, s: (group, i, 0, 0)),
        pl.BlockSpec((1, 1, 1, LANES), lambda i, s: (group, i, 0, 0)),
        pl.BlockSpec((BLK, D), lambda i, s: (i, 0)),
    )
    return pl.pallas_call(
        functools.partial(attend_kernel, peer),
        grid_spec=pltpu.PrefetchScalarGridSpec(
            num_scalar_prefetch=1,
            grid=(NBLK,),
            in_specs=specs,
            out_specs=out_specs,
            scratch_shapes=scratch,
        ),
        out_shape=out_shape,
        input_output_aliases=aliases,
        compiler_params=pltpu.CompilerParams(vmem_limit_bytes=48 * MIB),
        name="attend_peer" if peer else "attend_own",
    )(where, *args)


def unit_block(u2, dy, up, down):
    k = 0.7978845608028654
    f = dot_nn(u2, up)
    da = dot_nt(dy, down)
    square = f * f
    t = jnp.tanh(f * (k + (k * 0.044715) * square))
    half = 0.5 * t + 0.5
    g = f * half
    slope = half + g * (1.0 - half) * (2 * k + (6 * k * 0.044715) * square)
    df = (da * slope).astype(bf16)
    return dot_nn(g.astype(bf16), down), dot_nt(df, up)


def mlp_own_kernel(where, x, p0, p1, p2, p3, gain, bias, dy, up, down, h1_out, u2_out, m_out, du_out):
    h1 = x[...].astype(f32) + (
        (p0[...].astype(f32) + p1[...].astype(f32)) + (p2[...].astype(f32) + p3[...].astype(f32))
    )
    h1_out[...] = h1
    normed, _ = norm_rows(h1)
    u2 = (normed * gain[...] + bias[...]).astype(bf16)
    u2_out[...] = u2
    m, du = unit_block(u2, dy[...], up[...], down[...])
    m_out[...] = m
    du_out[...] = du


def mlp_own(where, x, parts, gain, bias, dy, up, down):
    row = pl.BlockSpec((1, D), lambda i, s: (0, 0))
    slot = pl.BlockSpec((BLK, D), lambda i, s: (s[0] * NBLK + i, 0))
    block = pl.BlockSpec((BLK, D), lambda i, s: (i, 0))
    full = lambda a: pl.BlockSpec(a.shape, lambda i, s: (0, 0))
    return pl.pallas_call(
        mlp_own_kernel,
        grid_spec=pltpu.PrefetchScalarGridSpec(
            num_scalar_prefetch=1,
            grid=(NBLK,),
            in_specs=[slot] + [block] * 4 + [row, row, slot, full(up), full(down)],
            out_specs=[block] * 4,
        ),
        out_shape=(
            jax.ShapeDtypeStruct((SEQ, D), f32),
            jax.ShapeDtypeStruct((SEQ, D), bf16),
            jax.ShapeDtypeStruct((SEQ, D), f32),
            jax.ShapeDtypeStruct((SEQ, D), f32),
        ),
        compiler_params=pltpu.CompilerParams(vmem_limit_bytes=48 * MIB),
        name="mlp_own",
    )(where, x, *parts, gain, bias, dy, up, down)


def mlp_peer_kernel(where, u2, dy, m_in, du_in, *rest):
    u_pieces, d_pieces = rest[:4], rest[4:8]
    m_out, du_out, up, down, sems = rest[8:]

    @pl.when(pl.program_id(0) == 0)
    def _():
        fetch(
            piece_copies(where[2], u_pieces, up, sems, 0)
            + piece_copies(where[2], d_pieces, down, sems, 4)
        )

    m, du = unit_block(u2[...], dy[...], up[...], down[...])
    m_out[...] = (m_in[...] + m).astype(bf16)
    du_out[...] = (du_in[...] + du).astype(bf16)


def mlp_peer(where, u2, dy, m, du, u_pieces, d_pieces):
    slot = pl.BlockSpec((BLK, D), lambda i, s: (s[0] * NBLK + i, 0))
    block = pl.BlockSpec((BLK, D), lambda i, s: (i, 0))
    any_spec = pl.BlockSpec(memory_space=pl.ANY)
    units = 4 * d_pieces[0].shape[0]
    return pl.pallas_call(
        mlp_peer_kernel,
        grid_spec=pltpu.PrefetchScalarGridSpec(
            num_scalar_prefetch=1,
            grid=(NBLK,),
            in_specs=[block, slot, block, block] + [any_spec] * 8,
            out_specs=[block] * 2,
            scratch_shapes=[
                pltpu.VMEM((D, units), bf16),
                pltpu.VMEM((units, D), bf16),
                pltpu.SemaphoreType.DMA((8,)),
            ],
        ),
        out_shape=(
            jax.ShapeDtypeStruct((SEQ, D), bf16),
            jax.ShapeDtypeStruct((SEQ, D), bf16),
        ),
        compiler_params=pltpu.CompilerParams(vmem_limit_bytes=48 * MIB),
        name="mlp_peer",
    )(where, u2, dy, m, du, *u_pieces, *d_pieces)


def turn_kernel(where, du_own, du_sib, h1, dy, gain, wo_own, *rest):
    o_pieces = rest[:4]
    dh_out, do_out, wo_peer, sems = rest[4:]

    @pl.when(pl.program_id(0) == 0)
    def _():
        fetch(piece_copies(where[2], o_pieces, wo_peer, sems, 0))

    normed, inv = norm_rows(h1[...])
    du = du_own[...].astype(f32) + du_sib[...].astype(f32)
    dh = dy[...].astype(f32) + norm_back(du, normed, inv, gain[...])
    dh_out[...] = dh
    low = dh.astype(bf16)
    do_out[0] = dot_nt(low, wo_own[...]).astype(bf16)
    do_out[1] = dot_nt(low, wo_peer[...]).astype(bf16)


def turn(where, du_own, du_sib, h1, dy, gain, wo_own, o_pieces):
    slot = pl.BlockSpec((BLK, D), lambda i, s: (s[0] * NBLK + i, 0))
    block = pl.BlockSpec((BLK, D), lambda i, s: (i, 0))
    row = pl.BlockSpec((1, D), lambda i, s: (0, 0))
    any_spec = pl.BlockSpec(memory_space=pl.ANY)
    return pl.pallas_call(
        turn_kernel,
        grid_spec=pltpu.PrefetchScalarGridSpec(
            num_scalar_prefetch=1,
            grid=(NBLK,),
            in_specs=[block, block, block, slot, row, pl.BlockSpec((COLS, D), lambda i, s: (0, 0))]
            + [any_spec] * 4,
            out_specs=[block, pl.BlockSpec((2, BLK, COLS), lambda i, s: (0, i, 0))],
            scratch_shapes=[pltpu.VMEM((COLS, D), bf16), pltpu.SemaphoreType.DMA((4,))],
        ),
        out_shape=(
            jax.ShapeDtypeStruct((SEQ, D), f32),
            jax.ShapeDtypeStruct((2, SEQ, COLS), bf16),
        ),
        compiler_params=pltpu.CompilerParams(vmem_limit_bytes=32 * MIB),
        name="turn",
    )(where, du_own, du_sib, h1, dy, gain, wo_own, *o_pieces)


def attend_back_kernel(
    where, proj, proj_all, o, do, e, ep, inv, kv, w_own, *rest
):
    q_pieces = rest[:4]
    du_out, dkv_out, kt_all, dk_all, dv_all, du_acc, w_peer, sems = rest[4:]
    j, g = pl.program_id(0), pl.program_id(1)
    i = NBLK - 1 - j
    bucket = where[1]

    @pl.when(jnp.logical_and(j == 0, g == 0))
    def _():
        fetch(piece_copies(where[2], q_pieces, w_peer, sems, 0))

    @pl.when(j == 0)
    def _():
        kt_all[g] = proj_all[0, :, COLS : 2 * COLS].astype(f32).T.astype(bf16)
        dk_all[g] = jnp.zeros((SEQ, COLS), f32)
        dv_all[g] = jnp.zeros((SEQ, COLS), f32)
        dkv_out[g] = jnp.zeros((2 * PREFIX_ROWS, COLS), f32)

    inv_row = inv[0, 0]
    do_wide = do[0].astype(f32)
    product = (do_wide * o[0].astype(f32)).T
    balance = (
        jnp.concatenate(
            [jnp.sum(product[head_rows(h)], axis=0, keepdims=True) for h in range(HEADS)], axis=1
        )
        * inv_row
    )
    inv_wide = jnp.concatenate(
        [jnp.broadcast_to(inv_row[:, head_lanes(h)], (HD, BLK)) for h in range(HEADS)], axis=0
    ).T
    do_stack = head_stack((do_wide * inv_wide).astype(bf16))
    q_stack = head_stack(proj[0, :, :COLS])

    ep_low = ep[0, 0]
    ds_prefix = (
        ep_low.astype(f32) * (dot_nt(kv[0, PREFIX_ROWS:], do_stack) - balance)
    ).astype(bf16)
    dkv_out[g] = dkv_out[g] + jnp.concatenate(
        [dot_nn(ds_prefix, q_stack) * SCALE, dot_nn(ep_low, do_stack)], axis=0
    )
    pk_t = kv[0, :PREFIX_ROWS].astype(f32).T.astype(bf16)

    def back(start, count):
        dq = [dot_nn(pk_t[head_rows(h)], ds_prefix[:, head_lanes(h)]) for h in range(HEADS)]
        for c in range(count):
            rows = pl.ds(start + c * BLK, BLK)
            e_low = e[0, 0, c * BLK : (c + 1) * BLK, :]
            dp = dot_nt(proj_all[0, rows, 2 * COLS :], do_stack)
            ds = (e_low.astype(f32) * (dp - balance)).astype(bf16)
            dv_all[g, rows, :] = dv_all[g, rows, :] + dot_nn(e_low, do_stack)
            dk_all[g, rows, :] = dk_all[g, rows, :] + dot_nn(ds, q_stack)
            for h in range(HEADS):
                dq[h] = dq[h] + dot_nn(kt_all[g, head_rows(h), rows], ds[:, head_lanes(h)])
        here = pl.ds(pl.multiple_of(i * BLK, BLK), BLK)
        dq_low = (jnp.concatenate(dq, axis=0).T * SCALE).astype(bf16)
        dk_low = (dk_all[g, here, :] * SCALE).astype(bf16)
        dv_low = dv_all[g, here, :].astype(bf16)
        grads = jnp.concatenate([dq_low, dk_low, dv_low], axis=1)

        @pl.when(g == 0)
        def _():
            du_acc[...] = dot_nt(grads, w_own[...])

        @pl.when(g == 1)
        def _():
            du_out[...] = (du_acc[...] + dot_nt(grads, w_peer[...])).astype(bf16)

    @pl.when(jnp.logical_or(bucket == 0, i == 0))
    def _():
        back(pl.multiple_of(i * BLK, BLK), 1)

    for count in range(2, NBLK + 1):

        @pl.when(jnp.logical_and(bucket != 0, i == count - 1))
        def _():
            back(0, count)


def attend_back(where, proj, o, do, e, ep, inv, kv, w_own, q_pieces):
    any_spec = pl.BlockSpec(memory_space=pl.ANY)
    rows = lambda width: pl.BlockSpec((1, BLK, width), lambda j, g, s: (g, NBLK - 1 - j, 0))
    block = lambda a, b: pl.BlockSpec((1, 1, a, b), lambda j, g, s: (g, NBLK - 1 - j, 0, 0))
    return pl.pallas_call(
        attend_back_kernel,
        grid_spec=pltpu.PrefetchScalarGridSpec(
            num_scalar_prefetch=1,
            grid=(NBLK, 2),
            in_specs=[
                rows(3 * COLS),
                pl.BlockSpec((1, SEQ, 3 * COLS), lambda j, g, s: (g, 0, 0)),
                rows(COLS),
                rows(COLS),
                block(SEQ, LANES),
                block(PREFIX_ROWS, LANES),
                block(1, LANES),
                pl.BlockSpec((1, 2 * PREFIX_ROWS, COLS), lambda j, g, s: (g, 0, 0)),
                pl.BlockSpec(w_own.shape, lambda j, g, s: (0, 0)),
            ]
            + [any_spec] * 4,
            out_specs=[
                pl.BlockSpec((BLK, D), lambda j, g, s: (NBLK - 1 - j, 0)),
                pl.BlockSpec((2, 2 * PREFIX_ROWS, COLS), lambda j, g, s: (0, 0, 0)),
            ],
            scratch_shapes=[
                pltpu.VMEM((2, COLS, SEQ), bf16),
                pltpu.VMEM((2, SEQ, COLS), f32),
                pltpu.VMEM((2, SEQ, COLS), f32),
                pltpu.VMEM((BLK, D), f32),
                pltpu.VMEM((D, 3 * COLS), bf16),
                pltpu.SemaphoreType.DMA((4,)),
            ],
        ),
        out_shape=(
            jax.ShapeDtypeStruct((SEQ, D), bf16),
            jax.ShapeDtypeStruct((2, 2 * PREFIX_ROWS, COLS), f32),
        ),
        compiler_params=pltpu.CompilerParams(vmem_limit_bytes=56 * MIB),
        name="attend_back",
    )(where, proj, proj, o, do, e, ep, inv, kv, w_own, *q_pieces)


def finish_kernel(where, du_own, du_sib, x, dh, gain, grad_out):
    normed, inv = norm_rows(x[...].astype(f32))
    du = du_own[...].astype(f32) + du_sib[...].astype(f32)
    grad_out[...] = dh[...] + norm_back(du, normed, inv, gain[...])


def finish(where, du_own, du_sib, x, dh, gain):
    half = SEQ // 2 // BLK
    mine = pl.BlockSpec((BLK, D), lambda i, s: (s[3] * half + i, 0))
    slot = pl.BlockSpec((BLK, D), lambda i, s: (s[0] * NBLK + s[3] * half + i, 0))
    block = pl.BlockSpec((BLK, D), lambda i, s: (i, 0))
    row = pl.BlockSpec((1, D), lambda i, s: (0, 0))
    return pl.pallas_call(
        finish_kernel,
        grid_spec=pltpu.PrefetchScalarGridSpec(
            num_scalar_prefetch=1,
            grid=(half,),
            in_specs=[mine, block, slot, mine, row],
            out_specs=block,
        ),
        out_shape=jax.ShapeDtypeStruct((SEQ // 2, D), f32),
        name="finish",
    )(where, du_own, du_sib, x, dh, gain)


def result_kernel(where, h1, m_own, m_sib, out):
    out[...] = (h1[...] + (m_own[...].astype(f32) + m_sib[...].astype(f32))).astype(bf16)


def result(where, h1, m_own, m_sib):
    half = SEQ // 2 // BLK
    mine = pl.BlockSpec((BLK, D), lambda i, s: (s[3] * half + i, 0))
    block = pl.BlockSpec((BLK, D), lambda i, s: (i, 0))
    return pl.pallas_call(
        result_kernel,
        grid_spec=pltpu.PrefetchScalarGridSpec(
            num_scalar_prefetch=1, grid=(half,), in_specs=[mine, mine, block], out_specs=block
        ),
        out_shape=jax.ShapeDtypeStruct((SEQ // 2, D), bf16),
        name="result",
    )(where, h1, m_own, m_sib)


def swap(values, axis, bit):
    size = lax.axis_size(axis)
    return lax.ppermute(values, axis, [(n, n ^ bit) for n in range(size)])


def on_device(
    inputs,
    buckets,
    ln1_gain,
    ln1_bias,
    w_qkv,
    w_out,
    ln2_gain,
    ln2_bias,
    w_up,
    w_down,
    prefix_embed,
    prefix_w1,
    prefix_b1,
    prefix_w2,
    prefix_b2,
    cotangent,
):
    prefix_count = prefix_embed.shape[0]
    width = prefix_w1.shape[1]
    member = lax.axis_index("tensor")
    place = lax.axis_index("batch") & 3
    slot = member // 2
    side = member & 1
    where = jnp.stack([slot, buckets[slot], place, side]).astype(jnp.int32)
    w_flat = w_qkv.reshape(D, 3 * COLS)
    w2_flat = prefix_w2.reshape(width, 2 * COLS)
    gain1, bias1 = ln1_gain.reshape(1, D), ln1_bias.reshape(1, D)
    gain2, bias2 = ln2_gain.reshape(1, D), ln2_bias.reshape(1, D)
    embed = jnp.pad(prefix_embed, ((0, PREFIX_ROWS - prefix_count), (0, 0)))

    def gather(weight):
        rows = weight.shape[0] // 4
        near = swap(lax.dynamic_slice_in_dim(weight, place * rows, rows, 0), "tensor", 2)
        beside = swap(near, "batch", 1)
        above = swap(near, "batch", 2)
        return near, beside, above, swap(above, "batch", 1)

    q_pieces = gather(w_flat)
    o_pieces = gather(w_out)
    hidden, kv_own = prefix_forward(
        embed, prefix_w1, prefix_b1.reshape(1, width), w2_flat, prefix_b2.reshape(1, 2 * COLS)
    )
    kv_peer = swap(kv_own, "tensor", 2)
    u_pieces = gather(w_up)
    d_pieces = gather(w_down)

    *saved, part_own = attend(where, inputs, gain1, bias1, (w_flat, w_out), kv_own)
    part_own_sib = swap(part_own, "tensor", 1)
    *saved, part_peer = attend(where, inputs, gain1, bias1, (q_pieces, o_pieces), kv_peer, saved)
    part_peer_sib = swap(part_peer, "tensor", 1)
    proj, o, e, ep, inv = saved
    h1, u2, m, du = mlp_own(
        where,
        inputs,
        (part_own, part_peer, part_own_sib, part_peer_sib),
        gain2,
        bias2,
        cotangent,
        w_up,
        w_down,
    )
    m, du = mlp_peer(where, u2, cotangent, m, du, u_pieces, d_pieces)
    du_sib = swap(du, "tensor", 1)
    half = SEQ // 2
    m_sib = swap(lax.dynamic_slice_in_dim(m, (1 - side) * half, half, 0), "tensor", 1)
    dh, do = turn(where, du, du_sib, h1, cotangent, gain2, w_out, o_pieces)
    kv = jnp.stack([kv_own, kv_peer])
    du1, dkv = attend_back(where, proj, o, do, e, ep, inv, kv, w_flat, q_pieces)
    du1_sib = swap(lax.dynamic_slice_in_dim(du1, (1 - side) * half, half, 0), "tensor", 1)
    output = result(where, h1, m, m_sib)
    input_grad = finish(where, du1, du1_sib, inputs, dh, gain1)

    dkv_t = dkv[0] + swap(dkv[1], "tensor", 2)
    dkv_t = lax.psum(dkv_t, "batch")
    grad_kv = jnp.concatenate([dkv_t[:prefix_count], dkv_t[PREFIX_ROWS : PREFIX_ROWS + prefix_count]], axis=1)
    hidden = hidden[:prefix_count]
    w2_grad = exact(hidden, grad_kv, ((0,), (0,))).reshape(width, 2, COLS)
    b2_grad = jnp.sum(grad_kv, axis=0).reshape(2, COLS)
    pre = lax.psum(exact(grad_kv, w2_flat.astype(f32), ((1,), (1,))), "tensor") * (1.0 - hidden * hidden)
    embed_grad = exact(pre, prefix_w1.astype(f32), ((1,), (1,)))
    w1_grad = exact(prefix_embed.astype(f32), pre, ((0,), (0,)))
    b1_grad = jnp.sum(pre, axis=0)
    return (output, input_grad, embed_grad, w1_grad, b1_grad, w2_grad, b2_grad)


def solution(mesh):
    placed = (
        P("batch", None),
        P("batch"),
        P(),
        P(),
        P(None, None, "tensor"),
        P("tensor", None),
        P(),
        P(),
        P(None, "tensor"),
        P("tensor", None),
        P(),
        P(),
        P(),
        P(None, None, "tensor"),
        P(None, "tensor"),
        P("batch", None),
    )
    return jax.shard_map(
        on_device,
        mesh=mesh,
        in_specs=placed,
        out_specs=(
            P(("batch", "tensor"), None),
            P(("batch", "tensor"), None),
            P(),
            P(),
            P(),
            P(None, None, "tensor"),
            P(None, "tensor"),
        ),
        check_vma=False,
    )
```

```python
import functools
import math

import jax
import jax.numpy as jnp
from jax import lax
from jax.experimental import pallas as pl
from jax.experimental.pallas import tpu as pltpu
from jax.sharding import PartitionSpec as P

D = 1024
HD = 64
SEQ = 1024
HEADS = 4
COLS = HEADS * HD
BLK = 256
NBLK = SEQ // BLK
HALF = NBLK // 2
LANES = HEADS * BLK
PREFIX_ROWS = 16
EXT = HD + 16
TRI = [BLK * i * (i + 1) // 2 for i in range(NBLK)]
E_ROWS = BLK * NBLK * (NBLK + 1) // 2
LOG2E = 1.4426950408889634
SCALE = 0.125
FAR = -1e30
MASKED = -1e9 * LOG2E
MIB = 1 << 20

f32 = jnp.float32
bf16 = jnp.bfloat16
precise = lax.Precision.HIGHEST


def dot_nn(a, b):
    return lax.dot_general(a, b, (((1,), (0,)), ((), ())), preferred_element_type=f32)


def dot_nt(a, b):
    return lax.dot_general(a, b, (((1,), (1,)), ((), ())), preferred_element_type=f32)


def exact(a, b, dims):
    return lax.dot_general(a, b, (dims, ((), ())), precision=precise, preferred_element_type=f32)


def norm_rows(values):
    average = jnp.mean(values, axis=-1, keepdims=True)
    centred = values - average
    inv = lax.rsqrt(jnp.mean(centred * centred, axis=-1, keepdims=True) + 1e-05)
    return centred * inv, inv


def norm_back(incoming, normed, inv, gain):
    scaled = incoming * gain
    return inv * (
        scaled
        - jnp.mean(scaled, axis=-1, keepdims=True)
        - normed * jnp.mean(scaled * normed, axis=-1, keepdims=True)
    )


def head_lanes(h):
    return slice(h * BLK, (h + 1) * BLK)


def head_rows(h):
    return slice(h * HD, (h + 1) * HD)


def head_blocks(cols):
    row_head = lax.broadcasted_iota(jnp.int32, cols.shape, 0) // HD
    return jnp.concatenate(
        [jnp.where(row_head == h, cols, jnp.zeros_like(cols)) for h in range(HEADS)], axis=1
    )


class Loose:
    def __init__(self, array):
        self.array = array


def hbm(*arrays):
    return [
        a.array if isinstance(a, Loose) else pltpu.with_memory_space_constraint(a, pltpu.HBM)
        for a in arrays
    ]


def plain(arrays):
    return [a.array if isinstance(a, Loose) else a for a in arrays]


def rows_at(i, count=1):
    return slice(i * BLK, (i + count) * BLK)


class Moves:
    def __init__(self, sems):
        self.sems = sems
        self.used = 0
        self.out = []
        self.halves = []

    def load(self, source, target):
        copy = pltpu.make_async_copy(source, target, self.sems.at[self.used])
        self.used += 1
        copy.start()
        return copy

    def store(self, source, target):
        self.out.append(self.load(source, target))

    def store_half(self, source, same, at, mine, other):
        sem = self.sems.at[self.used]
        self.used += 1
        here = pltpu.make_async_copy(source, mine.at[at], sem)
        there = pltpu.make_async_copy(source, other.at[at], sem)
        pl.when(same)(here.start)
        pl.when(jnp.logical_not(same))(there.start)
        self.halves.append((same, here, there))

    def finish(self):
        for copy in self.out:
            copy.wait()
        for same, here, there in self.halves:
            pl.when(same)(here.wait)
            pl.when(jnp.logical_not(same))(there.wait)


def once(copies):
    left = list(copies)

    def wait():
        while left:
            left.pop().wait()

    return wait


def weave(*tasks):
    live = list(tasks)
    while live:
        for task in list(live):
            if next(task, live) is live:
                live.remove(task)
        yield


def drain(*tasks):
    for _ in weave(*tasks):
        pass


ANY = pl.BlockSpec(memory_space=pl.ANY)
SMALL = pl.BlockSpec(memory_space=pltpu.SMEM)


def room(scratch):
    return sum(math.prod(shape) * jnp.dtype(kind).itemsize for shape, kind in scratch)


def call(kernel, name, where, args, outs, scratch, sems, aliases=None, flops=0):
    return pl.pallas_call(
        kernel,
        in_specs=[SMALL] + [ANY] * len(args),
        out_specs=[ANY] * len(outs),
        out_shape=[pltpu.HBM(shape, kind) for shape, kind in outs],
        scratch_shapes=[pltpu.VMEM(shape, kind) for shape, kind in scratch]
        + [pltpu.SemaphoreType.DMA((sems,))],
        input_output_aliases=aliases or {},
        compiler_params=pltpu.CompilerParams(
            vmem_limit_bytes=room(scratch) // MIB * MIB + 10 * MIB
        ),
        cost_estimate=pl.CostEstimate(
            flops=flops,
            transcendentals=0,
            bytes_accessed=sum(a.size * a.dtype.itemsize for a in plain(args)),
        ),
        name=name,
    )(where, *hbm(*args))


def first_pieces(moves, place, pieces, w, wo):
    rows, thin = D // 4, COLS // 4
    loads = []
    for k, piece in enumerate(pieces):
        at = pl.ds(pl.multiple_of((place ^ k) * rows, rows), rows)
        for part in range(3):
            loads.append(moves.load(piece.at[rows_at(part)], w.at[part, at]))
    late = []
    for k, piece in enumerate(pieces):
        at = pl.ds(pl.multiple_of((place ^ k) * thin, thin), thin)
        for c in range(D // COLS):
            late.append(
                moves.load(
                    piece.at[3 * BLK + c * thin : 3 * BLK + (c + 1) * thin],
                    wo.at[at, c * COLS : (c + 1) * COLS],
                )
            )
    return loads, late


def pack_pieces(moves, place, w, wo, out):
    rows, thin = D // 4, COLS // 4
    at = pl.ds(pl.multiple_of(place * rows, rows), rows)
    for part in range(3):
        moves.store(w.at[part, at], out.at[rows_at(part)])
    at = pl.ds(pl.multiple_of(place * thin, thin), thin)
    for c in range(D // COLS):
        moves.store(
            wo.at[at, c * COLS : (c + 1) * COLS],
            out.at[3 * BLK + c * thin : 3 * BLK + (c + 1) * thin],
        )


def pack_kernel(w, wo, out, sems):
    moves = Moves(sems)
    pack_pieces(moves, lax.axis_index("batch") & 3, w, wo, out)
    moves.finish()


def pack(w, wo):
    return pl.pallas_call(
        pack_kernel,
        in_specs=[ANY, ANY],
        out_specs=pl.BlockSpec(memory_space=pltpu.VMEM),
        out_shape=jax.ShapeDtypeStruct((4 * BLK, COLS), bf16),
        scratch_shapes=[pltpu.SemaphoreType.DMA((7,))],
        name="pack",
    )(*hbm(w, wo))


def prefix_kernel(embed, w1, b1, w2, b2, w, wo, up, down, *refs):
    hidden_out, kv_out, first_out, up_out, down_out, far_out, sems = refs
    place = lax.axis_index("batch") & 3
    moves = Moves(sems)
    near = pl.ds(pl.multiple_of(place * BLK, BLK), BLK)
    far = pl.ds(pl.multiple_of((place ^ 3) * BLK, BLK), BLK)
    pack_pieces(moves, place ^ 3, w, wo, first_out)
    moves.store(up.at[near], up_out)
    moves.store(down.at[near], down_out)
    moves.store(up.at[far], far_out.at[:BLK])
    moves.store(down.at[far], far_out.at[BLK:])
    hidden = jnp.tanh(dot_nn(embed[...], w1[...]) + b1[...])
    kv = exact(hidden, w2[...].astype(f32), ((1,), (0,))) + b2[...]
    real = lax.broadcasted_iota(jnp.int32, kv.shape, 0) < 10
    kv = jnp.where(real, kv, 0.0)
    hidden_out[...] = hidden
    kv = jnp.concatenate([kv[:, :COLS], kv[:, COLS:]], axis=0).astype(bf16)
    kv_out[...] = kv
    first_out[4 * BLK :, :] = kv
    moves.finish()


def prefix_forward(embed, w1, b1, w2, b2, w, wo, up, down):
    width = w1.shape[1]
    full = pl.BlockSpec(memory_space=pltpu.VMEM)
    return pl.pallas_call(
        prefix_kernel,
        in_specs=[full] * 5 + [ANY] * 4,
        out_specs=[full] * 6,
        out_shape=(
            pltpu.HBM((PREFIX_ROWS, width), f32),
            pltpu.HBM((2 * PREFIX_ROWS, COLS), bf16),
            jax.ShapeDtypeStruct((4 * BLK + 2 * PREFIX_ROWS, COLS), bf16),
            jax.ShapeDtypeStruct((BLK, D), bf16),
            jax.ShapeDtypeStruct((BLK, D), bf16),
            jax.ShapeDtypeStruct((2 * BLK, D), bf16),
        ),
        scratch_shapes=[pltpu.SemaphoreType.DMA((11,))],
        name="prefix_forward",
    )(*hbm(embed, w1, b1, w2, b2, w, wo, up, down))


def peer_prefix(moves, first_far, kv):
    return [moves.load(first_far.at[4 * BLK :], kv)]


def prefix_mid_kernel(dkv, hidden, w2_own, w2_peer, w2_out, b2_out, da_out):
    total = 0.0
    for part in range(2):
        rows = slice(part * PREFIX_ROWS, (part + 1) * PREFIX_ROWS)
        cols = slice(part * COLS, (part + 1) * COLS)
        grad = dkv[0, rows, :]
        w2_out[:, part, :] = exact(hidden[...], grad, ((0,), (0,)))
        b2_out[part : part + 1, :] = jnp.sum(grad, axis=0, keepdims=True)
        for g, w2 in enumerate((w2_own, w2_peer)):
            total = total + exact(dkv[g, rows, :], w2[:, cols].astype(f32), ((1,), (1,)))
    da_out[...] = total


def prefix_mid(dkv, hidden, w2_own, w2_peer):
    width = w2_own.shape[0]
    return pl.pallas_call(
        prefix_mid_kernel,
        out_shape=(
            pltpu.HBM((width, 2, COLS), f32),
            pltpu.HBM((2, COLS), f32),
            jax.ShapeDtypeStruct((PREFIX_ROWS, width), f32),
        ),
        compiler_params=pltpu.CompilerParams(vmem_limit_bytes=32 * MIB),
        name="prefix_mid",
    )(dkv, *hbm(hidden, w2_own), w2_peer)


def prefix_back_kernel(pre, hidden, embed, w1, embed_out, w1_out, b1_out):
    wide = hidden[...]
    da = pre[...] * (1.0 - wide * wide)
    b1_out[...] = jnp.sum(da, axis=0, keepdims=True)
    w1_out[...] = exact(embed[...].astype(f32), da, ((0,), (0,)))
    embed_out[...] = exact(da, w1[...].astype(f32), ((1,), (1,)))


def prefix_back(pre, hidden, embed, w1):
    width = w1.shape[1]
    return pl.pallas_call(
        prefix_back_kernel,
        out_shape=(
            pltpu.HBM((PREFIX_ROWS, D), f32),
            pltpu.HBM((D, width), f32),
            pltpu.HBM((1, width), f32),
        ),
        compiler_params=pltpu.CompilerParams(vmem_limit_bytes=32 * MIB),
        name="prefix_back",
    )(pre, *hbm(hidden, embed, w1))


def attend_kernel(peer, where, *refs):
    slot, place, bucket = where[0], where[1], where[3]
    if peer:
        u1_in, *pieces = refs[:5]
        kv_in, part_in = refs[5:7]
        refs = refs[7 + 6 :]
    else:
        x_in, gain_in, bias_in, w_in, wo_in, kv_in = refs[:6]
        refs = refs[6:]
    qt_out, kt_out, v_out, ot_out, e_out, stat_out, part_out = refs[:7]
    if peer:
        w_out, wo_out = refs[7:9]
        rows_v, part_v, w, wo, kv, qt_v, kt_v, k_v, v_v, vt_v, ot_v, e_v, stat_v, mix_v, s_v, sems = refs[9:]
    else:
        (u1_out,) = refs[7:8]
        rows_v, gain, bias, u1_v, w, wo, kv, qt_v, kt_v, k_v, v_v, vt_v, ot_v, e_v, stat_v, mix_v, s_v, sems = (
            refs[8:]
        )
    group = 1 if peer else 0
    moves = Moves(sems)
    if peer:
        rows = [moves.load(u1_in.at[rows_at(0)], rows_v.at[rows_at(0)])]
        got_w, got_wo = first_pieces(moves, place, pieces, w, wo)
        got_w, got_wo = once(got_w), once(got_wo)
        got_kv = once(peer_prefix(moves, kv_in, kv))
        rows += [moves.load(u1_in.at[rows_at(i)], rows_v.at[rows_at(i)]) for i in range(1, NBLK)]
        got_part = once([moves.load(part_in, part_v)])
    else:
        got_norm = once([moves.load(gain_in, gain), moves.load(bias_in, bias)])
        first = pl.multiple_of(slot * SEQ, SEQ)
        rows = [moves.load(x_in.at[pl.ds(first, BLK)], rows_v.at[rows_at(0)])]
        got_w = once([moves.load(w_in, w)])
        got_kv = once([moves.load(kv_in, kv)])
        rows += [
            moves.load(x_in.at[pl.ds(first + i * BLK, BLK)], rows_v.at[rows_at(i)])
            for i in range(1, NBLK)
        ]
        got_wo = once([moves.load(wo_in, wo)])
    filler = jnp.where(
        lax.broadcasted_iota(jnp.int32, (EXT - HD, SEQ), 0) == 0, 1.0, 0.0
    ).astype(bf16)
    for h in range(HEADS):
        vt_v[h * EXT + HD : (h + 1) * EXT, :] = filler

    def project(i):
        rows[i].wait()
        if not peer:
            got_norm()
            for part in range(4):
                at = slice(i * BLK + part * 64, i * BLK + part * 64 + 64)
                normed, _ = norm_rows(rows_v[at, :].astype(f32))
                u1_v[at, :] = (normed * gain[...] + bias[...]).astype(bf16)
                yield
            moves.store(u1_v.at[rows_at(i)], u1_out.at[rows_at(i)])
        u1 = (rows_v if peer else u1_v)[rows_at(i), :]
        got_w()
        if peer and i == 0:
            moves.store(w, w_out)
        keys = dot_nn(u1, w[1])
        yield
        qs = dot_nn(u1, w[0])
        k_v[rows_at(i), :] = keys.astype(bf16)
        kt_v[:, rows_at(i)] = keys.T.astype(bf16)
        yield
        values = dot_nn(u1, w[2])
        qt_v[:, rows_at(i)] = (qs * (SCALE * LOG2E)).T.astype(bf16)
        yield
        v_v[rows_at(i), :] = values.astype(bf16)
        values_t = values.T.astype(bf16)
        for h in range(HEADS):
            vt_v[h * EXT : h * EXT + HD, rows_at(i)] = values_t[head_rows(h)]
        moves.store(v_v.at[rows_at(i)], v_out.at[group, rows_at(i)])
        yield

    tops = {}
    done = {}

    def scores(n, i, h, first, count):
        got_kv()
        qt = qt_v[:, rows_at(i)]
        q_h = jnp.where(
            lax.broadcasted_iota(jnp.int32, qt.shape, 0) // HD == h, qt, jnp.zeros_like(qt)
        )
        real = lax.broadcasted_iota(jnp.int32, (PREFIX_ROWS, BLK), 0) < 10
        prefix = jnp.where(real, dot_nn(kv[:PREFIX_ROWS], q_h), FAR)
        top = jnp.max(prefix, axis=0, keepdims=True)
        for c in range(count):
            block = dot_nn(k_v[rows_at(first + c), :], q_h)
            if c == count - 1:
                keep = lax.broadcasted_iota(jnp.int32, (BLK, BLK), 0) <= lax.broadcasted_iota(
                    jnp.int32, (BLK, BLK), 1
                )
                block = jnp.where(keep, block, MASKED)
            s_v[n % 2, rows_at(c), :] = block
            top = jnp.maximum(top, jnp.max(block, axis=0, keepdims=True))
            yield
        tops[n] = prefix, top

    def mix(n, i, h, first, count):
        prefix, top = tops.pop(n)
        ep = jnp.exp2(prefix - top)
        stat_v[h, :PREFIX_ROWS, rows_at(i)] = ep
        one = jnp.where(
            lax.broadcasted_iota(jnp.int32, (EXT - HD, PREFIX_ROWS), 0) == 0, 1.0, 0.0
        )
        pv_t = kv[PREFIX_ROWS:].astype(f32).T
        pv_ext = jnp.concatenate([pv_t[head_rows(h)], one], axis=0).astype(bf16)
        mixed = dot_nn(pv_ext, ep.astype(bf16))
        for c in range(count):
            e_low = jnp.exp2(s_v[n % 2, rows_at(c), :] - top).astype(bf16)
            e_v[TRI[i] + c * BLK : TRI[i] + (c + 1) * BLK, head_lanes(h)] = e_low
            mixed = mixed + dot_nn(vt_v[h * EXT : (h + 1) * EXT, rows_at(first + c)], e_low)
            yield
        inv = 1.0 / mixed[HD : HD + 1]
        stat_v[h, PREFIX_ROWS:, rows_at(i)] = jnp.broadcast_to(inv, (8, BLK))
        done[n] = mixed[:HD] * inv

    def write(i, count):
        e_at = slice(TRI[i], TRI[i] + count * BLK)
        moves.store(e_v.at[e_at], e_out.at[group, e_at])
        ot = jnp.concatenate([done.pop(i * HEADS + h) for h in range(HEADS)], axis=0)
        ot_v[:, rows_at(i)] = ot.astype(bf16)
        o = ot.T.astype(bf16)
        yield
        got_wo()
        if peer:
            if i == 0:
                moves.store(wo, wo_out)
            got_part()
        for c in range(D // BLK):
            part = dot_nn(o, wo[:, rows_at(c)])
            if peer:
                part = part + part_v[rows_at(i), rows_at(c)].astype(f32)
            mix_v[rows_at(i), rows_at(c)] = part.astype(bf16)
            yield
        moves.store(mix_v.at[rows_at(i)], part_out.at[rows_at(i)])

    def run(local):
        units = []
        for i in range(NBLK):
            for h in range(HEADS):
                units.append((len(units), i, h, *((i, 1) if local else (0, i + 1))))
        drain(project(0))
        side = None
        drain(scores(*units[0]))
        for n, unit in enumerate(units):
            i, h = unit[1:3]
            if h == 0:
                side = iter(())
                steps = []
                if i > 0:
                    steps.append(write(i - 1, units[n - 1][4]))
                if i + 1 < NBLK:
                    steps.append(project(i + 1))
                side = weave(*steps)
                if i + 2 == NBLK:
                    pass
            ahead = []
            if n + 1 < len(units):
                if h == HEADS - 1:
                    drain(side)
                    if i + 2 == NBLK:
                        moves.store(qt_v, qt_out.at[group])
                        moves.store(kt_v, kt_out.at[group])
                ahead = [scores(*units[n + 1])]
            for _ in weave(*ahead, mix(*unit)):
                next(side, None)
                next(side, None)
        drain(side)
        moves.store(stat_v, stat_out.at[group])
        drain(write(NBLK - 1, units[-1][4]))
        moves.store(ot_v, ot_out.at[group])
        moves.finish()

    return run


def attend_main(peer, where, *refs):
    bucket = where[3]

    @pl.when(bucket == 0)
    def _():
        attend_kernel(peer, where, *refs)(True)

    @pl.when(bucket != 0)
    def _():
        attend_kernel(peer, where, *refs)(False)


def attend(where, group, args, saved=()):
    peer = group == 1
    outs = [
        ((2, COLS, SEQ), bf16),
        ((2, COLS, SEQ), bf16),
        ((2, SEQ, COLS), bf16),
        ((2, COLS, SEQ), bf16),
        ((2, E_ROWS, LANES), bf16),
        ((2, HEADS, PREFIX_ROWS + 8, SEQ), f32),
        ((SEQ, D), bf16),
    ]
    if peer:
        outs += [((3, D, COLS), bf16), ((COLS, D), bf16)]
        scratch = [((SEQ, D), bf16), ((SEQ, D), bf16)]
    else:
        outs += [((SEQ, D), bf16)]
        scratch = [((SEQ, D), bf16), ((1, D), f32), ((1, D), f32), ((SEQ, D), bf16)]
    scratch += [
        ((3, D, COLS), bf16),
        ((COLS, D), bf16),
        ((2 * PREFIX_ROWS, COLS), bf16),
        ((COLS, SEQ), bf16),
        ((COLS, SEQ), bf16),
        ((SEQ, COLS), bf16),
        ((SEQ, COLS), bf16),
        ((HEADS * EXT, SEQ), bf16),
        ((COLS, SEQ), bf16),
        ((E_ROWS, LANES), bf16),
        ((HEADS, PREFIX_ROWS + 8, SEQ), f32),
        ((SEQ, D), bf16),
        ((2, SEQ, BLK), f32),
    ]
    return call(
        functools.partial(attend_main, peer),
        "attend_peer" if peer else "attend_own",
        where,
        (*args, *saved),
        outs,
        scratch,
        64,
        {1 + len(args) + k: k for k in range(6)} if peer else None,
        flops=10 * 10**9,
    )


UNITS = 512
WIDE = 512
PARTS = 4


def unit_blocks(u2, dy, up, down, g_v, df_v, f_v, da_v, got, ready, put, side=None):
    k = 0.7978845608028654
    chunks = up.shape[1] // UNITS
    last = NBLK * chunks

    def products(n):
        i, c = divmod(n, chunks)
        if c == 0:
            ready(i)
        if i == 0:
            for part in range(UNITS // BLK):
                got[c * (UNITS // BLK) + part]()
        at, units = rows_at(i), slice(c * UNITS, (c + 1) * UNITS)
        f_v[n % 2] = dot_nn(u2[at, :], up[:, units])
        yield
        da_v[n % 2] = dot_nt(dy[at, :], down[units, :])
        yield

    def bend(n):
        i, c = divmod(n, chunks)
        units = slice(c * UNITS, (c + 1) * UNITS)
        size = BLK // PARTS
        for part in range(PARTS):
            at = slice(part * size, (part + 1) * size)
            f, da = f_v[n % 2, at, :], da_v[n % 2, at, :]
            square = f * f
            t = jnp.tanh(f * (k + (k * 0.044715) * square))
            half = 0.5 * t + 0.5
            g = f * half
            slope = half + g * (1.0 - half) * (2 * k + (6 * k * 0.044715) * square)
            g_v[i % 2, at, units] = g.astype(bf16)
            df_v[i % 2, at, units] = (da * slope).astype(bf16)
            yield

    def close(i):
        for part in range(D // WIDE):
            cols = slice(part * WIDE, (part + 1) * WIDE)
            m = dot_nn(g_v[i % 2], down[:, cols])
            yield
            du = dot_nt(df_v[i % 2], up[cols, :])
            put(i, cols, m, du)
            yield

    side = side or (lambda i: iter(()))
    drain(products(0))
    for n in range(last):
        i, c = divmod(n, chunks)
        if c == 0:
            extra = side(i)
        if c == chunks - 1:
            drain(extra)
        for _ in weave(*([products(n + 1)] if n + 1 < last else []), bend(n)):
            next(extra, None)
        if c == chunks - 1:
            drain(close(i))


def mlp_own_kernel(
    where, x_in, p0_in, p1_in, gain_in, bias_in, dy_in, up_in, down_in, *refs
):
    h1_out, n2_out, r2_out, u2_out, m_out, du_out = refs[:6]
    x, p0, p1, gain, bias, dy, up, down, h1_v, n2_v, r2_v, u2_v, m_v, du_v, g_v, df_v, f_v, da_v, sems = refs[6:]
    slot, side = where[0], where[2]
    first = pl.multiple_of(slot * SEQ, SEQ)
    moves = Moves(sems)
    got_norm = once([moves.load(gain_in, gain), moves.load(bias_in, bias)])

    def rows(i):
        here = pl.ds(first + i * BLK, BLK)
        return once(
            [
                moves.load(x_in.at[here], x.at[rows_at(i)]),
                moves.load(p0_in.at[rows_at(i)], p0.at[rows_at(i)]),
                moves.load(p1_in.at[rows_at(i)], p1.at[rows_at(i)]),
            ]
        ), once([moves.load(dy_in.at[here], dy.at[rows_at(i)])])

    blocks = [rows(0)]
    got = [
        once(
            [
                moves.load(up_in.at[:, rows_at(c)], up.at[:, rows_at(c)]),
                moves.load(down_in.at[rows_at(c)], down.at[rows_at(c)]),
            ]
        )
        for c in range(up.shape[1] // BLK)
    ]
    blocks += [rows(i) for i in range(1, NBLK)]

    def norm(i):
        blocks[i][0]()
        got_norm()
        for part in range(4):
            at = slice(i * BLK + part * 64, i * BLK + part * 64 + 64)
            h1 = x[at, :].astype(f32) + (p0[at, :].astype(f32) + p1[at, :].astype(f32))
            h1_v[at, :] = h1
            normed, inv = norm_rows(h1)
            n2_v[at, :] = normed.astype(bf16)
            r2_v[at, :] = jnp.broadcast_to(inv, (64, 128))
            u2_v[at, :] = (normed * gain[...] + bias[...]).astype(bf16)
            yield
        for source, target in ((n2_v, n2_out), (r2_v, r2_out), (u2_v, u2_out)):
            moves.store(source.at[rows_at(i)], target.at[rows_at(i)])
        if i + 1 == NBLK:
            half = SEQ // 2
            mine = pl.ds(pl.multiple_of(side * half, half), half)
            moves.store(h1_v.at[mine], h1_out)

    def put(i, cols, m, du):
        at = rows_at(i)
        m_v[at, cols] = m.astype(bf16)
        du_v[at, cols] = du.astype(bf16)
        if cols.stop == D:
            moves.store(m_v.at[at], m_out.at[at])
            moves.store(du_v.at[at], du_out.at[at])

    drain(norm(0))
    unit_blocks(
        u2_v,
        dy,
        up,
        down,
        g_v,
        df_v,
        f_v,
        da_v,
        got,
        lambda i: blocks[i][1](),
        put,
        lambda i: norm(i + 1) if i + 1 < NBLK else iter(()),
    )
    moves.finish()


def mlp_own(where, x, p0, p1, gain, bias, dy, up, down):
    full = ((SEQ, D), bf16)
    return call(
        mlp_own_kernel,
        "mlp_own",
        where,
        (x, p0, p1, gain, bias, dy, up, down),
        [((SEQ // 2, D), f32), full, ((SEQ, 128), f32), full, full, full],
        [
            full,
            full,
            full,
            ((1, D), f32),
            ((1, D), f32),
            full,
            (up.shape, bf16),
            (down.shape, bf16),
            ((SEQ, D), f32),
            full,
            ((SEQ, 128), f32),
            full,
            full,
            full,
            ((2, BLK, up.shape[1]), bf16),
            ((2, BLK, up.shape[1]), bf16),
            ((2, BLK, UNITS), f32),
            ((2, BLK, UNITS), f32),
        ],
        64,
        flops=12 * 10**9,
    )


def mlp_peer_kernel(where, u2_in, dy_in, m_in, du_in, *refs):
    u_pieces, d_pieces, far = list(refs[:3]), list(refs[3:6]), refs[6]
    u_pieces.append(far.at[:BLK])
    d_pieces.append(far.at[BLK:])
    mine_out, other_out, du_out, u2, dy, m_v, du_v, up, down, m_sum, du_sum, g_v, df_v, f_v, da_v, sems = refs[7:]
    slot, place, side = where[0], where[1], where[2]
    first = pl.multiple_of(slot * SEQ, SEQ)
    moves = Moves(sems)

    def rows(i):
        here = pl.ds(first + i * BLK, BLK)
        return once(
            [
                moves.load(u2_in.at[rows_at(i)], u2.at[rows_at(i)]),
                moves.load(dy_in.at[here], dy.at[rows_at(i)]),
            ]
        )

    blocks = [rows(0)]
    got = []
    for c in range(4):
        units = pl.ds(pl.multiple_of((place ^ c) * BLK, BLK), BLK)
        loads = [moves.load(d_pieces[c].at[:BLK], down.at[rows_at(c)])]
        for k in range(4):
            inner = pl.ds(pl.multiple_of((place ^ k) * BLK, BLK), BLK)
            loads.append(moves.load(u_pieces[k].at[:BLK, units], up.at[inner, rows_at(c)]))
        got.append(once(loads))
    blocks += [rows(i) for i in range(1, NBLK)]
    sums = [
        once(
            [
                moves.load(m_in.at[rows_at(i)], m_v.at[rows_at(i)]),
                moves.load(du_in.at[rows_at(i)], du_v.at[rows_at(i)]),
            ]
        )
        for i in range(NBLK)
    ]
    def put(i, cols, m, du):
        at = rows_at(i)
        sums[i]()
        m_sum[at, cols] = (m_v[at, cols].astype(f32) + m).astype(bf16)
        du_sum[at, cols] = (du_v[at, cols].astype(f32) + du).astype(bf16)
        if cols.stop == D:
            moves.store(du_sum.at[at], du_out.at[at])
            moves.store_half(
                m_sum.at[at], side == i // HALF, rows_at(i % HALF), mine_out, other_out
            )

    unit_blocks(u2, dy, up, down, g_v, df_v, f_v, da_v, got, lambda i: blocks[i](), put)
    moves.finish()


def mlp_peer(where, u2, dy, m, du, u_pieces, d_pieces, far):
    full = ((SEQ, D), bf16)
    half = ((SEQ // 2, D), bf16)
    units = 4 * BLK
    return call(
        mlp_peer_kernel,
        "mlp_peer",
        where,
        (u2, dy, m, du, *u_pieces, *d_pieces, far),
        [half, half, full],
        [full] * 4
        + [((D, units), bf16), ((units, D), bf16), full, full]
        + [((2, BLK, units), bf16)] * 2
        + [((2, BLK, UNITS), f32)] * 2,
        64,
        flops=12 * 10**9,
    )


def turn_kernel(where, *refs):
    own_in, sib_in, n2_in, r2_in, dy_in, gain_in, wo_own_in, wo_peer_in = refs[:8]
    ot_in, stat_in, qt_in, kv_own_in, kv_peer_in = refs[8:13]
    dh_out, dot_out, stat_out, dkv_out = refs[13:17]
    own, sib, n2, r2, dy, gain, wo, ot, stat, qt, kv, dh_v, dot_v, stat_v, dkv_v, low_v, sems = refs[17:]
    slot, side = where[0], where[2]
    first = pl.multiple_of(slot * SEQ, SEQ)
    moves = Moves(sems)
    got_gain = once([moves.load(gain_in, gain)])

    def rows(i):
        at = rows_at(i)
        return once(
            [
                moves.load(own_in.at[at], own.at[at]),
                moves.load(sib_in.at[at], sib.at[at]),
                moves.load(n2_in.at[at], n2.at[at]),
                moves.load(r2_in.at[at], r2.at[at]),
                moves.load(dy_in.at[pl.ds(first + i * BLK, BLK)], dy.at[at]),
            ]
        )

    blocks = [rows(0)]
    got_wo = once([moves.load(wo_own_in, wo.at[0]), moves.load(wo_peer_in, wo.at[1])])
    got_rest = once(
        [
            moves.load(ot_in, ot),
            moves.load(stat_in, stat),
            moves.load(qt_in, qt),
            moves.load(kv_own_in, kv.at[0]),
        ]
        + peer_prefix(moves, kv_peer_in, kv.at[1])
    )
    blocks += [rows(i) for i in range(1, NBLK)]
    def norm(i):
        blocks[i]()
        got_gain()
        for part in range(4):
            at = slice(i * BLK + part * 64, i * BLK + part * 64 + 64)
            du = own[at, :].astype(f32) + sib[at, :].astype(f32)
            dh = dy[at, :].astype(f32) + norm_back(
                du, n2[at, :].astype(f32), r2[at, 0:1], gain[...]
            )
            dh_v[at, :] = dh
            low_v[at, :] = dh.astype(bf16)
            yield

    def grads(i, g):
        at = rows_at(i)
        got_wo()
        do = dot_nt(low_v[at, :], wo[g])
        yield
        do_t = do.T
        yield
        got_rest()
        for h in range(HEADS):
            scaled = do_t[head_rows(h)] * stat[g, h, PREFIX_ROWS : PREFIX_ROWS + 1, at]
            dot_v[g, head_rows(h), at] = scaled.astype(bf16)
            balance = jnp.sum(
                scaled * ot[g, head_rows(h), at].astype(f32), axis=0, keepdims=True
            )
            stat_v[g, h, PREFIX_ROWS:, at] = jnp.broadcast_to(balance, (8, BLK))
            yield

    def prefix(g, h):
        pv = kv[g, PREFIX_ROWS:]
        pv = jnp.where(
            lax.broadcasted_iota(jnp.int32, pv.shape, 1) // HD == h, pv, jnp.zeros_like(pv)
        )
        ep = stat[g, h, :PREFIX_ROWS, :]
        dp = dot_nn(pv, dot_v[g])
        dpv = dot_nt(ep.astype(bf16), dot_v[g, head_rows(h), :])
        yield
        grad = ep * (dp - stat_v[g, h, PREFIX_ROWS : PREFIX_ROWS + 1, :])
        stat_v[g, h, :PREFIX_ROWS, :] = grad
        yield
        dpk = dot_nt(grad.astype(bf16), qt[g, head_rows(h), :])
        yield
        dkv_v[g, :PREFIX_ROWS, head_rows(h)] = dpk * (1.0 / LOG2E)
        dkv_v[g, PREFIX_ROWS:, head_rows(h)] = dpv

    drain(norm(0))
    for i in range(NBLK):
        drain(grads(i, 0), grads(i, 1), *([norm(i + 1)] if i + 1 < NBLK else []))
    half = SEQ // 2
    mine = pl.ds(pl.multiple_of(side * half, half), half)
    moves.store(dh_v.at[mine], dh_out)
    moves.store(dot_v, dot_out)
    drain(*[prefix(g, h) for g in range(2) for h in range(HEADS)])
    moves.store(dkv_v, dkv_out)
    moves.store(stat_v, stat_out)
    moves.finish()


def turn(where, *args):
    full = ((SEQ, D), bf16)
    pair = ((2, COLS, SEQ), bf16)
    stat = ((2, HEADS, PREFIX_ROWS + 8, SEQ), f32)
    dkv = ((2, 2 * PREFIX_ROWS, COLS), f32)
    return call(
        turn_kernel,
        "turn",
        where,
        args,
        [((SEQ // 2, D), f32), pair, stat, dkv],
        [
            full,
            full,
            full,
            ((SEQ, 128), f32),
            full,
            ((1, D), f32),
            ((2, COLS, D), bf16),
            pair,
            stat,
            pair,
            ((2, 2 * PREFIX_ROWS, COLS), bf16),
            ((SEQ, D), f32),
            pair,
            stat,
            dkv,
            full,
        ],
        40,
        flops=6 * 10**9,
    )


def attend_back_kernel(where, *refs):
    dot_in, qt_in, v_in, kt_in, e_in, stat_in, kv_own_in, kv_peer_in, w_own_in, w_peer_in = refs[:10]
    mine_out, other_out, do_t, qt, v, kt, e, stat, kv, w, dkt, dvt, du_v, ds_v, sems = refs[10:]

    def run(local):
        moves = Moves(sems)
        spans = [(i, 1) if local else (0, i + 1) for i in range(NBLK)]

        def e_rows(g, i):
            at = slice(TRI[i], TRI[i] + spans[i][1] * BLK)
            return moves.load(e_in.at[g, at], e.at[g, at])

        last = NBLK - 1
        e_got = {}
        wait_base = []
        for g in range(2):
            loads = [
                moves.load(dot_in.at[g], do_t.at[g]),
                moves.load(v_in.at[g], v.at[g]),
                moves.load(stat_in.at[g], stat.at[g]),
            ]
            e_got[g, last] = once([e_rows(g, last)])
            loads.append(moves.load(qt_in.at[g], qt.at[g]))
            loads.append(moves.load(kt_in.at[g], kt.at[g]))
            if g == 0:
                loads.append(moves.load(kv_own_in, kv.at[0]))
            else:
                loads += peer_prefix(moves, kv_peer_in, kv.at[1])
            wait_base.append(once(loads))
        got_w = [once([moves.load(w_own_in, w.at[0])]), once([moves.load(w_peer_in, w.at[1])])]
        for i in reversed(range(last)):
            for g in range(2):
                e_got[g, i] = once([e_rows(g, i)])
        dqs = {}

        def slopes(n, i, g, h, first, count):
            wait_base[g]()
            here = rows_at(i)
            do_h = do_t[g, :, here]
            do_h = jnp.where(
                lax.broadcasted_iota(jnp.int32, do_h.shape, 0) // HD == h, do_h, jnp.zeros_like(do_h)
            )
            balance = stat[g, h, PREFIX_ROWS : PREFIX_ROWS + 1, here]
            e_got[g, i]()
            for c in range(count):
                dp = dot_nn(v[g, rows_at(first + c), :], do_h)
                e_low = e[g, TRI[i] + c * BLK : TRI[i] + (c + 1) * BLK, head_lanes(h)]
                ds_v[n % 2, rows_at(c), :] = (e_low.astype(f32) * (dp - balance)).astype(bf16)
                yield

        def use(n, i, g, h, first, count):
            heads, here = head_rows(h), rows_at(i)
            pk_t = kv[g, :PREFIX_ROWS].astype(f32).T.astype(bf16)
            dq = dot_nn(pk_t[heads], stat[g, h, :PREFIX_ROWS, here].astype(bf16))
            for c in range(count):
                at = rows_at(first + c)
                e_low = e[g, TRI[i] + c * BLK : TRI[i] + (c + 1) * BLK, head_lanes(h)]
                ds = ds_v[n % 2, rows_at(c), :]
                dv = dot_nt(do_t[g, heads, here], e_low)
                dk = dot_nt(qt[g, heads, here], ds)
                if local or i == last:
                    dvt[g, heads, at] = dv
                    dkt[g, heads, at] = dk
                else:
                    dvt[g, heads, at] += dv
                    dkt[g, heads, at] += dk
                dq = dq + dot_nn(kt[g, heads, at], ds)
                yield
            dqs[i, g, h] = dq

        def share(i):
            here = rows_at(i)
            grads = []
            for g in range(2):
                dq = jnp.concatenate([dqs.pop((i, g, h)) for h in range(HEADS)], axis=0)
                for value, scale in ((dq, SCALE), (dkt[g, :, here], 1.0 / LOG2E), (dvt[g, :, here], 1.0)):
                    grads.append((value.T * scale).astype(bf16))
                    yield
            for c in range(D // BLK):
                total = None
                for g in range(2):
                    got_w[g]()
                    for part in range(3):
                        term = dot_nt(grads[3 * g + part], w[g, part, rows_at(c), :])
                        total = term if total is None else total + term
                du_v[here, rows_at(c)] = total.astype(bf16)
                yield
            moves.store_half(du_v.at[here], where[2] == i // HALF, rows_at(i % HALF), mine_out, other_out)

        units = []
        for i in reversed(range(NBLK)):
            for g in range(2):
                for h in range(HEADS):
                    units.append((len(units), i, g, h, *spans[i]))
        side = iter(())
        drain(slopes(*units[0]))
        for n, unit in enumerate(units):
            i, g, h = unit[1:4]
            ahead = [slopes(*units[n + 1])] if n + 1 < len(units) else []
            for _ in weave(*ahead, use(*unit)):
                next(side, None)
            if g == 1 and h == HEADS - 1:
                drain(side)
                side = share(i)
        drain(side)
        moves.finish()

    bucket = where[3]

    @pl.when(bucket == 0)
    def _():
        run(True)

    @pl.when(bucket != 0)
    def _():
        run(False)


def attend_back(where, *args):
    pair = ((2, COLS, SEQ), bf16)
    return call(
        attend_back_kernel,
        "attend_back",
        where,
        args,
        [((SEQ // 2, D), bf16)] * 2,
        [
            pair,
            pair,
            ((2, SEQ, COLS), bf16),
            pair,
            ((2, E_ROWS, LANES), bf16),
            ((2, HEADS, PREFIX_ROWS + 8, SEQ), f32),
            ((2, 2 * PREFIX_ROWS, COLS), bf16),
            ((2, 3, D, COLS), bf16),
            ((2, COLS, SEQ), f32),
            ((2, COLS, SEQ), f32),
            ((SEQ, D), bf16),
            ((2, SEQ, BLK), bf16),
        ],
        32,
        flops=16 * 10**9,
    )


def finish_kernel(where, own_in, sib_in, x_in, dh_in, gain_in, out, own, sib, x, dh, gain, out_v, sems):
    slot, side = where[0], where[2]
    half = SEQ // 2
    mine = pl.multiple_of(side * half, half)
    moves = Moves(sems)
    got_gain = once([moves.load(gain_in, gain)])
    size = BLK // 2

    def rows(i):
        at = slice(i * size, (i + 1) * size)
        return once([
            moves.load(x_in.at[pl.ds(slot * SEQ + mine + i * size, size)], x.at[at]),
        ]), once([
            moves.load(own_in.at[at], own.at[at]),
            moves.load(sib_in.at[at], sib.at[at]),
            moves.load(dh_in.at[at], dh.at[at]),
        ])

    blocks = [rows(i) for i in range(half // size)]
    for i, (got_x, got_rest) in enumerate(blocks):
        at = slice(i * size, (i + 1) * size)
        got_x()
        normed, inv = norm_rows(x[at, :].astype(f32))
        got_rest()
        got_gain()
        du = own[at, :].astype(f32) + sib[at, :].astype(f32)
        out_v[at, :] = dh[at, :] + norm_back(du, normed, inv, gain[...])
        moves.store(out_v.at[at], out.at[at])
    moves.finish()


def finish(where, *args):
    half = ((SEQ // 2, D), bf16)
    wide = ((SEQ // 2, D), f32)
    return call(
        finish_kernel, "finish", where, args, [wide], [half, half, half, wide, ((1, D), f32), wide], 24
    )[0]


def result_kernel(where, h1_in, own_in, sib_in, after, out, h1, own, sib, out_v, sems):
    half = SEQ // 2
    moves = Moves(sems)
    size = BLK

    def rows(i):
        at = slice(i * size, (i + 1) * size)
        return once([
            moves.load(h1_in.at[at], h1.at[at]),
            moves.load(own_in.at[at], own.at[at]),
            moves.load(sib_in.at[at], sib.at[at]),
        ])

    blocks = [rows(i) for i in range(half // size)]
    for i, got in enumerate(blocks):
        at = slice(i * size, (i + 1) * size)
        got()
        out_v[at, :] = (h1[at, :] + (own[at, :].astype(f32) + sib[at, :].astype(f32))).astype(bf16)
        moves.store(out_v.at[at], out.at[at])
    moves.finish()


def result(where, *args):
    half = ((SEQ // 2, D), bf16)
    wide = ((SEQ // 2, D), f32)
    return call(result_kernel, "result", where, args, [half], [wide, half, half, half], 12)[0]


def swap(values, axis, bit):
    size = lax.axis_size(axis)
    return lax.ppermute(values, axis, [(n, n ^ bit) for n in range(size)])


def after(values, *others):
    return lax.optimization_barrier((values, *others))[0]


def other_half(values, side):
    half = values.shape[0] // 2
    return lax.dynamic_slice_in_dim(values, (1 - side) * half, half, 0)


def on_device(
    inputs,
    buckets,
    ln1_gain,
    ln1_bias,
    w_qkv,
    w_out,
    ln2_gain,
    ln2_bias,
    w_up,
    w_down,
    prefix_embed,
    prefix_w1,
    prefix_b1,
    prefix_w2,
    prefix_b2,
    cotangent,
):
    prefix_count = prefix_embed.shape[0]
    width = prefix_w1.shape[1]
    member = lax.axis_index("tensor")
    place = lax.axis_index("batch") & 3
    side = member & 1
    slot = member // 2
    where = jnp.stack([slot, place, side, buckets[slot]]).astype(jnp.int32)
    w = w_qkv.transpose(1, 0, 2)
    w2_flat = prefix_w2.reshape(width, 2 * COLS)
    gain1, bias1 = ln1_gain.reshape(1, D), ln1_bias.reshape(1, D)
    gain2, bias2 = ln2_gain.reshape(1, D), ln2_bias.reshape(1, D)
    embed = jnp.pad(prefix_embed, ((0, PREFIX_ROWS - prefix_count), (0, 0)))

    def across(values):
        return swap(values, "tensor", 2)

    first_near = across(pack(w, w_out))
    hidden, kv_own, first_quarter, up_quarter, down_quarter, far_quarter = prefix_forward(
        embed,
        prefix_w1,
        prefix_b1.reshape(1, width),
        w2_flat,
        prefix_b2.reshape(1, 2 * COLS),
        w,
        w_out,
        w_up,
        w_down,
    )
    first_far = across(first_quarter)
    up_near = across(up_quarter)
    down_near = across(down_quarter)
    kv_peer = first_far

    first_beside = swap(first_near, "batch", 1)
    first_above = swap(first_near, "batch", 2)
    *saved, part, u1 = attend(
        where, 0, (after(inputs, first_near), gain1, bias1, w, w_out, kv_own)
    )
    first = [Loose(a) for a in (first_near, first_beside, first_above, first_far)]
    *saved, part, w_peer, wo_peer = attend(
        where, 1, (u1, *first, Loose(kv_peer), part), saved
    )
    rest_far = across(after(far_quarter, u1))
    part_sib = swap(after(part, up_near, down_near), "tensor", 1)
    up_sent, down_sent = after(up_near, part), after(down_near, part)
    up_pieces = (up_near, swap(up_sent, "batch", 1), swap(up_sent, "batch", 2))
    down_pieces = (down_near, swap(down_sent, "batch", 1), swap(down_sent, "batch", 2))
    qt, kt, v, ot, e, stat = saved
    h1, n2, r2, u2, m, du = mlp_own(
        where,
        inputs,
        part,
        Loose(part_sib),
        gain2,
        bias2,
        after(cotangent, down_sent),
        w_up,
        w_down,
    )
    m_mine, m_other, du = mlp_peer(
        where,
        u2,
        cotangent,
        m,
        du,
        [Loose(a) for a in up_pieces],
        [Loose(a) for a in down_pieces],
        Loose(rest_far),
    )
    w2_peer = across(after(w2_flat, h1))
    du_sib = swap(after(du, w2_peer), "tensor", 1)
    m_sib = swap(m_other, "tensor", 1)
    dh, do_t, stat_back, dkv = turn(
        where,
        du,
        Loose(du_sib),
        n2,
        r2,
        cotangent,
        gain2,
        w_out,
        wo_peer,
        ot,
        stat,
        qt,
        kv_own,
        Loose(kv_peer),
    )
    dkv_peer = across(dkv)
    du1_mine, du1_other = attend_back(
        where, do_t, qt, v, kt, e, stat_back, kv_own, Loose(kv_peer), w, w_peer
    )
    du1_sib = swap(after(du1_other, dkv_peer), "tensor", 1)
    dkv = dkv + after(dkv_peer, du1_mine)[::-1]
    bits = [1 << n for n in range(lax.axis_size("batch").bit_length() - 1)]
    output = result(where, h1, m_mine, Loose(m_sib), after(du1_mine, dkv))
    dkv_next = dkv + after(swap(dkv, "batch", bits[0]), output)
    input_grad = finish(where, du1_mine, Loose(after(du1_sib, dkv_next)), inputs, dh, gain1)
    dkv = dkv_next + after(swap(dkv_next, "batch", bits[1]), input_grad)
    for bit in bits[2:]:
        dkv = dkv + swap(dkv, "batch", bit)
    w2_grad, b2_grad, pre = prefix_mid(dkv, hidden, w2_flat, w2_peer)
    pre = pre + swap(pre, "tensor", 1)
    embed_grad, w1_grad, b1_grad = prefix_back(pre, hidden, embed, prefix_w1)
    return (
        output,
        input_grad,
        embed_grad[:prefix_count],
        w1_grad,
        b1_grad.reshape(width),
        w2_grad,
        b2_grad,
    )


def solution(mesh):
    placed = (
        P("batch", None),
        P("batch"),
        P(),
        P(),
        P(None, None, "tensor"),
        P("tensor", None),
        P(),
        P(),
        P(None, "tensor"),
        P("tensor", None),
        P(),
        P(),
        P(),
        P(None, None, "tensor"),
        P(None, "tensor"),
        P("batch", None),
    )
    return jax.shard_map(
        on_device,
        mesh=mesh,
        in_specs=placed,
        out_specs=(
            P(("batch", "tensor"), None),
            P(("batch", "tensor"), None),
            P(),
            P(),
            P(),
            P(None, None, "tensor"),
            P(None, "tensor"),
        ),
        check_vma=False,
    )
```

```python
import functools
import math

import jax
import jax.numpy as jnp
from jax import lax
from jax.experimental import pallas as pl
from jax.experimental.pallas import tpu as pltpu
from jax.sharding import PartitionSpec as P

D = 1024
HD = 64
SEQ = 1024
HEADS = 4
COLS = HEADS * HD
BLK = 256
NBLK = SEQ // BLK
HALF = NBLK // 2
LANES = HEADS * BLK
PREFIX_ROWS = 16
EXT = HD + 16
TRI = [BLK * i * (i + 1) // 2 for i in range(NBLK)]
E_ROWS = BLK * NBLK * (NBLK + 1) // 2
LOG2E = 1.4426950408889634
SCALE = 0.125
FAR = -1e30
MASKED = -1e9 * LOG2E
MIB = 1 << 20

f32 = jnp.float32
bf16 = jnp.bfloat16
precise = lax.Precision.HIGHEST


def dot_nn(a, b):
    return lax.dot_general(a, b, (((1,), (0,)), ((), ())), preferred_element_type=f32)


def dot_nt(a, b):
    return lax.dot_general(a, b, (((1,), (1,)), ((), ())), preferred_element_type=f32)


def exact(a, b, dims):
    return lax.dot_general(a, b, (dims, ((), ())), precision=precise, preferred_element_type=f32)


def norm_rows(values):
    average = jnp.mean(values, axis=-1, keepdims=True)
    centred = values - average
    inv = lax.rsqrt(jnp.mean(centred * centred, axis=-1, keepdims=True) + 1e-05)
    return centred * inv, inv


def norm_back(incoming, normed, inv, gain):
    scaled = incoming * gain
    return inv * (
        scaled
        - jnp.mean(scaled, axis=-1, keepdims=True)
        - normed * jnp.mean(scaled * normed, axis=-1, keepdims=True)
    )


def head_lanes(h):
    return slice(h * BLK, (h + 1) * BLK)


def head_rows(h):
    return slice(h * HD, (h + 1) * HD)


def head_blocks(cols):
    row_head = lax.broadcasted_iota(jnp.int32, cols.shape, 0) // HD
    return jnp.concatenate(
        [jnp.where(row_head == h, cols, jnp.zeros_like(cols)) for h in range(HEADS)], axis=1
    )


class Loose:
    def __init__(self, array):
        self.array = array


def hbm(*arrays):
    return [
        a.array if isinstance(a, Loose) else pltpu.with_memory_space_constraint(a, pltpu.HBM)
        for a in arrays
    ]


def plain(arrays):
    return [a.array if isinstance(a, Loose) else a for a in arrays]


def rows_at(i, count=1):
    return slice(i * BLK, (i + count) * BLK)


class Moves:
    def __init__(self, sems):
        self.sems = sems
        self.used = 0
        self.out = []
        self.halves = []

    def load(self, source, target):
        copy = pltpu.make_async_copy(source, target, self.sems.at[self.used])
        self.used += 1
        copy.start()
        return copy

    def store(self, source, target):
        self.out.append(self.load(source, target))

    def store_half(self, source, same, at, mine, other):
        sem = self.sems.at[self.used]
        self.used += 1
        here = pltpu.make_async_copy(source, mine.at[at], sem)
        there = pltpu.make_async_copy(source, other.at[at], sem)
        pl.when(same)(here.start)
        pl.when(jnp.logical_not(same))(there.start)
        self.halves.append((same, here, there))

    def finish(self):
        for copy in self.out:
            copy.wait()
        for same, here, there in self.halves:
            pl.when(same)(here.wait)
            pl.when(jnp.logical_not(same))(there.wait)


def once(copies):
    left = list(copies)

    def wait():
        while left:
            left.pop().wait()

    return wait


def weave(*tasks):
    live = list(tasks)
    while live:
        for task in list(live):
            if next(task, live) is live:
                live.remove(task)
        yield


def drain(*tasks):
    for _ in weave(*tasks):
        pass


ANY = pl.BlockSpec(memory_space=pl.ANY)
SMALL = pl.BlockSpec(memory_space=pltpu.SMEM)


def room(scratch):
    return sum(math.prod(shape) * jnp.dtype(kind).itemsize for shape, kind in scratch)


def call(kernel, name, where, args, outs, scratch, sems, aliases=None, flops=0):
    return pl.pallas_call(
        kernel,
        in_specs=[SMALL] + [ANY] * len(args),
        out_specs=[ANY] * len(outs),
        out_shape=[pltpu.HBM(shape, kind) for shape, kind in outs],
        scratch_shapes=[pltpu.VMEM(shape, kind) for shape, kind in scratch]
        + [pltpu.SemaphoreType.DMA((sems,))],
        input_output_aliases=aliases or {},
        compiler_params=pltpu.CompilerParams(
            vmem_limit_bytes=room(scratch) // MIB * MIB + 10 * MIB
        ),
        cost_estimate=pl.CostEstimate(
            flops=flops,
            transcendentals=0,
            bytes_accessed=sum(a.size * a.dtype.itemsize for a in plain(args)),
        ),
        name=name,
    )(where, *hbm(*args))


def first_pieces(moves, place, pieces, w, wo):
    rows, thin = D // 4, COLS // 4
    loads = []
    for k, piece in enumerate(pieces):
        at = pl.ds(pl.multiple_of((place ^ k) * rows, rows), rows)
        for part in range(3):
            loads.append(moves.load(piece.at[rows_at(part)], w.at[part, at]))
    late = []
    for k, piece in enumerate(pieces):
        at = pl.ds(pl.multiple_of((place ^ k) * thin, thin), thin)
        for c in range(D // COLS):
            late.append(
                moves.load(
                    piece.at[3 * BLK + c * thin : 3 * BLK + (c + 1) * thin],
                    wo.at[at, c * COLS : (c + 1) * COLS],
                )
            )
    return loads, late


def pack_pieces(moves, place, w, wo, out):
    rows, thin = D // 4, COLS // 4
    at = pl.ds(pl.multiple_of(place * rows, rows), rows)
    for part in range(3):
        moves.store(w.at[part, at], out.at[rows_at(part)])
    at = pl.ds(pl.multiple_of(place * thin, thin), thin)
    for c in range(D // COLS):
        moves.store(
            wo.at[at, c * COLS : (c + 1) * COLS],
            out.at[3 * BLK + c * thin : 3 * BLK + (c + 1) * thin],
        )


def pack_kernel(w, wo, out, sems):
    moves = Moves(sems)
    pack_pieces(moves, lax.axis_index("batch") & 3, w, wo, out)
    moves.finish()


def pack(w, wo):
    return pl.pallas_call(
        pack_kernel,
        in_specs=[ANY, ANY],
        out_specs=pl.BlockSpec(memory_space=pltpu.VMEM),
        out_shape=jax.ShapeDtypeStruct((4 * BLK, COLS), bf16),
        scratch_shapes=[pltpu.SemaphoreType.DMA((7,))],
        name="pack",
    )(*hbm(w, wo))


def unit_copies(move, units, up, down, out):
    copies = []
    for source, target in [(up.at[:, units], out.at[:D])] + [
        (down.at[units, rows_at(c)], out.at[D + c * BLK : D + (c + 1) * BLK])
        for c in range(D // BLK)
    ]:
        copies.append(move(source, target))
    return copies


def prefix_kernel(embed, w1, b1, w2, b2, w, wo, up, down, *refs):
    hidden_out, kv_out, first_out, near_out, far_out, sems = refs
    place = lax.axis_index("batch") & 3
    moves = Moves(sems)
    pack_pieces(moves, place ^ 3, w, wo, first_out)
    for bits, out in ((0, near_out), (3, far_out)):
        units = pl.ds(pl.multiple_of((place ^ bits) * BLK, BLK), BLK)
        unit_copies(moves.store, units, up, down, out)
    hidden = jnp.tanh(dot_nn(embed[...], w1[...]) + b1[...])
    kv = exact(hidden, w2[...].astype(f32), ((1,), (0,))) + b2[...]
    real = lax.broadcasted_iota(jnp.int32, kv.shape, 0) < 10
    kv = jnp.where(real, kv, 0.0)
    hidden_out[...] = hidden
    kv = jnp.concatenate([kv[:, :COLS], kv[:, COLS:]], axis=0).astype(bf16)
    kv_out[...] = kv
    first_out[4 * BLK :, :] = kv
    moves.finish()


def prefix_forward(embed, w1, b1, w2, b2, w, wo, up, down):
    width = w1.shape[1]
    full = pl.BlockSpec(memory_space=pltpu.VMEM)
    return pl.pallas_call(
        prefix_kernel,
        in_specs=[full] * 5 + [ANY] * 4,
        out_specs=[full] * 5,
        out_shape=(
            pltpu.HBM((PREFIX_ROWS, width), f32),
            pltpu.HBM((2 * PREFIX_ROWS, COLS), bf16),
            jax.ShapeDtypeStruct((4 * BLK + 2 * PREFIX_ROWS, COLS), bf16),
            jax.ShapeDtypeStruct((2 * D, BLK), bf16),
            jax.ShapeDtypeStruct((2 * D, BLK), bf16),
        ),
        scratch_shapes=[pltpu.SemaphoreType.DMA((17,))],
        compiler_params=pltpu.CompilerParams(vmem_limit_bytes=24 * MIB),
        name="prefix_forward",
    )(*hbm(embed, w1, b1, w2, b2, w, wo, up, down))


def peer_prefix(moves, first_far, kv):
    return [moves.load(first_far.at[4 * BLK :], kv)]


def prefix_back_kernel(dkv, da, hidden, embed, w1, w2_out, b2_out, embed_out, w1_out, b1_out):
    wide = hidden[...]
    low = wide.astype(bf16)
    over_rows = (((0,), (0,)), ((), ()))
    for part in range(2):
        grad = dkv[part * PREFIX_ROWS : (part + 1) * PREFIX_ROWS, :]
        w2_out[:, part, :] = lax.dot_general(
            low, grad.astype(bf16), over_rows, preferred_element_type=f32
        )
        b2_out[part : part + 1, :] = jnp.sum(grad, axis=0, keepdims=True)
    pre = jnp.concatenate([da[:PREFIX_ROWS], da[PREFIX_ROWS:]], axis=1) * (1.0 - wide * wide)
    b1_out[...] = jnp.sum(pre, axis=0, keepdims=True)
    pre_low = pre.astype(bf16)
    w1_out[...] = lax.dot_general(embed[...], pre_low, over_rows, preferred_element_type=f32)
    embed_out[...] = dot_nt(pre_low, w1[...])


def prefix_back(dkv, da, hidden, embed, w1):
    width = w1.shape[1]
    return pl.pallas_call(
        prefix_back_kernel,
        out_shape=(
            pltpu.HBM((width, 2, COLS), f32),
            pltpu.HBM((2, COLS), f32),
            pltpu.HBM((PREFIX_ROWS, D), f32),
            pltpu.HBM((D, width), f32),
            pltpu.HBM((1, width), f32),
        ),
        compiler_params=pltpu.CompilerParams(vmem_limit_bytes=24 * MIB),
        name="prefix_back",
    )(dkv, da, *hbm(hidden, embed, w1))


def attend_kernel(peer, where, *refs):
    slot, place, bucket = where[0], where[1], where[3]
    if peer:
        u1_in, *pieces = refs[:5]
        kv_in, part_in = refs[5:7]
        refs = refs[7 + 6 :]
    else:
        x_in, gain_in, bias_in, w_in, wo_in, kv_in = refs[:6]
        refs = refs[6:]
    qt_out, kt_out, v_out, ot_out, e_out, stat_out, part_out = refs[:7]
    if peer:
        w_out, wo_out = refs[7:9]
        rows_v, part_v, w, wo, kv, qt_v, kt_v, k_v, v_v, vt_v, ot_v, e_v, stat_v, mix_v, s_v, sems = refs[9:]
    else:
        (u1_out,) = refs[7:8]
        rows_v, gain, bias, u1_v, w, wo, kv, qt_v, kt_v, k_v, v_v, vt_v, ot_v, e_v, stat_v, mix_v, s_v, sems = (
            refs[8:]
        )
    group = 1 if peer else 0
    moves = Moves(sems)
    if peer:
        rows = [moves.load(u1_in.at[rows_at(0)], rows_v.at[rows_at(0)])]
        got_w, got_wo = first_pieces(moves, place, pieces, w, wo)
        got_w, got_wo = once(got_w), once(got_wo)
        got_kv = once(peer_prefix(moves, kv_in, kv))
        rows += [moves.load(u1_in.at[rows_at(i)], rows_v.at[rows_at(i)]) for i in range(1, NBLK)]
        got_part = once([moves.load(part_in, part_v)])
    else:
        got_norm = once([moves.load(gain_in, gain), moves.load(bias_in, bias)])
        first = pl.multiple_of(slot * SEQ, SEQ)
        rows = [moves.load(x_in.at[pl.ds(first, BLK)], rows_v.at[rows_at(0)])]
        got_w = once([moves.load(w_in, w)])
        got_kv = once([moves.load(kv_in, kv)])
        rows += [
            moves.load(x_in.at[pl.ds(first + i * BLK, BLK)], rows_v.at[rows_at(i)])
            for i in range(1, NBLK)
        ]
        got_wo = once([moves.load(wo_in, wo)])
    filler = jnp.where(
        lax.broadcasted_iota(jnp.int32, (EXT - HD, SEQ), 0) == 0, 1.0, 0.0
    ).astype(bf16)
    for h in range(HEADS):
        vt_v[h * EXT + HD : (h + 1) * EXT, :] = filler

    def project(i):
        rows[i].wait()
        if not peer:
            got_norm()
            for part in range(4):
                at = slice(i * BLK + part * 64, i * BLK + part * 64 + 64)
                normed, _ = norm_rows(rows_v[at, :].astype(f32))
                u1_v[at, :] = (normed * gain[...] + bias[...]).astype(bf16)
                yield
            moves.store(u1_v.at[rows_at(i)], u1_out.at[rows_at(i)])
        u1 = (rows_v if peer else u1_v)[rows_at(i), :]
        got_w()
        if peer and i == 0:
            moves.store(w, w_out)
        keys = dot_nn(u1, w[1])
        yield
        qs = dot_nn(u1, w[0])
        k_v[rows_at(i), :] = keys.astype(bf16)
        kt_v[:, rows_at(i)] = keys.T.astype(bf16)
        yield
        values = dot_nn(u1, w[2])
        qt_v[:, rows_at(i)] = (qs * (SCALE * LOG2E)).T.astype(bf16)
        yield
        v_v[rows_at(i), :] = values.astype(bf16)
        values_t = values.T.astype(bf16)
        for h in range(HEADS):
            vt_v[h * EXT : h * EXT + HD, rows_at(i)] = values_t[head_rows(h)]
        moves.store(v_v.at[rows_at(i)], v_out.at[group, rows_at(i)])
        yield

    tops = {}
    done = {}

    def scores(n, i, h, first, count):
        got_kv()
        qt = qt_v[:, rows_at(i)]
        q_h = jnp.where(
            lax.broadcasted_iota(jnp.int32, qt.shape, 0) // HD == h, qt, jnp.zeros_like(qt)
        )
        real = lax.broadcasted_iota(jnp.int32, (PREFIX_ROWS, BLK), 0) < 10
        prefix = jnp.where(real, dot_nn(kv[:PREFIX_ROWS], q_h), FAR)
        top = jnp.max(prefix, axis=0, keepdims=True)
        for c in range(count):
            block = dot_nn(k_v[rows_at(first + c), :], q_h)
            if c == count - 1:
                keep = lax.broadcasted_iota(jnp.int32, (BLK, BLK), 0) <= lax.broadcasted_iota(
                    jnp.int32, (BLK, BLK), 1
                )
                block = jnp.where(keep, block, MASKED)
            s_v[n % 2, rows_at(c), :] = block
            top = jnp.maximum(top, jnp.max(block, axis=0, keepdims=True))
            yield
        tops[n] = prefix, top

    def mix(n, i, h, first, count):
        prefix, top = tops.pop(n)
        ep = jnp.exp2(prefix - top)
        stat_v[h, :PREFIX_ROWS, rows_at(i)] = ep
        one = jnp.where(
            lax.broadcasted_iota(jnp.int32, (EXT - HD, PREFIX_ROWS), 0) == 0, 1.0, 0.0
        )
        pv_t = kv[PREFIX_ROWS:].astype(f32).T
        pv_ext = jnp.concatenate([pv_t[head_rows(h)], one], axis=0).astype(bf16)
        mixed = dot_nn(pv_ext, ep.astype(bf16))
        for c in range(count):
            e_low = jnp.exp2(s_v[n % 2, rows_at(c), :] - top).astype(bf16)
            e_v[TRI[i] + c * BLK : TRI[i] + (c + 1) * BLK, head_lanes(h)] = e_low
            mixed = mixed + dot_nn(vt_v[h * EXT : (h + 1) * EXT, rows_at(first + c)], e_low)
            yield
        inv = 1.0 / mixed[HD : HD + 1]
        stat_v[h, PREFIX_ROWS:, rows_at(i)] = jnp.broadcast_to(inv, (8, BLK))
        done[n] = mixed[:HD] * inv

    def write(i, count):
        e_at = slice(TRI[i], TRI[i] + count * BLK)
        moves.store(e_v.at[e_at], e_out.at[group, e_at])
        ot = jnp.concatenate([done.pop(i * HEADS + h) for h in range(HEADS)], axis=0)
        ot_v[:, rows_at(i)] = ot.astype(bf16)
        o = ot.T.astype(bf16)
        yield
        got_wo()
        if peer:
            if i == 0:
                moves.store(wo, wo_out)
            got_part()
        for c in range(D // BLK):
            part = dot_nn(o, wo[:, rows_at(c)])
            if peer:
                part = part + part_v[rows_at(i), rows_at(c)].astype(f32)
            mix_v[rows_at(i), rows_at(c)] = part.astype(bf16)
            yield
        moves.store(mix_v.at[rows_at(i)], part_out.at[rows_at(i)])

    def run(local):
        units = []
        for i in range(NBLK):
            for h in range(HEADS):
                units.append((len(units), i, h, *((i, 1) if local else (0, i + 1))))
        drain(project(0))
        side = None
        drain(scores(*units[0]))
        for n, unit in enumerate(units):
            i, h = unit[1:3]
            if h == 0:
                side = iter(())
                steps = []
                if i > 0:
                    steps.append(write(i - 1, units[n - 1][4]))
                if i + 1 < NBLK:
                    steps.append(project(i + 1))
                side = weave(*steps)
                if i + 2 == NBLK:
                    pass
            ahead = []
            if n + 1 < len(units):
                if h == HEADS - 1:
                    drain(side)
                    if i + 2 == NBLK:
                        moves.store(qt_v, qt_out.at[group])
                        moves.store(kt_v, kt_out.at[group])
                ahead = [scores(*units[n + 1])]
            for _ in weave(*ahead, mix(*unit)):
                next(side, None)
                next(side, None)
        drain(side)
        moves.store(stat_v, stat_out.at[group])
        drain(write(NBLK - 1, units[-1][4]))
        moves.store(ot_v, ot_out.at[group])
        moves.finish()

    return run


def attend_main(peer, where, *refs):
    bucket = where[3]

    @pl.when(bucket == 0)
    def _():
        attend_kernel(peer, where, *refs)(True)

    @pl.when(bucket != 0)
    def _():
        attend_kernel(peer, where, *refs)(False)


def attend(where, group, args, saved=()):
    peer = group == 1
    outs = [
        ((2, COLS, SEQ), bf16),
        ((2, COLS, SEQ), bf16),
        ((2, SEQ, COLS), bf16),
        ((2, COLS, SEQ), bf16),
        ((2, E_ROWS, LANES), bf16),
        ((2, HEADS, PREFIX_ROWS + 8, SEQ), f32),
        ((SEQ, D), bf16),
    ]
    if peer:
        outs += [((3, D, COLS), bf16), ((COLS, D), bf16)]
        scratch = [((SEQ, D), bf16), ((SEQ, D), bf16)]
    else:
        outs += [((SEQ, D), bf16)]
        scratch = [((SEQ, D), bf16), ((1, D), f32), ((1, D), f32), ((SEQ, D), bf16)]
    scratch += [
        ((3, D, COLS), bf16),
        ((COLS, D), bf16),
        ((2 * PREFIX_ROWS, COLS), bf16),
        ((COLS, SEQ), bf16),
        ((COLS, SEQ), bf16),
        ((SEQ, COLS), bf16),
        ((SEQ, COLS), bf16),
        ((HEADS * EXT, SEQ), bf16),
        ((COLS, SEQ), bf16),
        ((E_ROWS, LANES), bf16),
        ((HEADS, PREFIX_ROWS + 8, SEQ), f32),
        ((SEQ, D), bf16),
        ((2, SEQ, BLK), f32),
    ]
    return call(
        functools.partial(attend_main, peer),
        "attend_peer" if peer else "attend_own",
        where,
        (*args, *saved),
        outs,
        scratch,
        64,
        {1 + len(args) + k: k for k in range(6)} if peer else None,
        flops=10 * 10**9,
    )


def unit_blocks(u2, dy, up, down, g_v, df_v, f_v, da_v, chunks, got, ready, put, side=None):
    k = 0.7978845608028654
    last = NBLK * len(chunks)

    def products(n):
        i, c = divmod(n, len(chunks))
        if c == 0:
            ready(i)
        if i == 0:
            got[c]()
        at, units = rows_at(i), chunks[c]
        size = units.stop - units.start
        f_v[n % 2, :, :size] = dot_nn(u2[at, :], up[:, units])
        yield
        da_v[n % 2, :, :size] = dot_nt(dy[at, :], down[units, :])
        yield

    def bend(n):
        i, c = divmod(n, len(chunks))
        units = chunks[c]
        size = units.stop - units.start
        for part in range(4):
            at = slice(part * 64, (part + 1) * 64)
            f, da = f_v[n % 2, at, :size], da_v[n % 2, at, :size]
            square = f * f
            t = jnp.tanh(f * (k + (k * 0.044715) * square))
            half = 0.5 * t + 0.5
            g = f * half
            slope = half + g * (1.0 - half) * (2 * k + (6 * k * 0.044715) * square)
            g_v[i % 2, at, units] = g.astype(bf16)
            df_v[i % 2, at, units] = (da * slope).astype(bf16)
            yield

    def close(i):
        for part in range(D // WIDE):
            cols = slice(part * WIDE, (part + 1) * WIDE)
            m = dot_nn(g_v[i % 2], down[:, cols])
            yield
            du = dot_nt(df_v[i % 2], up[cols, :])
            put(i, cols, m, du)
            yield

    side = side or (lambda i: iter(()))
    drain(products(0))
    for n in range(last):
        i, c = divmod(n, len(chunks))
        if c == 0:
            extra = side(i)
        if c == len(chunks) - 1:
            drain(extra)
        for _ in weave(*([products(n + 1)] if n + 1 < last else []), bend(n)):
            next(extra, None)
        if c == len(chunks) - 1:
            drain(close(i))


WIDE = 512
OWN_CHUNKS = [slice(0, 512), slice(512, 1024), slice(1024, 1280)]
PEER_CHUNKS = [slice(0, 256), slice(256, 512), slice(512, 768)]


def unit_scratch(chunks):
    units = chunks[-1].stop
    widest = max(chunk.stop - chunk.start for chunk in chunks)
    return [
        ((D, units), bf16),
        ((units, D), bf16),
        ((2, BLK, units), bf16),
        ((2, BLK, units), bf16),
        ((2, BLK, widest), f32),
        ((2, BLK, widest), f32),
    ]


def unpack_units(moves, piece, k, up, down):
    units = slice(k * BLK, (k + 1) * BLK)

    def move(place, packed):
        return moves.load(packed, place)

    return unit_copies(move, units, up, down, piece)


def mlp_own_kernel(where, x_in, p0_in, p1_in, gain_in, bias_in, dy_in, up_in, down_in, near, *refs):
    h1_out, n2_out, r2_out, u2_out, m_out, du_out = refs[:6]
    x, p0, p1, gain, bias, dy, h1_v, n2_v, r2_v, u2_v, m_v, du_v = refs[6:18]
    up, down, g_v, df_v, f_v, da_v, sems = refs[18:]
    slot, side = where[0], where[2]
    first = pl.multiple_of(slot * SEQ, SEQ)
    moves = Moves(sems)
    got_norm = once([moves.load(gain_in, gain), moves.load(bias_in, bias)])

    def rows(i):
        here = pl.ds(first + i * BLK, BLK)
        return once(
            [
                moves.load(x_in.at[here], x.at[rows_at(i)]),
                moves.load(p0_in.at[rows_at(i)], p0.at[rows_at(i)]),
                moves.load(p1_in.at[rows_at(i)], p1.at[rows_at(i)]),
            ]
        ), once([moves.load(dy_in.at[here], dy.at[rows_at(i)])])

    blocks = [rows(0)]
    got = [
        once(
            [
                moves.load(up_in.at[:, chunk], up.at[:, chunk]),
                moves.load(down_in.at[chunk], down.at[chunk]),
            ]
        )
        for chunk in OWN_CHUNKS[:2]
    ]
    got.append(once(unpack_units(moves, near, D // BLK, up, down)))
    blocks += [rows(i) for i in range(1, NBLK)]

    def norm(i):
        blocks[i][0]()
        got_norm()
        for part in range(4):
            at = slice(i * BLK + part * 64, i * BLK + part * 64 + 64)
            h1 = x[at, :].astype(f32) + (p0[at, :].astype(f32) + p1[at, :].astype(f32))
            h1_v[at, :] = h1
            normed, inv = norm_rows(h1)
            n2_v[at, :] = normed.astype(bf16)
            r2_v[at, :] = jnp.broadcast_to(inv, (64, 128))
            u2_v[at, :] = (normed * gain[...] + bias[...]).astype(bf16)
            yield
        for source, target in ((n2_v, n2_out), (r2_v, r2_out), (u2_v, u2_out)):
            moves.store(source.at[rows_at(i)], target.at[rows_at(i)])
        if i + 1 == NBLK:
            half = SEQ // 2
            mine = pl.ds(pl.multiple_of(side * half, half), half)
            moves.store(h1_v.at[mine], h1_out)

    def put(i, cols, m, du):
        at = rows_at(i)
        m_v[at, cols] = m.astype(bf16)
        du_v[at, cols] = du.astype(bf16)
        if cols.stop == D:
            moves.store(m_v.at[at], m_out.at[at])
            moves.store(du_v.at[at], du_out.at[at])

    drain(norm(0))
    unit_blocks(
        u2_v,
        dy,
        up,
        down,
        g_v,
        df_v,
        f_v,
        da_v,
        OWN_CHUNKS,
        got,
        lambda i: blocks[i][1](),
        put,
        lambda i: norm(i + 1) if i + 1 < NBLK else iter(()),
    )
    moves.finish()


def mlp_own(where, x, p0, p1, gain, bias, dy, up, down, near):
    full = ((SEQ, D), bf16)
    return call(
        mlp_own_kernel,
        "mlp_own",
        where,
        (x, p0, p1, gain, bias, dy, up, down, near),
        [((SEQ // 2, D), f32), full, ((SEQ, 128), f32), full, full, full],
        [
            full,
            full,
            full,
            ((1, D), f32),
            ((1, D), f32),
            full,
            ((SEQ, D), f32),
            full,
            ((SEQ, 128), f32),
            full,
            full,
            full,
            *unit_scratch(OWN_CHUNKS),
        ],
        64,
        flops=12 * 10**9,
    )


def mlp_peer_kernel(where, u2_in, dy_in, m_in, du_in, *refs):
    pieces = refs[:3]
    mine_out, other_out, du_out, u2, dy, m_v, du_v, m_sum, du_sum = refs[3:12]
    up, down, g_v, df_v, f_v, da_v, sems = refs[12:]
    slot, side = where[0], where[2]
    first = pl.multiple_of(slot * SEQ, SEQ)
    moves = Moves(sems)

    def rows(i):
        here = pl.ds(first + i * BLK, BLK)
        return once(
            [
                moves.load(u2_in.at[rows_at(i)], u2.at[rows_at(i)]),
                moves.load(dy_in.at[here], dy.at[rows_at(i)]),
            ]
        )

    blocks = [rows(0)]
    got = [once(unpack_units(moves, piece, k, up, down)) for k, piece in enumerate(pieces)]
    blocks += [rows(i) for i in range(1, NBLK)]
    sums = [
        once(
            [
                moves.load(m_in.at[rows_at(i)], m_v.at[rows_at(i)]),
                moves.load(du_in.at[rows_at(i)], du_v.at[rows_at(i)]),
            ]
        )
        for i in range(NBLK)
    ]

    def put(i, cols, m, du):
        at = rows_at(i)
        sums[i]()
        m_sum[at, cols] = (m_v[at, cols].astype(f32) + m).astype(bf16)
        du_sum[at, cols] = (du_v[at, cols].astype(f32) + du).astype(bf16)
        if cols.stop == D:
            moves.store(du_sum.at[at], du_out.at[at])
            moves.store_half(
                m_sum.at[at], side == i // HALF, rows_at(i % HALF), mine_out, other_out
            )

    unit_blocks(
        u2, dy, up, down, g_v, df_v, f_v, da_v, PEER_CHUNKS, got, lambda i: blocks[i](), put
    )
    moves.finish()


def mlp_peer(where, u2, dy, m, du, pieces):
    full = ((SEQ, D), bf16)
    half = ((SEQ // 2, D), bf16)
    return call(
        mlp_peer_kernel,
        "mlp_peer",
        where,
        (u2, dy, m, du, *pieces),
        [half, half, full],
        [full] * 6 + unit_scratch(PEER_CHUNKS),
        64,
        flops=12 * 10**9,
    )


def turn_kernel(where, *refs):
    own_in, sib_in, n2_in, r2_in, dy_in, gain_in, wo_own_in, wo_peer_in = refs[:8]
    ot_in, stat_in, qt_in, kv_own_in, kv_peer_in, w2_own_in, w2_peer_in = refs[8:15]
    dh_out, dot_out, stat_out, dkv_out = refs[15:19]
    own, sib, n2, r2, dy, gain, wo, ot, stat, qt, kv, dh_v, dot_v, stat_v, dkv_v, low_v, w2, sems = refs[19:]
    slot, side = where[0], where[2]
    first = pl.multiple_of(slot * SEQ, SEQ)
    moves = Moves(sems)
    got_gain = once([moves.load(gain_in, gain)])

    def rows(i):
        at = rows_at(i)
        return once(
            [
                moves.load(own_in.at[at], own.at[at]),
                moves.load(sib_in.at[at], sib.at[at]),
                moves.load(n2_in.at[at], n2.at[at]),
                moves.load(r2_in.at[at], r2.at[at]),
                moves.load(dy_in.at[pl.ds(first + i * BLK, BLK)], dy.at[at]),
            ]
        )

    blocks = [rows(0)]
    got_wo = once([moves.load(wo_own_in, wo.at[0]), moves.load(wo_peer_in, wo.at[1])])
    got_rest = once(
        [
            moves.load(ot_in, ot),
            moves.load(stat_in, stat),
            moves.load(qt_in, qt),
            moves.load(kv_own_in, kv.at[0]),
        ]
        + peer_prefix(moves, kv_peer_in, kv.at[1])
    )
    got_w2 = once([moves.load(w2_own_in, w2.at[0]), moves.load(w2_peer_in, w2.at[1])])
    blocks += [rows(i) for i in range(1, NBLK)]
    def norm(i):
        blocks[i]()
        got_gain()
        for part in range(4):
            at = slice(i * BLK + part * 64, i * BLK + part * 64 + 64)
            du = own[at, :].astype(f32) + sib[at, :].astype(f32)
            dh = dy[at, :].astype(f32) + norm_back(
                du, n2[at, :].astype(f32), r2[at, 0:1], gain[...]
            )
            dh_v[at, :] = dh
            low_v[at, :] = dh.astype(bf16)
            yield

    def grads(i, g):
        at = rows_at(i)
        got_wo()
        do = dot_nt(low_v[at, :], wo[g])
        yield
        do_t = do.T
        yield
        got_rest()
        for h in range(HEADS):
            scaled = do_t[head_rows(h)] * stat[g, h, PREFIX_ROWS : PREFIX_ROWS + 1, at]
            dot_v[g, head_rows(h), at] = scaled.astype(bf16)
            balance = jnp.sum(
                scaled * ot[g, head_rows(h), at].astype(f32), axis=0, keepdims=True
            )
            stat_v[g, h, PREFIX_ROWS:, at] = jnp.broadcast_to(balance, (8, BLK))
            yield

    def prefix(g, h):
        pv = kv[g, PREFIX_ROWS:]
        pv = jnp.where(
            lax.broadcasted_iota(jnp.int32, pv.shape, 1) // HD == h, pv, jnp.zeros_like(pv)
        )
        ep = stat[g, h, :PREFIX_ROWS, :]
        dp = dot_nn(pv, dot_v[g])
        dpv = dot_nt(ep.astype(bf16), dot_v[g, head_rows(h), :])
        yield
        grad = ep * (dp - stat_v[g, h, PREFIX_ROWS : PREFIX_ROWS + 1, :])
        stat_v[g, h, :PREFIX_ROWS, :] = grad
        yield
        dpk = dot_nt(grad.astype(bf16), qt[g, head_rows(h), :])
        yield
        low = 2 * g * PREFIX_ROWS
        dkv_v[low : low + PREFIX_ROWS, head_rows(h)] = dpk * (1.0 / LOG2E)
        dkv_v[low + PREFIX_ROWS : low + 2 * PREFIX_ROWS, head_rows(h)] = dpv

    drain(norm(0))
    for i in range(NBLK):
        drain(grads(i, 0), grads(i, 1), *([norm(i + 1)] if i + 1 < NBLK else []))
    half = SEQ // 2
    mine = pl.ds(pl.multiple_of(side * half, half), half)
    moves.store(dh_v.at[mine], dh_out)
    moves.store(dot_v, dot_out)
    drain(*[prefix(g, h) for g in range(2) for h in range(HEADS)])
    moves.store(stat_v, stat_out)
    got_w2()
    da = 0.0
    for n in range(4):
        grad = dkv_v[n * PREFIX_ROWS : (n + 1) * PREFIX_ROWS, :].astype(bf16)
        da = da + dot_nt(grad, w2[n // 2, :, (n % 2) * COLS : (n % 2 + 1) * COLS])
    dkv_v[4 * PREFIX_ROWS : 5 * PREFIX_ROWS, :] = da[:, :COLS]
    dkv_v[5 * PREFIX_ROWS :, :] = da[:, COLS:]
    moves.store(dkv_v, dkv_out)
    moves.finish()


def turn(where, *args):
    full = ((SEQ, D), bf16)
    pair = ((2, COLS, SEQ), bf16)
    stat = ((2, HEADS, PREFIX_ROWS + 8, SEQ), f32)
    dkv = ((6 * PREFIX_ROWS, COLS), f32)
    return call(
        turn_kernel,
        "turn",
        where,
        args,
        [((SEQ // 2, D), f32), pair, stat, dkv],
        [
            full,
            full,
            full,
            ((SEQ, 128), f32),
            full,
            ((1, D), f32),
            ((2, COLS, D), bf16),
            pair,
            stat,
            pair,
            ((2, 2 * PREFIX_ROWS, COLS), bf16),
            ((SEQ, D), f32),
            pair,
            stat,
            dkv,
            full,
            ((2, 2 * COLS, 2 * COLS), bf16),
        ],
        48,
        flops=6 * 10**9,
    )


def attend_back_kernel(where, *refs):
    dot_in, qt_in, v_in, kt_in, e_in, stat_in, kv_own_in, kv_peer_in, w_own_in, w_peer_in = refs[:10]
    mine_out, other_out, do_t, qt, v, kt, e, stat, kv, w, dkt, dvt, du_v, ds_v, sems = refs[10:]

    def run(local):
        moves = Moves(sems)
        spans = [(i, 1) if local else (0, i + 1) for i in range(NBLK)]

        def e_rows(g, i):
            at = slice(TRI[i], TRI[i] + spans[i][1] * BLK)
            return moves.load(e_in.at[g, at], e.at[g, at])

        last = NBLK - 1
        e_got = {}
        wait_base = []
        for g in range(2):
            loads = [
                moves.load(dot_in.at[g], do_t.at[g]),
                moves.load(v_in.at[g], v.at[g]),
                moves.load(stat_in.at[g], stat.at[g]),
            ]
            e_got[g, last] = once([e_rows(g, last)])
            loads.append(moves.load(qt_in.at[g], qt.at[g]))
            loads.append(moves.load(kt_in.at[g], kt.at[g]))
            if g == 0:
                loads.append(moves.load(kv_own_in, kv.at[0]))
            else:
                loads += peer_prefix(moves, kv_peer_in, kv.at[1])
            wait_base.append(once(loads))
        got_w = [once([moves.load(w_own_in, w.at[0])]), once([moves.load(w_peer_in, w.at[1])])]
        for i in reversed(range(last)):
            for g in range(2):
                e_got[g, i] = once([e_rows(g, i)])
        dqs = {}

        def slopes(n, i, g, h, first, count):
            wait_base[g]()
            here = rows_at(i)
            do_h = do_t[g, :, here]
            do_h = jnp.where(
                lax.broadcasted_iota(jnp.int32, do_h.shape, 0) // HD == h, do_h, jnp.zeros_like(do_h)
            )
            balance = stat[g, h, PREFIX_ROWS : PREFIX_ROWS + 1, here]
            e_got[g, i]()
            for c in range(count):
                dp = dot_nn(v[g, rows_at(first + c), :], do_h)
                e_low = e[g, TRI[i] + c * BLK : TRI[i] + (c + 1) * BLK, head_lanes(h)]
                ds_v[n % 2, rows_at(c), :] = (e_low.astype(f32) * (dp - balance)).astype(bf16)
                yield

        def use(n, i, g, h, first, count):
            heads, here = head_rows(h), rows_at(i)
            pk_t = kv[g, :PREFIX_ROWS].astype(f32).T.astype(bf16)
            dq = dot_nn(pk_t[heads], stat[g, h, :PREFIX_ROWS, here].astype(bf16))
            for c in range(count):
                at = rows_at(first + c)
                e_low = e[g, TRI[i] + c * BLK : TRI[i] + (c + 1) * BLK, head_lanes(h)]
                ds = ds_v[n % 2, rows_at(c), :]
                dv = dot_nt(do_t[g, heads, here], e_low)
                dk = dot_nt(qt[g, heads, here], ds)
                if local or i == last:
                    dvt[g, heads, at] = dv
                    dkt[g, heads, at] = dk
                else:
                    dvt[g, heads, at] += dv
                    dkt[g, heads, at] += dk
                dq = dq + dot_nn(kt[g, heads, at], ds)
                yield
            dqs[i, g, h] = dq

        def share(i):
            here = rows_at(i)
            grads = []
            for g in range(2):
                dq = jnp.concatenate([dqs.pop((i, g, h)) for h in range(HEADS)], axis=0)
                for value, scale in ((dq, SCALE), (dkt[g, :, here], 1.0 / LOG2E), (dvt[g, :, here], 1.0)):
                    grads.append((value.T * scale).astype(bf16))
                    yield
            for c in range(D // BLK):
                total = None
                for g in range(2):
                    got_w[g]()
                    for part in range(3):
                        term = dot_nt(grads[3 * g + part], w[g, part, rows_at(c), :])
                        total = term if total is None else total + term
                du_v[here, rows_at(c)] = total.astype(bf16)
                yield
            moves.store_half(du_v.at[here], where[2] == i // HALF, rows_at(i % HALF), mine_out, other_out)

        units = []
        for i in reversed(range(NBLK)):
            for g in range(2):
                for h in range(HEADS):
                    units.append((len(units), i, g, h, *spans[i]))
        side = iter(())
        drain(slopes(*units[0]))
        for n, unit in enumerate(units):
            i, g, h = unit[1:4]
            ahead = [slopes(*units[n + 1])] if n + 1 < len(units) else []
            for _ in weave(*ahead, use(*unit)):
                next(side, None)
            if g == 1 and h == HEADS - 1:
                drain(side)
                side = share(i)
        drain(side)
        moves.finish()

    bucket = where[3]

    @pl.when(bucket == 0)
    def _():
        run(True)

    @pl.when(bucket != 0)
    def _():
        run(False)


def attend_back(where, *args):
    pair = ((2, COLS, SEQ), bf16)
    return call(
        attend_back_kernel,
        "attend_back",
        where,
        args,
        [((SEQ // 2, D), bf16)] * 2,
        [
            pair,
            pair,
            ((2, SEQ, COLS), bf16),
            pair,
            ((2, E_ROWS, LANES), bf16),
            ((2, HEADS, PREFIX_ROWS + 8, SEQ), f32),
            ((2, 2 * PREFIX_ROWS, COLS), bf16),
            ((2, 3, D, COLS), bf16),
            ((2, COLS, SEQ), f32),
            ((2, COLS, SEQ), f32),
            ((SEQ, D), bf16),
            ((2, SEQ, BLK), bf16),
        ],
        32,
        flops=16 * 10**9,
    )


def finish_kernel(where, own_in, sib_in, x_in, dh_in, gain_in, out, own, sib, x, dh, gain, out_v, sems):
    slot, side = where[0], where[2]
    half = SEQ // 2
    mine = pl.multiple_of(side * half, half)
    moves = Moves(sems)
    got_gain = once([moves.load(gain_in, gain)])
    size = BLK // 2

    def rows(i):
        at = slice(i * size, (i + 1) * size)
        return once([
            moves.load(x_in.at[pl.ds(slot * SEQ + mine + i * size, size)], x.at[at]),
        ]), once([
            moves.load(own_in.at[at], own.at[at]),
            moves.load(sib_in.at[at], sib.at[at]),
            moves.load(dh_in.at[at], dh.at[at]),
        ])

    blocks = [rows(i) for i in range(half // size)]
    for i, (got_x, got_rest) in enumerate(blocks):
        at = slice(i * size, (i + 1) * size)
        got_x()
        normed, inv = norm_rows(x[at, :].astype(f32))
        got_rest()
        got_gain()
        du = own[at, :].astype(f32) + sib[at, :].astype(f32)
        out_v[at, :] = dh[at, :] + norm_back(du, normed, inv, gain[...])
        moves.store(out_v.at[at], out.at[at])
    moves.finish()


def finish(where, *args):
    half = ((SEQ // 2, D), bf16)
    wide = ((SEQ // 2, D), f32)
    return call(
        finish_kernel, "finish", where, args, [wide], [half, half, half, wide, ((1, D), f32), wide], 24
    )[0]


def result_kernel(where, h1_in, own_in, sib_in, after, out, h1, own, sib, out_v, sems):
    half = SEQ // 2
    moves = Moves(sems)
    size = BLK

    def rows(i):
        at = slice(i * size, (i + 1) * size)
        return once([
            moves.load(h1_in.at[at], h1.at[at]),
            moves.load(own_in.at[at], own.at[at]),
            moves.load(sib_in.at[at], sib.at[at]),
        ])

    blocks = [rows(i) for i in range(half // size)]
    for i, got in enumerate(blocks):
        at = slice(i * size, (i + 1) * size)
        got()
        out_v[at, :] = (h1[at, :] + (own[at, :].astype(f32) + sib[at, :].astype(f32))).astype(bf16)
        moves.store(out_v.at[at], out.at[at])
    moves.finish()


def result(where, *args):
    half = ((SEQ // 2, D), bf16)
    wide = ((SEQ // 2, D), f32)
    return call(result_kernel, "result", where, args, [half], [wide, half, half, half], 12)[0]


def swap(values, axis, bit):
    size = lax.axis_size(axis)
    return lax.ppermute(values, axis, [(n, n ^ bit) for n in range(size)])


def after(values, *others):
    return lax.optimization_barrier((values, *others))[0]


def other_half(values, side):
    half = values.shape[0] // 2
    return lax.dynamic_slice_in_dim(values, (1 - side) * half, half, 0)


def on_device(
    inputs,
    buckets,
    ln1_gain,
    ln1_bias,
    w_qkv,
    w_out,
    ln2_gain,
    ln2_bias,
    w_up,
    w_down,
    prefix_embed,
    prefix_w1,
    prefix_b1,
    prefix_w2,
    prefix_b2,
    cotangent,
):
    prefix_count = prefix_embed.shape[0]
    width = prefix_w1.shape[1]
    member = lax.axis_index("tensor")
    place = lax.axis_index("batch") & 3
    side = member & 1
    slot = member // 2
    where = jnp.stack([slot, place, side, buckets[slot]]).astype(jnp.int32)
    w = w_qkv.transpose(1, 0, 2)
    w2_flat = prefix_w2.reshape(width, 2 * COLS)
    gain1, bias1 = ln1_gain.reshape(1, D), ln1_bias.reshape(1, D)
    gain2, bias2 = ln2_gain.reshape(1, D), ln2_bias.reshape(1, D)
    embed = jnp.pad(prefix_embed, ((0, PREFIX_ROWS - prefix_count), (0, 0)))

    def across(values):
        return swap(values, "tensor", 2)

    first_near = across(pack(w, w_out))
    hidden, kv_own, first_quarter, near_quarter, far_quarter = prefix_forward(
        embed,
        prefix_w1,
        prefix_b1.reshape(1, width),
        w2_flat,
        prefix_b2.reshape(1, 2 * COLS),
        w,
        w_out,
        w_up,
        w_down,
    )
    first_far = across(first_quarter)
    units_near = across(after(near_quarter, where))
    first_beside = swap(first_near, "batch", 1)
    first_above = swap(first_near, "batch", 2)
    *saved, part, u1 = attend(
        where, 0, (after(inputs, first_near), gain1, bias1, w, w_out, kv_own)
    )
    units_far = across(after(far_quarter, u1))
    first = (first_near, first_beside, first_above, first_far)
    *saved, part, w_peer, wo_peer = attend(where, 1, (u1, *first, first_far, part), saved)
    part_sib = swap(after(part, units_near), "tensor", 1)
    units_sent = after(units_near, part)
    units_beside = swap(units_sent, "batch", 1)
    units_above = swap(units_sent, "batch", 2)
    qt, kt, v, ot, e, stat = saved
    h1, n2, r2, u2, m, du = mlp_own(
        where,
        inputs,
        part,
        Loose(part_sib),
        gain2,
        bias2,
        after(cotangent, units_sent),
        w_up,
        w_down,
        Loose(units_near),
    )
    w2_peer = across(after(w2_flat, h1))
    m_mine, m_other, du = mlp_peer(
        where, u2, cotangent, m, du, [Loose(a) for a in (units_beside, units_above, units_far)]
    )
    du_sib = swap(after(du, w2_peer), "tensor", 1)
    m_sib = swap(m_other, "tensor", 1)
    dh, do_t, stat_back, dkv = turn(
        where,
        du,
        Loose(du_sib),
        n2,
        r2,
        cotangent,
        gain2,
        w_out,
        wo_peer,
        ot,
        stat,
        qt,
        kv_own,
        Loose(first_far),
        w2_flat,
        Loose(w2_peer),
    )

    dkv_peer = across(dkv)
    output = result(where, h1, m_mine, Loose(m_sib), dkv)
    dkv_peer = after(dkv_peer, output)
    rows = 2 * PREFIX_ROWS
    sums = jnp.concatenate(
        [dkv[:rows] + dkv_peer[rows : 2 * rows], dkv[2 * rows :] + dkv_peer[2 * rows :]], axis=0
    )
    bits = [1 << n for n in reversed(range(lax.axis_size("batch").bit_length() - 1))]
    sums_away = swap(sums, "batch", bits[0])
    du1_mine, du1_other = attend_back(
        where, after(do_t, sums), qt, v, kt, e, stat_back, kv_own, Loose(first_far), w, w_peer
    )
    du1_sib = swap(after(du1_other, sums_away), "tensor", 1)
    sums = sums + after(sums_away, du1_mine)
    input_grad = finish(where, du1_mine, Loose(after(du1_sib, sums)), inputs, dh, gain1)
    sums = sums + after(swap(sums, "batch", bits[1]), input_grad)
    for bit in bits[2:]:
        sums = sums + swap(sums, "batch", bit)
    da = sums[rows:] + swap(sums[rows:], "tensor", 1)
    w2_grad, b2_grad, embed_grad, w1_grad, b1_grad = prefix_back(
        sums[:rows], da, hidden, embed, prefix_w1
    )
    return (
        output,
        input_grad,
        embed_grad[:prefix_count],
        w1_grad,
        b1_grad.reshape(width),
        w2_grad,
        b2_grad,
    )


def solution(mesh):
    placed = (
        P("batch", None),
        P("batch"),
        P(),
        P(),
        P(None, None, "tensor"),
        P("tensor", None),
        P(),
        P(),
        P(None, "tensor"),
        P("tensor", None),
        P(),
        P(),
        P(),
        P(None, None, "tensor"),
        P(None, "tensor"),
        P("batch", None),
    )
    return jax.shard_map(
        on_device,
        mesh=mesh,
        in_specs=placed,
        out_specs=(
            P(("batch", "tensor"), None),
            P(("batch", "tensor"), None),
            P(),
            P(),
            P(),
            P(None, None, "tensor"),
            P(None, "tensor"),
        ),
        check_vma=False,
    )
```

```python
import functools
import math

import jax
import jax.numpy as jnp
from jax import lax
from jax.experimental import pallas as pl
from jax.experimental.pallas import tpu as pltpu
from jax.sharding import PartitionSpec as P

D = 1024
HD = 64
SEQ = 1024
HEADS = 4
COLS = HEADS * HD
BLK = 256
NBLK = SEQ // BLK
HALF = NBLK // 2
LANES = HEADS * BLK
PREFIX_ROWS = 16
EXT = HD + 16
TRI = [BLK * i * (i + 1) // 2 for i in range(NBLK)]
E_ROWS = BLK * NBLK * (NBLK + 1) // 2
LOG2E = 1.4426950408889634
SCALE = 0.125
FAR = -1e30
MASKED = -1e9 * LOG2E
MIB = 1 << 20

f32 = jnp.float32
bf16 = jnp.bfloat16
precise = lax.Precision.HIGHEST


def dot_nn(a, b):
    return lax.dot_general(a, b, (((1,), (0,)), ((), ())), preferred_element_type=f32)


def dot_nt(a, b):
    return lax.dot_general(a, b, (((1,), (1,)), ((), ())), preferred_element_type=f32)


def exact(a, b, dims):
    return lax.dot_general(a, b, (dims, ((), ())), precision=precise, preferred_element_type=f32)


def norm_rows(values):
    average = jnp.mean(values, axis=-1, keepdims=True)
    centred = values - average
    inv = lax.rsqrt(jnp.mean(centred * centred, axis=-1, keepdims=True) + 1e-05)
    return centred * inv, inv


def norm_back(incoming, normed, inv, gain):
    scaled = incoming * gain
    return inv * (
        scaled
        - jnp.mean(scaled, axis=-1, keepdims=True)
        - normed * jnp.mean(scaled * normed, axis=-1, keepdims=True)
    )


def head_lanes(h):
    return slice(h * BLK, (h + 1) * BLK)


def head_rows(h):
    return slice(h * HD, (h + 1) * HD)


def head_blocks(cols):
    row_head = lax.broadcasted_iota(jnp.int32, cols.shape, 0) // HD
    return jnp.concatenate(
        [jnp.where(row_head == h, cols, jnp.zeros_like(cols)) for h in range(HEADS)], axis=1
    )


class Loose:
    def __init__(self, array):
        self.array = array


class Near:
    def __init__(self, array):
        self.array = array


def placed(a):
    if isinstance(a, Loose):
        return a.array
    if isinstance(a, Near):
        return pltpu.with_memory_space_constraint(a.array, pltpu.VMEM)
    return pltpu.with_memory_space_constraint(a, pltpu.HBM)


def hbm(*arrays):
    return [placed(a) for a in arrays]


def plain(arrays):
    return [a.array if isinstance(a, (Loose, Near)) else a for a in arrays]


def rows_at(i, count=1):
    return slice(i * BLK, (i + count) * BLK)


class Moves:
    def __init__(self, sems):
        self.sems = sems
        self.used = 0
        self.out = []
        self.halves = []

    def load(self, source, target):
        copy = pltpu.make_async_copy(source, target, self.sems.at[self.used])
        self.used += 1
        copy.start()
        return copy

    def store(self, source, target):
        self.out.append(self.load(source, target))

    def store_half(self, source, same, at, mine, other):
        sem = self.sems.at[self.used]
        self.used += 1
        here = pltpu.make_async_copy(source, mine.at[at], sem)
        there = pltpu.make_async_copy(source, other.at[at], sem)
        pl.when(same)(here.start)
        pl.when(jnp.logical_not(same))(there.start)
        self.halves.append((same, here, there))

    def finish(self):
        for copy in self.out:
            copy.wait()
        for same, here, there in self.halves:
            pl.when(same)(here.wait)
            pl.when(jnp.logical_not(same))(there.wait)


def once(copies):
    left = list(copies)

    def wait():
        while left:
            left.pop().wait()

    return wait


def weave(*tasks):
    live = list(tasks)
    while live:
        for task in list(live):
            if next(task, live) is live:
                live.remove(task)
        yield


def drain(*tasks):
    for _ in weave(*tasks):
        pass


ANY = pl.BlockSpec(memory_space=pl.ANY)
SMALL = pl.BlockSpec(memory_space=pltpu.SMEM)


def room(scratch):
    return sum(math.prod(shape) * jnp.dtype(kind).itemsize for shape, kind in scratch)


FULL = pl.BlockSpec(memory_space=pltpu.VMEM)


def call(kernel, name, where, args, outs, scratch, sems, aliases=None, flops=0, near=0):
    far = len(outs) - near
    return pl.pallas_call(
        kernel,
        in_specs=[SMALL] + [FULL if isinstance(a, Near) else ANY for a in args],
        out_specs=[ANY] * far + [FULL] * near,
        out_shape=[pltpu.HBM(shape, kind) for shape, kind in outs[:far]]
        + [pltpu.VMEM(shape, kind) for shape, kind in outs[far:]],
        scratch_shapes=[pltpu.VMEM(shape, kind) for shape, kind in scratch]
        + [pltpu.SemaphoreType.DMA((sems,))],
        input_output_aliases=aliases or {},
        compiler_params=pltpu.CompilerParams(
            vmem_limit_bytes=room(scratch) // MIB * MIB + 8 * MIB
        ),
        cost_estimate=pl.CostEstimate(
            flops=flops,
            transcendentals=0,
            bytes_accessed=sum(a.size * a.dtype.itemsize for a in plain(args)),
        ),
        name=name,
    )(where, *hbm(*args))


def unpack_first(place, pieces, w, wo):
    rows, thin = D // 4, COLS // 4
    near, beside, above, top, bottom = pieces
    for k in range(4):

        def rows_of(first, count):
            if k < 3:
                return (near, beside, above)[k][first : first + count, :]
            half = 2 * BLK
            return (top if first < half else bottom)[first % half : first % half + count, :]

        at = pl.ds(pl.multiple_of((place ^ k) * rows, rows), rows)
        for part in range(3):
            w[part, at, :] = rows_of(part * BLK, BLK)
        at = pl.ds(pl.multiple_of((place ^ k) * thin, thin), thin)
        for c in range(D // COLS):
            wo[at, rows_at(c)] = rows_of(3 * BLK + c * thin, thin)


def pack_pieces(moves, place, w, wo, out):
    rows, thin = D // 4, COLS // 4
    at = pl.ds(pl.multiple_of(place * rows, rows), rows)
    for part in range(3):
        moves.store(w.at[part, at], out.at[rows_at(part)])
    at = pl.ds(pl.multiple_of(place * thin, thin), thin)
    for c in range(D // COLS):
        moves.store(
            wo.at[at, c * COLS : (c + 1) * COLS],
            out.at[3 * BLK + c * thin : 3 * BLK + (c + 1) * thin],
        )


def pack_kernel(w, wo, out, sems):
    moves = Moves(sems)
    pack_pieces(moves, lax.axis_index("batch") & 3, w, wo, out)
    moves.finish()


def pack(w, wo):
    return pl.pallas_call(
        pack_kernel,
        in_specs=[ANY, ANY],
        out_specs=pl.BlockSpec(memory_space=pltpu.VMEM),
        out_shape=jax.ShapeDtypeStruct((4 * BLK, COLS), bf16),
        scratch_shapes=[pltpu.SemaphoreType.DMA((7,))],
        name="pack",
    )(*hbm(w, wo))


def prefix_kernel(embed, w1, b1, w2, b2, up, down, *refs):
    hidden_out, kv_out, up_near, down_near, up_far, down_far, sems = refs
    place = lax.axis_index("batch") & 3
    moves = Moves(sems)
    for bits, up_out, down_out in ((0, up_near, down_near), (3, up_far, down_far)):
        units = pl.ds(pl.multiple_of((place ^ bits) * BLK, BLK), BLK)
        moves.store(up.at[:, units], up_out.at[:D])
        for c in range(D // BLK):
            moves.store(down.at[units, rows_at(c)], down_out.at[rows_at(c)])
    hidden = jnp.tanh(dot_nn(embed[...], w1[...]) + b1[...])
    kv = exact(hidden, w2[...].astype(f32), ((1,), (0,))) + b2[...]
    real = lax.broadcasted_iota(jnp.int32, kv.shape, 0) < 10
    kv = jnp.where(real, kv, 0.0)
    hidden_out[...] = hidden
    kv = jnp.concatenate([kv[:, :COLS], kv[:, COLS:]], axis=0).astype(bf16)
    kv_out[...] = kv
    up_near[D:, :] = kv
    moves.finish()


def prefix_forward(embed, w1, b1, w2, b2, up, down):
    width = w1.shape[1]
    full = pl.BlockSpec(memory_space=pltpu.VMEM)
    return pl.pallas_call(
        prefix_kernel,
        in_specs=[full] * 5 + [ANY] * 2,
        out_specs=[full] * 6,
        out_shape=(
            pltpu.HBM((PREFIX_ROWS, width), f32),
            pltpu.HBM((2 * PREFIX_ROWS, COLS), bf16),
            jax.ShapeDtypeStruct((D + 2 * PREFIX_ROWS, BLK), bf16),
            jax.ShapeDtypeStruct((D, BLK), bf16),
            jax.ShapeDtypeStruct((D, BLK), bf16),
            jax.ShapeDtypeStruct((D, BLK), bf16),
        ),
        scratch_shapes=[pltpu.SemaphoreType.DMA((10,))],
        compiler_params=pltpu.CompilerParams(vmem_limit_bytes=24 * MIB),
        name="prefix_forward",
    )(*hbm(embed, w1, b1, w2, b2, up, down))


def peer_prefix(moves, units_near, kv):
    return [moves.load(units_near.at[D:], kv)]


def prefix_back_kernel(dkv, da, hidden, embed, w1, w2_out, b2_out, embed_out, w1_out, b1_out):
    wide = hidden[...]
    low = wide.astype(bf16)
    over_rows = (((0,), (0,)), ((), ()))
    for part in range(2):
        grad = dkv[part * PREFIX_ROWS : (part + 1) * PREFIX_ROWS, :]
        w2_out[:, part, :] = lax.dot_general(
            low, grad.astype(bf16), over_rows, preferred_element_type=f32
        )
        b2_out[part : part + 1, :] = jnp.sum(grad, axis=0, keepdims=True)
    pre = jnp.concatenate([da[:PREFIX_ROWS], da[PREFIX_ROWS:]], axis=1) * (1.0 - wide * wide)
    b1_out[...] = jnp.sum(pre, axis=0, keepdims=True)
    pre_low = pre.astype(bf16)
    w1_out[...] = lax.dot_general(embed[...], pre_low, over_rows, preferred_element_type=f32)
    embed_out[...] = dot_nt(pre_low, w1[...])


def prefix_back(dkv, da, hidden, embed, w1):
    width = w1.shape[1]
    return pl.pallas_call(
        prefix_back_kernel,
        out_shape=(
            pltpu.HBM((width, 2, COLS), f32),
            pltpu.HBM((2, COLS), f32),
            pltpu.HBM((PREFIX_ROWS, D), f32),
            pltpu.HBM((D, width), f32),
            pltpu.HBM((1, width), f32),
        ),
        compiler_params=pltpu.CompilerParams(vmem_limit_bytes=24 * MIB),
        name="prefix_back",
    )(dkv, da, *hbm(Near(hidden), Near(embed), Near(w1)))


def attend_kernel(peer, where, *refs):
    slot, place, bucket = where[0], where[1], where[3]
    if peer:
        u1_v, *pieces = refs[:6]
        units_near, part_v, dy_in, up_in, down_in = refs[6:11]
        refs = refs[11 + 6 :]
    else:
        x_in, gain_in, bias_in, w_in, wo_in, kv_in = refs[:6]
        refs = refs[6:]
    qt_out, kt_out, v_out, ot_out, e_out, stat_out = refs[:6]
    if peer:
        w_out, wo_out, mix_v, dy_v, up_v, down_v = refs[6:12]
        w, wo, kv, qt_v, kt_v, k_v, v_v, vt_v, ot_v, e_v, stat_v, s_v, sems = refs[12:]
    else:
        rows_v, u1_v, mix_v = refs[6:9]
        gain, bias, w, wo, kv, qt_v, kt_v, k_v, v_v, vt_v, ot_v, e_v, stat_v, s_v, sems = (
            refs[9:]
        )
    group = 1 if peer else 0
    moves = Moves(sems)
    if peer:
        unpack_first(place, pieces, w, wo)
        kv[...] = units_near[D:, :]
        got_w = got_wo = got_kv = once([])
        first = pl.multiple_of(slot * SEQ, SEQ)
        moves.store(dy_in.at[pl.ds(first, SEQ)], dy_v)
        moves.store(up_in, up_v)
        moves.store(down_in, down_v)
    else:
        got_norm = once([moves.load(gain_in, gain), moves.load(bias_in, bias)])
        first = pl.multiple_of(slot * SEQ, SEQ)
        rows = [moves.load(x_in.at[pl.ds(first, BLK)], rows_v.at[rows_at(0)])]
        got_w = once([moves.load(w_in, w)])
        got_kv = once([moves.load(kv_in, kv)])
        rows += [
            moves.load(x_in.at[pl.ds(first + i * BLK, BLK)], rows_v.at[rows_at(i)])
            for i in range(1, NBLK)
        ]
        got_wo = once([moves.load(wo_in, wo)])
    filler = jnp.where(
        lax.broadcasted_iota(jnp.int32, (EXT - HD, SEQ), 0) == 0, 1.0, 0.0
    ).astype(bf16)
    for h in range(HEADS):
        vt_v[h * EXT + HD : (h + 1) * EXT, :] = filler

    def project(i):
        if not peer:
            rows[i].wait()
            got_norm()
            for part in range(4):
                at = slice(i * BLK + part * 64, i * BLK + part * 64 + 64)
                normed, _ = norm_rows(rows_v[at, :].astype(f32))
                u1_v[at, :] = (normed * gain[...] + bias[...]).astype(bf16)
                yield
        u1 = u1_v[rows_at(i), :]
        got_w()
        if peer and i == 0:
            moves.store(w, w_out)
        keys = dot_nn(u1, w[1])
        yield
        qs = dot_nn(u1, w[0])
        k_v[rows_at(i), :] = keys.astype(bf16)
        kt_v[:, rows_at(i)] = keys.T.astype(bf16)
        yield
        values = dot_nn(u1, w[2])
        qt_v[:, rows_at(i)] = (qs * (SCALE * LOG2E)).T.astype(bf16)
        yield
        v_v[rows_at(i), :] = values.astype(bf16)
        values_t = values.T.astype(bf16)
        for h in range(HEADS):
            vt_v[h * EXT : h * EXT + HD, rows_at(i)] = values_t[head_rows(h)]
        moves.store(v_v.at[rows_at(i)], v_out.at[group, rows_at(i)])
        yield

    tops = {}
    done = {}

    def scores(n, i, h, first, count):
        got_kv()
        qt = qt_v[:, rows_at(i)]
        q_h = jnp.where(
            lax.broadcasted_iota(jnp.int32, qt.shape, 0) // HD == h, qt, jnp.zeros_like(qt)
        )
        real = lax.broadcasted_iota(jnp.int32, (PREFIX_ROWS, BLK), 0) < 10
        prefix = jnp.where(real, dot_nn(kv[:PREFIX_ROWS], q_h), FAR)
        top = jnp.max(prefix, axis=0, keepdims=True)
        for c in range(count):
            block = dot_nn(k_v[rows_at(first + c), :], q_h)
            if c == count - 1:
                keep = lax.broadcasted_iota(jnp.int32, (BLK, BLK), 0) <= lax.broadcasted_iota(
                    jnp.int32, (BLK, BLK), 1
                )
                block = jnp.where(keep, block, MASKED)
            s_v[n % 2, rows_at(c), :] = block
            top = jnp.maximum(top, jnp.max(block, axis=0, keepdims=True))
            yield
        tops[n] = prefix, top

    def mix(n, i, h, first, count):
        prefix, top = tops.pop(n)
        ep = jnp.exp2(prefix - top)
        stat_v[h, :PREFIX_ROWS, rows_at(i)] = ep
        one = jnp.where(
            lax.broadcasted_iota(jnp.int32, (EXT - HD, PREFIX_ROWS), 0) == 0, 1.0, 0.0
        )
        pv_t = kv[PREFIX_ROWS:].astype(f32).T
        pv_ext = jnp.concatenate([pv_t[head_rows(h)], one], axis=0).astype(bf16)
        mixed = dot_nn(pv_ext, ep.astype(bf16))
        for c in range(count):
            e_low = jnp.exp2(s_v[n % 2, rows_at(c), :] - top).astype(bf16)
            e_v[TRI[i] + c * BLK : TRI[i] + (c + 1) * BLK, head_lanes(h)] = e_low
            mixed = mixed + dot_nn(vt_v[h * EXT : (h + 1) * EXT, rows_at(first + c)], e_low)
            yield
        e_at = slice(TRI[i], TRI[i] + count * BLK)
        moves.store(e_v.at[e_at, head_lanes(h)], e_out.at[group, e_at, head_lanes(h)])
        inv = 1.0 / mixed[HD : HD + 1]
        stat_v[h, PREFIX_ROWS:, rows_at(i)] = jnp.broadcast_to(inv, (8, BLK))
        done[n] = mixed[:HD] * inv

    def write(i, count):
        ot = jnp.concatenate([done.pop(i * HEADS + h) for h in range(HEADS)], axis=0)
        ot_v[:, rows_at(i)] = ot.astype(bf16)
        o = ot.T.astype(bf16)
        yield
        got_wo()
        if peer:
            if i == 0:
                moves.store(wo, wo_out)
        for c in range(D // BLK):
            part = dot_nn(o, wo[:, rows_at(c)])
            if peer:
                part = part + part_v[rows_at(i), rows_at(c)].astype(f32)
            mix_v[rows_at(i), rows_at(c)] = part.astype(bf16)
            yield

    def run(local):
        units = []
        for i in range(NBLK):
            for h in range(HEADS):
                units.append((len(units), i, h, *((i, 1) if local else (0, i + 1))))
        drain(project(0))
        side = None
        drain(scores(*units[0]))
        for n, unit in enumerate(units):
            i, h = unit[1:3]
            if h == 0:
                side = iter(())
                steps = []
                if i > 0:
                    steps.append(write(i - 1, units[n - 1][4]))
                if i + 1 < NBLK:
                    steps.append(project(i + 1))
                side = weave(*steps)
                if i + 2 == NBLK:
                    pass
            ahead = []
            if n + 1 < len(units):
                if h == HEADS - 1:
                    drain(side)
                    if i + 2 == NBLK:
                        moves.store(qt_v, qt_out.at[group])
                        moves.store(kt_v, kt_out.at[group])
                ahead = [scores(*units[n + 1])]
            for _ in weave(*ahead, mix(*unit)):
                next(side, None)
                next(side, None)
        drain(side)
        moves.store(stat_v, stat_out.at[group])
        drain(write(NBLK - 1, units[-1][4]))
        moves.store(ot_v, ot_out.at[group])
        moves.finish()

    return run


def attend_main(peer, where, *refs):
    bucket = where[3]

    @pl.when(bucket == 0)
    def _():
        attend_kernel(peer, where, *refs)(True)

    @pl.when(bucket != 0)
    def _():
        attend_kernel(peer, where, *refs)(False)


def attend(where, group, args, saved=()):
    peer = group == 1
    full = ((SEQ, D), bf16)
    outs = [
        ((2, COLS, SEQ), bf16),
        ((2, COLS, SEQ), bf16),
        ((2, SEQ, COLS), bf16),
        ((2, COLS, SEQ), bf16),
        ((2, E_ROWS, LANES), bf16),
        ((2, HEADS, PREFIX_ROWS + 8, SEQ), f32),
    ]
    if peer:
        outs += [((3, D, COLS), bf16), ((COLS, D), bf16), full, full]
        outs += [(a.shape, bf16) for a in args[-2:]]
        scratch = []
    else:
        outs += [full, full, full]
        scratch = [((1, D), f32), ((1, D), f32)]
    scratch += [
        ((3, D, COLS), bf16),
        ((COLS, D), bf16),
        ((2 * PREFIX_ROWS, COLS), bf16),
        ((COLS, SEQ), bf16),
        ((COLS, SEQ), bf16),
        ((SEQ, COLS), bf16),
        ((SEQ, COLS), bf16),
        ((HEADS * EXT, SEQ), bf16),
        ((COLS, SEQ), bf16),
        ((E_ROWS, LANES), bf16),
        ((HEADS, PREFIX_ROWS + 8, SEQ), f32),
        ((2, SEQ, BLK), f32),
    ]
    return call(
        functools.partial(attend_main, peer),
        "attend_peer" if peer else "attend_own",
        where,
        (*args, *saved),
        outs,
        scratch,
        40,
        {1 + len(args) + k: k for k in range(6)} if peer else None,
        flops=10 * 10**9,
        near=4 if peer else 3,
    )


def unit_blocks(u2, dy, shards, g_v, df_v, f_v, da_v, put, side=None):
    k = 0.7978845608028654
    chunks, spans, start = [], [], 0
    for up, down, widths in shards:
        inner = 0
        for size in widths:
            chunks.append((up, down, slice(inner, inner + size), slice(start + inner, start + inner + size)))
            inner += size
        spans.append((up, down, slice(start, start + inner)))
        start += inner
    last = NBLK * len(chunks)

    def products(n):
        i, c = divmod(n, len(chunks))
        up, down, units, _ = chunks[c]
        at, size = rows_at(i), units.stop - units.start
        f_v[n % 2, :, :size] = dot_nn(u2[at, :], up[:, units])
        yield
        da_v[n % 2, :, :size] = dot_nt(dy[at, :], down[units, :])
        yield

    def bend(n):
        i, c = divmod(n, len(chunks))
        units = chunks[c][3]
        size = units.stop - units.start
        for part in range(4):
            at = slice(part * 64, (part + 1) * 64)
            f, da = f_v[n % 2, at, :size], da_v[n % 2, at, :size]
            square = f * f
            t = jnp.tanh(f * (k + (k * 0.044715) * square))
            half = 0.5 * t + 0.5
            g = f * half
            slope = half + g * (1.0 - half) * (2 * k + (6 * k * 0.044715) * square)
            g_v[i % 2, at, units] = g.astype(bf16)
            df_v[i % 2, at, units] = (da * slope).astype(bf16)
            yield

    def close(i):
        for part in range(D // WIDE):
            cols = slice(part * WIDE, (part + 1) * WIDE)
            m = sum(dot_nn(g_v[i % 2, :, span], down[:, cols]) for _, down, span in spans)
            yield
            du = sum(dot_nt(df_v[i % 2, :, span], up[cols, :]) for up, _, span in spans)
            put(i, cols, m, du)
            yield

    side = side or (lambda i: iter(()))
    drain(products(0))
    for n in range(last):
        i, c = divmod(n, len(chunks))
        if c == 0:
            extra = side(i)
        if c == len(chunks) - 1:
            drain(extra)
        for _ in weave(*([products(n + 1)] if n + 1 < last else []), bend(n)):
            next(extra, None)
        if c == len(chunks) - 1:
            drain(close(i))


WIDE = 512


def unit_scratch(units, widest):
    return [
        ((2, BLK, units), bf16),
        ((2, BLK, units), bf16),
        ((2, BLK, widest), f32),
        ((2, BLK, widest), f32),
    ]


def unpack_units(ups, downs, up, down):
    for k, (up_piece, down_piece) in enumerate(zip(ups, downs)):
        up[:, rows_at(k)] = up_piece[:D, :]
        for c in range(D // BLK):
            down[rows_at(k), rows_at(c)] = down_piece[rows_at(c), :]


def mlp_own_kernel(where, x, p0, p1, gain, bias, dy, up, down, more_up, more_down, *refs):
    h1_out, n2_out, r2_out, u2_out, m_out, du_out = refs[:6]
    near_up, near_down, h1_v, g_v, df_v, f_v, da_v, _ = refs[6:]
    half = SEQ // 2
    mine = pl.ds(pl.multiple_of(where[2] * half, half), half)

    def norm(i):
        for part in range(4):
            at = slice(i * BLK + part * 64, i * BLK + part * 64 + 64)
            h1 = x[at, :].astype(f32) + (p0[at, :].astype(f32) + p1[at, :].astype(f32))
            h1_v[at, :] = h1
            normed, inv = norm_rows(h1)
            n2_out[at, :] = normed.astype(bf16)
            r2_out[at, :] = jnp.broadcast_to(inv, (64, 128))
            u2_out[at, :] = (normed * gain[...] + bias[...]).astype(bf16)
            yield

    def put(i, cols, m, du):
        m_out[rows_at(i), cols] = m.astype(bf16)
        du_out[rows_at(i), cols] = du.astype(bf16)

    unpack_units([more_up], [more_down], near_up, near_down)
    drain(norm(0))
    unit_blocks(
        u2_out,
        dy,
        [(up, down, [512] * (up.shape[1] // 512)), (near_up, near_down, [BLK])],
        g_v,
        df_v,
        f_v,
        da_v,
        put,
        lambda i: norm(i + 1) if i + 1 < NBLK else iter(()),
    )
    h1_out[...] = h1_v[mine, :]


def mlp_own(where, *args):
    full = ((SEQ, D), bf16)
    units = args[6].shape[1] + BLK
    return call(
        mlp_own_kernel,
        "mlp_own",
        where,
        [Near(a) for a in args],
        [((SEQ // 2, D), f32), full, ((SEQ, 128), f32), full, full, full],
        [((D, BLK), bf16), ((BLK, D), bf16), ((SEQ, D), f32), *unit_scratch(units, 512)],
        1,
        flops=1,
        near=6,
    )


def mlp_peer_kernel(where, u2, dy, m_in, du_in, *refs):
    ups, downs, refs = refs[:3], refs[3:6], refs[6:]
    wo_own_in, wo_peer_in, ot_in, stat_in, qt_in = refs[:5]
    m_mine, m_other, du_out, wo, ot, stat, qt = refs[5:12]
    m_v, up, down, g_v, df_v, f_v, da_v, sems = refs[12:]
    moves = Moves(sems)
    for source, target in (
        (wo_own_in, wo.at[0]),
        (wo_peer_in, wo.at[1]),
        (ot_in, ot),
        (stat_in, stat),
        (qt_in, qt),
    ):
        moves.store(source, target)

    def put(i, cols, m, du):
        at = rows_at(i)
        m_v[at, cols] = (m_in[at, cols].astype(f32) + m).astype(bf16)
        du_out[at, cols] = (du_in[at, cols].astype(f32) + du).astype(bf16)

    unpack_units(ups, downs, up, down)
    unit_blocks(u2, dy, [(up, down, [BLK] * 3)], g_v, df_v, f_v, da_v, put)
    split_halves(where[2], m_v, m_mine, m_other)
    moves.finish()


def split_halves(side, values, mine, other):
    half = SEQ // 2
    mine[...] = values[pl.ds(pl.multiple_of(side * half, half), half), :]
    other[...] = values[pl.ds(pl.multiple_of((1 - side) * half, half), half), :]


def mlp_peer(where, near, kept):
    ot, stat, qt = kept[2:]
    full = ((SEQ, D), bf16)
    half = ((SEQ // 2, D), bf16)
    units = 3 * BLK
    return call(
        mlp_peer_kernel,
        "mlp_peer",
        where,
        [Near(a) for a in near] + [*kept],
        [half, half, full, ((2, COLS, D), bf16)] + [(a.shape, a.dtype) for a in (ot, stat, qt)],
        [full, ((D, units), bf16), ((units, D), bf16), *unit_scratch(units, BLK)],
        5,
        flops=1,
        near=7,
    )


def turn_kernel(where, *refs):
    own, sib, n2, r2, dy, gain, wo, ot, stat, qt = refs[:10]
    kv_own_in, units_near, w2_own_in, w2_peer_in, v_in, kt_in, w_own_in, w_peer_in = refs[10:18]
    dh_out, dot_v, stat_v, dkv_v, v, kt, w = refs[18:25]
    kv, dh_v, low_v, w2, sems = refs[25:]
    side = where[2]
    moves = Moves(sems)
    got_kv = once([moves.load(kv_own_in, kv.at[0])] + peer_prefix(moves, units_near, kv.at[1]))
    got_w2 = once([moves.load(w2_own_in, w2.at[0]), moves.load(w2_peer_in, w2.at[1])])
    for source, target in (
        (v_in, v),
        (kt_in, kt),
        (w_own_in, w.at[0]),
        (w_peer_in, w.at[1]),
    ):
        moves.store(source, target)

    def norm(i):
        for part in range(4):
            at = slice(i * BLK + part * 64, i * BLK + part * 64 + 64)
            du = own[at, :].astype(f32) + sib[at, :].astype(f32)
            dh = dy[at, :].astype(f32) + norm_back(
                du, n2[at, :].astype(f32), r2[at, 0:1], gain[...]
            )
            dh_v[at, :] = dh
            low_v[at, :] = dh.astype(bf16)
            yield

    def grads(i, g):
        at = rows_at(i)
        do = dot_nt(low_v[at, :], wo[g])
        yield
        do_t = do.T
        yield
        for h in range(HEADS):
            scaled = do_t[head_rows(h)] * stat[g, h, PREFIX_ROWS : PREFIX_ROWS + 1, at]
            dot_v[g, head_rows(h), at] = scaled.astype(bf16)
            balance = jnp.sum(
                scaled * ot[g, head_rows(h), at].astype(f32), axis=0, keepdims=True
            )
            stat_v[g, h, PREFIX_ROWS:, at] = jnp.broadcast_to(balance, (8, BLK))
            yield

    def prefix(g, h):
        got_kv()
        pv = kv[g, PREFIX_ROWS:]
        pv = jnp.where(
            lax.broadcasted_iota(jnp.int32, pv.shape, 1) // HD == h, pv, jnp.zeros_like(pv)
        )
        ep = stat[g, h, :PREFIX_ROWS, :]
        dp = dot_nn(pv, dot_v[g])
        dpv = dot_nt(ep.astype(bf16), dot_v[g, head_rows(h), :])
        yield
        grad = ep * (dp - stat_v[g, h, PREFIX_ROWS : PREFIX_ROWS + 1, :])
        stat_v[g, h, :PREFIX_ROWS, :] = grad
        yield
        dpk = dot_nt(grad.astype(bf16), qt[g, head_rows(h), :])
        yield
        low = 2 * g * PREFIX_ROWS
        dkv_v[low : low + PREFIX_ROWS, head_rows(h)] = dpk * (1.0 / LOG2E)
        dkv_v[low + PREFIX_ROWS : low + 2 * PREFIX_ROWS, head_rows(h)] = dpv

    drain(norm(0))
    for i in range(NBLK):
        drain(grads(i, 0), grads(i, 1), *([norm(i + 1)] if i + 1 < NBLK else []))
    drain(*[prefix(g, h) for g in range(2) for h in range(HEADS)])
    got_w2()
    da = 0.0
    for n in range(4):
        grad = dkv_v[n * PREFIX_ROWS : (n + 1) * PREFIX_ROWS, :].astype(bf16)
        da = da + dot_nt(grad, w2[n // 2, :, (n % 2) * COLS : (n % 2 + 1) * COLS])
    dkv_v[4 * PREFIX_ROWS : 5 * PREFIX_ROWS, :] = da[:, :COLS]
    dkv_v[5 * PREFIX_ROWS :, :] = da[:, COLS:]
    half = SEQ // 2
    dh_out[...] = dh_v[pl.ds(pl.multiple_of(side * half, half), half), :]
    moves.finish()


def turn(where, near, small, kept):
    v, kt = kept[:2]
    return call(
        turn_kernel,
        "turn",
        where,
        [Near(a) for a in near] + [*small, *kept],
        [
            ((SEQ // 2, D), f32),
            ((2, COLS, SEQ), bf16),
            ((2, HEADS, PREFIX_ROWS + 8, SEQ), f32),
            ((6 * PREFIX_ROWS, COLS), f32),
        ]
        + [(a.shape, bf16) for a in (v, kt)]
        + [((2, 3, D, COLS), bf16)],
        [
            ((2, 2 * PREFIX_ROWS, COLS), bf16),
            ((SEQ, D), f32),
            ((SEQ, D), bf16),
            ((2, 2 * COLS, 2 * COLS), bf16),
        ],
        8,
        flops=6 * 10**9,
        near=7,
    )


def attend_back_kernel(where, *refs):
    do_t, qt, v, kt, stat, w, e_in, kv_own_in, units_near, x_in = refs[:10]
    mine_out, other_out, x_v, e, kv, dkt, dvt, du_v, ds_v, sems = refs[10:]
    slot, side = where[0], where[2]
    half = SEQ // 2
    moves = Moves(sems)
    kv_loads = [moves.load(kv_own_in, kv.at[0])] + peer_prefix(moves, units_near, kv.at[1])
    moves.store(x_in.at[pl.ds(pl.multiple_of(slot * SEQ + side * half, half), half)], x_v)

    def run(local):
        spans = [(i, 1) if local else (0, i + 1) for i in range(NBLK)]
        last = NBLK - 1
        parts = Moves(sems)
        parts.used = moves.used
        e_got = {}
        for i in reversed(range(NBLK)):
            at = slice(TRI[i], TRI[i] + spans[i][1] * BLK)
            for g in range(2):
                for h in range(HEADS):
                    if i == last and g == 0:
                        lanes = head_lanes(h)
                        e_got[i, g, h] = once([parts.load(e_in.at[g, at, lanes], e.at[g, at, lanes])])
                    elif h == 0:
                        e_got[i, g, h] = once([parts.load(e_in.at[g, at], e.at[g, at])])
        once(kv_loads)()
        dqs = {}

        def slopes(n, i, g, h, first, count):
            here = rows_at(i)
            do_h = do_t[g, :, here]
            do_h = jnp.where(
                lax.broadcasted_iota(jnp.int32, do_h.shape, 0) // HD == h, do_h, jnp.zeros_like(do_h)
            )
            balance = stat[g, h, PREFIX_ROWS : PREFIX_ROWS + 1, here]
            if (i, g, h) in e_got:
                e_got[i, g, h]()
            for c in range(count):
                dp = dot_nn(v[g, rows_at(first + c), :], do_h)
                e_low = e[g, TRI[i] + c * BLK : TRI[i] + (c + 1) * BLK, head_lanes(h)]
                ds_v[n % 2, rows_at(c), :] = (e_low.astype(f32) * (dp - balance)).astype(bf16)
                yield

        def use(n, i, g, h, first, count):
            heads, here = head_rows(h), rows_at(i)
            pk_t = kv[g, :PREFIX_ROWS].astype(f32).T.astype(bf16)
            dq = dot_nn(pk_t[heads], stat[g, h, :PREFIX_ROWS, here].astype(bf16))
            for c in range(count):
                at = rows_at(first + c)
                e_low = e[g, TRI[i] + c * BLK : TRI[i] + (c + 1) * BLK, head_lanes(h)]
                ds = ds_v[n % 2, rows_at(c), :]
                dv = dot_nt(do_t[g, heads, here], e_low)
                dk = dot_nt(qt[g, heads, here], ds)
                if local or i == last:
                    dvt[g, heads, at] = dv
                    dkt[g, heads, at] = dk
                else:
                    dvt[g, heads, at] += dv
                    dkt[g, heads, at] += dk
                dq = dq + dot_nn(kt[g, heads, at], ds)
                yield
            dqs[i, g, h] = dq

        def share(i):
            here = rows_at(i)
            grads = []
            for g in range(2):
                dq = jnp.concatenate([dqs.pop((i, g, h)) for h in range(HEADS)], axis=0)
                for value, scale in ((dq, SCALE), (dkt[g, :, here], 1.0 / LOG2E), (dvt[g, :, here], 1.0)):
                    grads.append((value.T * scale).astype(bf16))
                    yield
            for c in range(D // BLK):
                total = None
                for g in range(2):
                    for part in range(3):
                        term = dot_nt(grads[3 * g + part], w[g, part, rows_at(c), :])
                        total = term if total is None else total + term
                du_v[here, rows_at(c)] = total.astype(bf16)
                yield

        units = []
        for i in reversed(range(NBLK)):
            for g in range(2):
                for h in range(HEADS):
                    units.append((len(units), i, g, h, *spans[i]))
        tail = iter(())
        drain(slopes(*units[0]))
        for n, unit in enumerate(units):
            i, g, h = unit[1:4]
            ahead = [slopes(*units[n + 1])] if n + 1 < len(units) else []
            for _ in weave(*ahead, use(*unit)):
                next(tail, None)
            if g == 1 and h == HEADS - 1:
                drain(tail)
                tail = share(i)
        drain(tail)

    bucket = where[3]

    @pl.when(bucket == 0)
    def _():
        run(True)

    @pl.when(bucket != 0)
    def _():
        run(False)

    split_halves(side, du_v, mine_out, other_out)
    moves.finish()


def attend_back(where, near, e, kv_own, units_near, x):
    half = ((SEQ // 2, D), bf16)
    return call(
        attend_back_kernel,
        "attend_back",
        where,
        [Near(a) for a in near] + [e, kv_own, units_near, x],
        [half, half, half],
        [
            ((2, E_ROWS, LANES), bf16),
            ((2, 2 * PREFIX_ROWS, COLS), bf16),
            ((2, COLS, SEQ), f32),
            ((2, COLS, SEQ), f32),
            ((SEQ, D), bf16),
            ((2, SEQ, BLK), bf16),
        ],
        16,
        flops=16 * 10**9,
        near=3,
    )


def finish_kernel(where, own, sib, x, dh, gain, out, out_v, sems):
    moves = Moves(sems)
    size = 64
    for n in range(SEQ // 2 // size):
        at = slice(n * size, (n + 1) * size)
        normed, inv = norm_rows(x[at, :].astype(f32))
        du = own[at, :].astype(f32) + sib[at, :].astype(f32)
        out_v[at, :] = dh[at, :] + norm_back(du, normed, inv, gain[...])
        moves.store(out_v.at[at], out.at[at])
    moves.finish()


def finish(where, *args):
    wide = ((SEQ // 2, D), f32)
    return call(finish_kernel, "finish", where, [Near(a) for a in args], [wide], [wide], 8)[0]


def result_kernel(where, h1, own, sib, after, out, out_v, sems):
    moves = Moves(sems)
    size = 64
    for n in range(SEQ // 2 // size):
        at = slice(n * size, (n + 1) * size)
        out_v[at, :] = (h1[at, :] + (own[at, :].astype(f32) + sib[at, :].astype(f32))).astype(bf16)
        moves.store(out_v.at[at], out.at[at])
    moves.finish()


def result(where, h1, own, sib, after):
    half = ((SEQ // 2, D), bf16)
    return call(
        result_kernel, "result", where, [Near(h1), Near(own), Near(sib), Loose(after)], [half], [half], 8
    )[0]


def swap(values, axis, bit):
    size = lax.axis_size(axis)
    return lax.ppermute(values, axis, [(n, n ^ bit) for n in range(size)])


def after(values, *others):
    return lax.optimization_barrier((values, *others))[0]


def other_half(values, side):
    half = values.shape[0] // 2
    return lax.dynamic_slice_in_dim(values, (1 - side) * half, half, 0)


def on_device(
    inputs,
    buckets,
    ln1_gain,
    ln1_bias,
    w_qkv,
    w_out,
    ln2_gain,
    ln2_bias,
    w_up,
    w_down,
    prefix_embed,
    prefix_w1,
    prefix_b1,
    prefix_w2,
    prefix_b2,
    cotangent,
):
    prefix_count = prefix_embed.shape[0]
    width = prefix_w1.shape[1]
    member = lax.axis_index("tensor")
    place = lax.axis_index("batch") & 3
    side = member & 1
    slot = member // 2
    where = jnp.stack([slot, place, side, buckets[slot]]).astype(jnp.int32)
    w = w_qkv.transpose(1, 0, 2)
    w2_flat = prefix_w2.reshape(width, 2 * COLS)
    gain1, bias1 = ln1_gain.reshape(1, D), ln1_bias.reshape(1, D)
    gain2, bias2 = ln2_gain.reshape(1, D), ln2_bias.reshape(1, D)
    embed = jnp.pad(prefix_embed, ((0, PREFIX_ROWS - prefix_count), (0, 0)))

    def across(values):
        return swap(values, "tensor", 2)

    first_near = across(pack(w, w_out))
    hidden, kv_own, up_near, down_near, up_far, down_far = prefix_forward(
        embed,
        prefix_w1,
        prefix_b1.reshape(1, width),
        w2_flat,
        prefix_b2.reshape(1, 2 * COLS),
        w_up,
        w_down,
    )
    up_near = across(up_near)
    down_near = across(after(down_near, where))
    first_beside = swap(first_near, "batch", 1)
    first_above = swap(first_near, "batch", 2)
    *saved, x, u1, part = attend(
        where, 0, (after(inputs, first_near), gain1, bias1, w, w_out, kv_own)
    )
    half = first_near.shape[0] // 2
    first_top = swap(after(first_above, u1)[:half], "batch", 1)
    first_bottom = swap(after(first_beside, u1)[half:], "batch", 2)
    first = (first_near, first_beside, first_above, first_top, first_bottom)
    up_sent = after(up_near, u1)
    up_far = across(after(up_far, u1))
    up_beside = swap(up_sent, "batch", 1)
    up_above = swap(up_sent, "batch", 2)
    *saved, w_peer, wo_peer, part, dy, up, down = attend(
        where,
        1,
        (*[Near(a) for a in (u1, *first, up_near, after(part, down_near))], cotangent, w_up, w_down),
        saved,
    )
    part_sib = swap(after(part, up_beside, up_above, up_far), "tensor", 1)
    down_sent = after(down_near, part)
    down_beside = swap(down_sent, "batch", 1)
    down_above = swap(down_sent, "batch", 2)
    down_far = across(after(down_far, part))
    qt, kt, v, ot, e, stat = saved
    h1, n2, r2, u2, m, du = mlp_own(
        where, x, part, part_sib, gain2, bias2, dy, up, down, up_near, down_near
    )
    w2_peer = across(after(w2_flat, part))
    m_mine, m_other, du, wo_pair, ot, stat, qt = mlp_peer(
        where,
        (u2, dy, m, du, up_beside, up_above, up_far, down_beside, down_above, down_far),
        (w_out, wo_peer, ot, stat, qt),
    )
    du_sib = swap(after(du, w2_peer), "tensor", 1)
    m_sib = swap(m_other, "tensor", 1)
    dh, do_t, stat, dkv, v, kt, w_pair = turn(
        where,
        (du, du_sib, n2, r2, dy, gain2, wo_pair, ot, stat, qt),
        (kv_own, Loose(up_near), w2_flat, Loose(w2_peer)),
        (v, kt, w, w_peer),
    )

    dkv_peer = across(dkv)
    output = result(where, h1, m_mine, m_sib, dkv)
    dkv_peer = after(dkv_peer, output)
    rows = 2 * PREFIX_ROWS
    sums = jnp.concatenate(
        [dkv[:rows] + dkv_peer[rows : 2 * rows], dkv[2 * rows :] + dkv_peer[2 * rows :]], axis=0
    )
    bits = [1 << n for n in reversed(range(lax.axis_size("batch").bit_length() - 1))]
    sums_away = swap(sums, "batch", bits[0])
    du1_mine, du1_other, x = attend_back(
        where, (after(do_t, sums), qt, v, kt, stat, w_pair), e, kv_own, Loose(up_near), inputs
    )
    du1_sib = swap(after(du1_other, sums_away), "tensor", 1)
    sums = sums + after(sums_away, du1_mine)
    input_grad = finish(where, du1_mine, after(du1_sib, sums), x, dh, gain1)
    sums = sums + after(swap(sums, "batch", bits[1]), input_grad)
    for bit in bits[2:]:
        sums = sums + swap(sums, "batch", bit)
    da = sums[rows:] + swap(sums[rows:], "tensor", 1)
    w2_grad, b2_grad, embed_grad, w1_grad, b1_grad = prefix_back(
        sums[:rows], da, hidden, embed, prefix_w1
    )
    return (
        output,
        input_grad,
        embed_grad[:prefix_count],
        w1_grad,
        b1_grad.reshape(width),
        w2_grad,
        b2_grad,
    )


def solution(mesh):
    placed = (
        P("batch", None),
        P("batch"),
        P(),
        P(),
        P(None, None, "tensor"),
        P("tensor", None),
        P(),
        P(),
        P(None, "tensor"),
        P("tensor", None),
        P(),
        P(),
        P(),
        P(None, None, "tensor"),
        P(None, "tensor"),
        P("batch", None),
    )
    return jax.shard_map(
        on_device,
        mesh=mesh,
        in_specs=placed,
        out_specs=(
            P(("batch", "tensor"), None),
            P(("batch", "tensor"), None),
            P(),
            P(),
            P(),
            P(None, None, "tensor"),
            P(None, "tensor"),
        ),
        check_vma=False,
    )
```

```python
import functools
import math

import jax
import jax.numpy as jnp
from jax import lax
from jax.experimental import pallas as pl
from jax.experimental.pallas import tpu as pltpu
from jax.sharding import PartitionSpec as P

D = 1024
HD = 64
SEQ = 1024
HEADS = 4
COLS = HEADS * HD
BLK = 256
NBLK = SEQ // BLK
HALF = NBLK // 2
LANES = HEADS * BLK
PREFIX_ROWS = 16
EXT = HD + 16
TRI = [BLK * i * (i + 1) // 2 for i in range(NBLK)]
E_ROWS = BLK * NBLK * (NBLK + 1) // 2
LOG2E = 1.4426950408889634
SCALE = 0.125
FAR = -1e30
MASKED = -1e9 * LOG2E
MIB = 1 << 20

f32 = jnp.float32
bf16 = jnp.bfloat16
precise = lax.Precision.HIGHEST


def dot_nn(a, b):
    return lax.dot_general(a, b, (((1,), (0,)), ((), ())), preferred_element_type=f32)


def dot_nt(a, b):
    return lax.dot_general(a, b, (((1,), (1,)), ((), ())), preferred_element_type=f32)


def exact(a, b, dims):
    return lax.dot_general(a, b, (dims, ((), ())), precision=precise, preferred_element_type=f32)


def norm_rows(values):
    average = jnp.mean(values, axis=-1, keepdims=True)
    centred = values - average
    inv = lax.rsqrt(jnp.mean(centred * centred, axis=-1, keepdims=True) + 1e-05)
    return centred * inv, inv


def norm_back(incoming, normed, inv, gain):
    scaled = incoming * gain
    return inv * (
        scaled
        - jnp.mean(scaled, axis=-1, keepdims=True)
        - normed * jnp.mean(scaled * normed, axis=-1, keepdims=True)
    )


def head_lanes(h):
    return slice(h * BLK, (h + 1) * BLK)


def head_rows(h):
    return slice(h * HD, (h + 1) * HD)


def head_blocks(cols):
    row_head = lax.broadcasted_iota(jnp.int32, cols.shape, 0) // HD
    return jnp.concatenate(
        [jnp.where(row_head == h, cols, jnp.zeros_like(cols)) for h in range(HEADS)], axis=1
    )


class Loose:
    def __init__(self, array):
        self.array = array


class Near:
    def __init__(self, array):
        self.array = array


def placed(a):
    if isinstance(a, Loose):
        return a.array
    if isinstance(a, Near):
        return pltpu.with_memory_space_constraint(a.array, pltpu.VMEM)
    return pltpu.with_memory_space_constraint(a, pltpu.HBM)


def hbm(*arrays):
    return [placed(a) for a in arrays]


def plain(arrays):
    return [a.array if isinstance(a, (Loose, Near)) else a for a in arrays]


def rows_at(i, count=1):
    return slice(i * BLK, (i + count) * BLK)


class Moves:
    def __init__(self, sems):
        self.sems = sems
        self.used = 0
        self.out = []
        self.halves = []

    def load(self, source, target):
        copy = pltpu.make_async_copy(source, target, self.sems.at[self.used])
        self.used += 1
        copy.start()
        return copy

    def store(self, source, target):
        self.out.append(self.load(source, target))

    def store_half(self, source, same, at, mine, other):
        sem = self.sems.at[self.used]
        self.used += 1
        here = pltpu.make_async_copy(source, mine.at[at], sem)
        there = pltpu.make_async_copy(source, other.at[at], sem)
        pl.when(same)(here.start)
        pl.when(jnp.logical_not(same))(there.start)
        self.halves.append((same, here, there))

    def finish(self):
        for copy in self.out:
            copy.wait()
        for same, here, there in self.halves:
            pl.when(same)(here.wait)
            pl.when(jnp.logical_not(same))(there.wait)


def once(copies):
    left = list(copies)

    def wait():
        while left:
            left.pop().wait()

    return wait


def weave(*tasks):
    live = list(tasks)
    while live:
        for task in list(live):
            if next(task, live) is live:
                live.remove(task)
        yield


def drain(*tasks):
    for _ in weave(*tasks):
        pass


ANY = pl.BlockSpec(memory_space=pl.ANY)
SMALL = pl.BlockSpec(memory_space=pltpu.SMEM)


def room(scratch):
    return sum(math.prod(shape) * jnp.dtype(kind).itemsize for shape, kind in scratch)


FULL = pl.BlockSpec(memory_space=pltpu.VMEM)


def call(kernel, name, where, args, outs, scratch, sems, aliases=None, flops=0, near=0):
    far = len(outs) - near
    return pl.pallas_call(
        kernel,
        in_specs=[SMALL] + [FULL if isinstance(a, Near) else ANY for a in args],
        out_specs=[ANY] * far + [FULL] * near,
        out_shape=[pltpu.HBM(shape, kind) for shape, kind in outs[:far]]
        + [pltpu.VMEM(shape, kind) for shape, kind in outs[far:]],
        scratch_shapes=[pltpu.VMEM(shape, kind) for shape, kind in scratch]
        + [pltpu.SemaphoreType.DMA((sems,))],
        input_output_aliases=aliases or {},
        compiler_params=pltpu.CompilerParams(
            vmem_limit_bytes=room(scratch) // MIB * MIB + 8 * MIB
        ),
        cost_estimate=pl.CostEstimate(
            flops=flops,
            transcendentals=0,
            bytes_accessed=sum(a.size * a.dtype.itemsize for a in plain(args)),
        ),
        name=name,
    )(where, *hbm(*args))


def unpack_first(place, pieces, w, wo):
    rows, thin = D // 4, COLS // 4
    near, beside, above, top, bottom = pieces
    for k in range(4):

        def rows_of(first, count):
            if k < 3:
                return (near, beside, above)[k][first : first + count, :]
            half = 2 * BLK
            return (top if first < half else bottom)[first % half : first % half + count, :]

        at = pl.ds(pl.multiple_of((place ^ k) * rows, rows), rows)
        for part in range(3):
            w[part, at, :] = rows_of(part * BLK, BLK)
        at = pl.ds(pl.multiple_of((place ^ k) * thin, thin), thin)
        for c in range(D // COLS):
            wo[at, rows_at(c)] = rows_of(3 * BLK + c * thin, thin)


def pack_pieces(moves, place, w, wo, out):
    rows, thin = D // 4, COLS // 4
    at = pl.ds(pl.multiple_of(place * rows, rows), rows)
    for part in range(3):
        moves.store(w.at[part, at], out.at[rows_at(part)])
    at = pl.ds(pl.multiple_of(place * thin, thin), thin)
    for c in range(D // COLS):
        moves.store(
            wo.at[at, c * COLS : (c + 1) * COLS],
            out.at[3 * BLK + c * thin : 3 * BLK + (c + 1) * thin],
        )


def pack_kernel(w, wo, out, sems):
    moves = Moves(sems)
    pack_pieces(moves, lax.axis_index("batch") & 3, w, wo, out)
    moves.finish()


def pack(w, wo):
    return pl.pallas_call(
        pack_kernel,
        in_specs=[ANY, ANY],
        out_specs=pl.BlockSpec(memory_space=pltpu.VMEM),
        out_shape=jax.ShapeDtypeStruct((4 * BLK, COLS), bf16),
        scratch_shapes=[pltpu.SemaphoreType.DMA((7,))],
        name="pack",
    )(*hbm(w, wo))


def prefix_kernel(embed, w1, b1, w2, b2, up, down, *refs):
    hidden_out, kv_out, up_near, down_near, up_far, down_far, sems = refs
    place = lax.axis_index("batch") & 3
    moves = Moves(sems)
    for bits, up_out, down_out in ((0, up_near, down_near), (3, up_far, down_far)):
        units = pl.ds(pl.multiple_of((place ^ bits) * BLK, BLK), BLK)
        moves.store(up.at[:, units], up_out.at[:D])
        for c in range(D // BLK):
            moves.store(down.at[units, rows_at(c)], down_out.at[rows_at(c)])
    hidden = jnp.tanh(dot_nn(embed[...], w1[...]) + b1[...])
    kv = exact(hidden, w2[...].astype(f32), ((1,), (0,))) + b2[...]
    real = lax.broadcasted_iota(jnp.int32, kv.shape, 0) < 10
    kv = jnp.where(real, kv, 0.0)
    hidden_out[...] = hidden
    kv = jnp.concatenate([kv[:, :COLS], kv[:, COLS:]], axis=0).astype(bf16)
    kv_out[...] = kv
    up_near[D:, :] = kv
    moves.finish()


def prefix_forward(embed, w1, b1, w2, b2, up, down):
    width = w1.shape[1]
    full = pl.BlockSpec(memory_space=pltpu.VMEM)
    return pl.pallas_call(
        prefix_kernel,
        in_specs=[full] * 5 + [ANY] * 2,
        out_specs=[full] * 6,
        out_shape=(
            pltpu.HBM((PREFIX_ROWS, width), f32),
            pltpu.HBM((2 * PREFIX_ROWS, COLS), bf16),
            jax.ShapeDtypeStruct((D + 2 * PREFIX_ROWS, BLK), bf16),
            jax.ShapeDtypeStruct((D, BLK), bf16),
            jax.ShapeDtypeStruct((D, BLK), bf16),
            jax.ShapeDtypeStruct((D, BLK), bf16),
        ),
        scratch_shapes=[pltpu.SemaphoreType.DMA((10,))],
        compiler_params=pltpu.CompilerParams(vmem_limit_bytes=24 * MIB),
        name="prefix_forward",
    )(*hbm(embed, w1, b1, w2, b2, up, down))


def peer_prefix(moves, units_near, kv):
    return [moves.load(units_near.at[D:], kv)]


def prefix_back_kernel(dkv, da, hidden, embed, w1, w2_out, b2_out, embed_out, w1_out, b1_out):
    wide = hidden[...]
    low = wide.astype(bf16)
    over_rows = (((0,), (0,)), ((), ()))
    for part in range(2):
        grad = dkv[part * PREFIX_ROWS : (part + 1) * PREFIX_ROWS, :]
        w2_out[:, part, :] = lax.dot_general(
            low, grad.astype(bf16), over_rows, preferred_element_type=f32
        )
        b2_out[part : part + 1, :] = jnp.sum(grad, axis=0, keepdims=True)
    pre = jnp.concatenate([da[:PREFIX_ROWS], da[PREFIX_ROWS:]], axis=1) * (1.0 - wide * wide)
    b1_out[...] = jnp.sum(pre, axis=0, keepdims=True)
    pre_low = pre.astype(bf16)
    w1_out[...] = lax.dot_general(embed[...], pre_low, over_rows, preferred_element_type=f32)
    embed_out[...] = dot_nt(pre_low, w1[...])


def prefix_back(dkv, da, hidden, embed, w1):
    width = w1.shape[1]
    return pl.pallas_call(
        prefix_back_kernel,
        out_shape=(
            pltpu.HBM((width, 2, COLS), f32),
            pltpu.HBM((2, COLS), f32),
            pltpu.HBM((PREFIX_ROWS, D), f32),
            pltpu.HBM((D, width), f32),
            pltpu.HBM((1, width), f32),
        ),
        compiler_params=pltpu.CompilerParams(vmem_limit_bytes=24 * MIB),
        name="prefix_back",
    )(dkv, da, *hbm(Near(hidden), Near(embed), Near(w1)))


def attend_kernel(peer, where, *refs):
    slot, place, bucket = where[0], where[1], where[3]
    if peer:
        u1_v, *pieces = refs[:6]
        units_near, part_v, up_in = refs[6:9]
        refs = refs[9 + 6 :]
    else:
        x_in, gain_in, bias_in, w_in, wo_in, kv_in, dy_in, down_in = refs[:8]
        refs = refs[8:]
    qt_out, kt_out, v_out, ot_out, e_out, stat_out = refs[:6]
    if peer:
        w_out, wo_out, mix_v, up_v = refs[6:10]
        w, wo, kv, qt_v, kt_v, k_v, v_v, vt_v, ot_v, e_v, stat_v, s_v, sems = refs[10:]
    else:
        rows_v, u1_v, mix_v, dy_v, down_v = refs[6:11]
        gain, bias, w, wo, kv, qt_v, kt_v, k_v, v_v, vt_v, ot_v, e_v, stat_v, s_v, sems = (
            refs[11:]
        )
    group = 1 if peer else 0
    moves = Moves(sems)
    if peer:
        unpack_first(place, pieces, w, wo)
        kv[...] = units_near[D:, :]
        got_w = got_wo = got_kv = once([])
        moves.store(up_in, up_v)
    else:
        got_norm = once([moves.load(gain_in, gain), moves.load(bias_in, bias)])
        first = pl.multiple_of(slot * SEQ, SEQ)
        rows = [moves.load(x_in.at[pl.ds(first, BLK)], rows_v.at[rows_at(0)])]
        got_w = once([moves.load(w_in, w)])
        got_kv = once([moves.load(kv_in, kv)])
        rows += [
            moves.load(x_in.at[pl.ds(first + i * BLK, BLK)], rows_v.at[rows_at(i)])
            for i in range(1, NBLK)
        ]
        got_wo = once([moves.load(wo_in, wo)])
        moves.store(dy_in.at[pl.ds(first, SEQ)], dy_v)
        moves.store(down_in, down_v)
    filler = jnp.where(
        lax.broadcasted_iota(jnp.int32, (EXT - HD, SEQ), 0) == 0, 1.0, 0.0
    ).astype(bf16)
    for h in range(HEADS):
        vt_v[h * EXT + HD : (h + 1) * EXT, :] = filler

    def project(i):
        if not peer:
            rows[i].wait()
            got_norm()
            for part in range(4):
                at = slice(i * BLK + part * 64, i * BLK + part * 64 + 64)
                normed, _ = norm_rows(rows_v[at, :].astype(f32))
                u1_v[at, :] = (normed * gain[...] + bias[...]).astype(bf16)
                yield
        u1 = u1_v[rows_at(i), :]
        got_w()
        if peer and i == 0:
            moves.store(w, w_out)
        keys = dot_nn(u1, w[1])
        yield
        qs = dot_nn(u1, w[0])
        k_v[rows_at(i), :] = keys.astype(bf16)
        kt_v[:, rows_at(i)] = keys.T.astype(bf16)
        yield
        values = dot_nn(u1, w[2])
        qt_v[:, rows_at(i)] = (qs * (SCALE * LOG2E)).T.astype(bf16)
        yield
        v_v[rows_at(i), :] = values.astype(bf16)
        values_t = values.T.astype(bf16)
        for h in range(HEADS):
            vt_v[h * EXT : h * EXT + HD, rows_at(i)] = values_t[head_rows(h)]
        moves.store(v_v.at[rows_at(i)], v_out.at[group, rows_at(i)])
        yield

    tops = {}
    done = {}

    def scores(n, i, h, first, count):
        got_kv()
        qt = qt_v[:, rows_at(i)]
        q_h = jnp.where(
            lax.broadcasted_iota(jnp.int32, qt.shape, 0) // HD == h, qt, jnp.zeros_like(qt)
        )
        real = lax.broadcasted_iota(jnp.int32, (PREFIX_ROWS, BLK), 0) < 10
        prefix = jnp.where(real, dot_nn(kv[:PREFIX_ROWS], q_h), FAR)
        top = jnp.max(prefix, axis=0, keepdims=True)
        for c in range(count):
            block = dot_nn(k_v[rows_at(first + c), :], q_h)
            if c == count - 1:
                keep = lax.broadcasted_iota(jnp.int32, (BLK, BLK), 0) <= lax.broadcasted_iota(
                    jnp.int32, (BLK, BLK), 1
                )
                block = jnp.where(keep, block, MASKED)
            s_v[n % 2, rows_at(c), :] = block
            top = jnp.maximum(top, jnp.max(block, axis=0, keepdims=True))
            yield
        tops[n] = prefix, top

    def mix(n, i, h, first, count):
        prefix, top = tops.pop(n)
        ep = jnp.exp2(prefix - top)
        stat_v[h, :PREFIX_ROWS, rows_at(i)] = ep
        one = jnp.where(
            lax.broadcasted_iota(jnp.int32, (EXT - HD, PREFIX_ROWS), 0) == 0, 1.0, 0.0
        )
        pv_t = kv[PREFIX_ROWS:].astype(f32).T
        pv_ext = jnp.concatenate([pv_t[head_rows(h)], one], axis=0).astype(bf16)
        mixed = dot_nn(pv_ext, ep.astype(bf16))
        for c in range(count):
            e_low = jnp.exp2(s_v[n % 2, rows_at(c), :] - top).astype(bf16)
            e_v[TRI[i] + c * BLK : TRI[i] + (c + 1) * BLK, head_lanes(h)] = e_low
            mixed = mixed + dot_nn(vt_v[h * EXT : (h + 1) * EXT, rows_at(first + c)], e_low)
            yield
        e_at = slice(TRI[i], TRI[i] + count * BLK)
        moves.store(e_v.at[e_at, head_lanes(h)], e_out.at[group, e_at, head_lanes(h)])
        inv = 1.0 / mixed[HD : HD + 1]
        stat_v[h, PREFIX_ROWS:, rows_at(i)] = jnp.broadcast_to(inv, (8, BLK))
        done[n] = mixed[:HD] * inv

    def write(i, count):
        ot = jnp.concatenate([done.pop(i * HEADS + h) for h in range(HEADS)], axis=0)
        ot_v[:, rows_at(i)] = ot.astype(bf16)
        o = ot.T.astype(bf16)
        yield
        got_wo()
        if peer:
            if i == 0:
                moves.store(wo, wo_out)
        for c in range(D // BLK):
            part = dot_nn(o, wo[:, rows_at(c)])
            if peer:
                part = part + part_v[rows_at(i), rows_at(c)].astype(f32)
            mix_v[rows_at(i), rows_at(c)] = part.astype(bf16)
            yield

    def run(local):
        units = []
        for i in range(NBLK):
            for h in range(HEADS):
                units.append((len(units), i, h, *((i, 1) if local else (0, i + 1))))
        drain(project(0))
        side = None
        drain(scores(*units[0]))
        for n, unit in enumerate(units):
            i, h = unit[1:3]
            if h == 0:
                side = iter(())
                steps = []
                if i > 0:
                    steps.append(write(i - 1, units[n - 1][4]))
                if i + 1 < NBLK:
                    steps.append(project(i + 1))
                side = weave(*steps)
                if i + 2 == NBLK:
                    pass
            ahead = []
            if n + 1 < len(units):
                if h == HEADS - 1:
                    drain(side)
                    if i + 2 == NBLK:
                        moves.store(qt_v, qt_out.at[group])
                        moves.store(kt_v, kt_out.at[group])
                ahead = [scores(*units[n + 1])]
            for _ in weave(*ahead, mix(*unit)):
                next(side, None)
                next(side, None)
        drain(side)
        moves.store(stat_v, stat_out.at[group])
        drain(write(NBLK - 1, units[-1][4]))
        moves.store(ot_v, ot_out.at[group])
        moves.finish()

    return run


def attend_main(peer, where, *refs):
    bucket = where[3]

    @pl.when(bucket == 0)
    def _():
        attend_kernel(peer, where, *refs)(True)

    @pl.when(bucket != 0)
    def _():
        attend_kernel(peer, where, *refs)(False)


def attend(where, group, args, saved=()):
    peer = group == 1
    full = ((SEQ, D), bf16)
    outs = [
        ((2, COLS, SEQ), bf16),
        ((2, COLS, SEQ), bf16),
        ((2, SEQ, COLS), bf16),
        ((2, COLS, SEQ), bf16),
        ((2, E_ROWS, LANES), bf16),
        ((2, HEADS, PREFIX_ROWS + 8, SEQ), f32),
    ]
    if peer:
        outs += [((3, D, COLS), bf16), ((COLS, D), bf16), full, (args[-1].shape, bf16)]
        scratch = []
    else:
        outs += [full, full, full, full, (args[-1].shape, bf16)]
        scratch = [((1, D), f32), ((1, D), f32)]
    scratch += [
        ((3, D, COLS), bf16),
        ((COLS, D), bf16),
        ((2 * PREFIX_ROWS, COLS), bf16),
        ((COLS, SEQ), bf16),
        ((COLS, SEQ), bf16),
        ((SEQ, COLS), bf16),
        ((SEQ, COLS), bf16),
        ((HEADS * EXT, SEQ), bf16),
        ((COLS, SEQ), bf16),
        ((E_ROWS, LANES), bf16),
        ((HEADS, PREFIX_ROWS + 8, SEQ), f32),
        ((2, SEQ, BLK), f32),
    ]
    return call(
        functools.partial(attend_main, peer),
        "attend_peer" if peer else "attend_own",
        where,
        (*args, *saved),
        outs,
        scratch,
        40,
        {1 + len(args) + k: k for k in range(6)} if peer else None,
        flops=10 * 10**9,
        near=2 if peer else 5,
    )


def unit_blocks(u2, dy, shards, g_v, df_v, f_v, da_v, put, side=None):
    k = 0.7978845608028654
    chunks, spans, start = [], [], 0
    for up, down, widths, known in shards:
        inner = 0
        for size in widths:
            chunks.append(
                (up, down, slice(inner, inner + size), slice(start + inner, start + inner + size), known)
            )
            inner += size
        spans.append((up, down, slice(start, start + inner)))
        start += inner
    last = NBLK * len(chunks)

    def products(n):
        i, c = divmod(n, len(chunks))
        up, down, units, _, known = chunks[c]
        at, size = rows_at(i), units.stop - units.start
        f_v[n % 2, :, :size] = dot_nn(u2[at, :], up[:, units])
        yield
        if known is None:
            da_v[n % 2, :, :size] = dot_nt(dy[at, :], down[units, :])
            yield

    def bend(n):
        i, c = divmod(n, len(chunks))
        _, _, inner, units, known = chunks[c]
        size = units.stop - units.start
        for part in range(4):
            at = slice(part * 64, (part + 1) * 64)
            f = f_v[n % 2, at, :size]
            if known is None:
                da = da_v[n % 2, at, :size]
            else:
                da = known[i * BLK + part * 64 : i * BLK + part * 64 + 64, inner].astype(f32)
            square = f * f
            t = jnp.tanh(f * (k + (k * 0.044715) * square))
            half = 0.5 * t + 0.5
            g = f * half
            slope = half + g * (1.0 - half) * (2 * k + (6 * k * 0.044715) * square)
            g_v[i % 2, at, units] = g.astype(bf16)
            df_v[i % 2, at, units] = (da * slope).astype(bf16)
            yield

    def close(i):
        for part in range(D // WIDE):
            cols = slice(part * WIDE, (part + 1) * WIDE)
            m = sum(dot_nn(g_v[i % 2, :, span], down[:, cols]) for _, down, span in spans)
            yield
            du = sum(dot_nt(df_v[i % 2, :, span], up[cols, :]) for up, _, span in spans)
            put(i, cols, m, du)
            yield

    side = side or (lambda i: iter(()))
    drain(products(0))
    for n in range(last):
        i, c = divmod(n, len(chunks))
        if c == 0:
            extra = side(i)
        if c == len(chunks) - 1:
            drain(extra)
        for _ in weave(*([products(n + 1)] if n + 1 < last else []), bend(n)):
            next(extra, None)
        if c == len(chunks) - 1:
            drain(close(i))


def cotangent_units_kernel(where, dy, down, out, sems):
    for i in range(NBLK):
        for c in range(down.shape[0] // WIDE):
            units = slice(c * WIDE, (c + 1) * WIDE)
            out[rows_at(i), units] = dot_nt(dy[rows_at(i), :], down[units, :]).astype(bf16)


def cotangent_units(where, dy, down):
    return call(
        cotangent_units_kernel,
        "cotangent_units",
        where,
        [Near(dy), Near(down)],
        [((SEQ, down.shape[0]), bf16)],
        [],
        1,
        flops=2 * 10**9,
        near=1,
    )[0]


WIDE = 512


def unit_scratch(units, widest):
    return [
        ((2, BLK, units), bf16),
        ((2, BLK, units), bf16),
        ((2, BLK, widest), f32),
        ((2, BLK, widest), f32),
    ]


def unpack_units(ups, downs, up, down):
    for k, (up_piece, down_piece) in enumerate(zip(ups, downs)):
        up[:, rows_at(k)] = up_piece[:D, :]
        for c in range(D // BLK):
            down[rows_at(k), rows_at(c)] = down_piece[rows_at(c), :]


def mlp_own_kernel(
    where, x, p0, p1, gain, bias, dy, da, up, down, more_up, more_down, *refs
):
    h1_out, n2_out, r2_out, u2_out, m_out, du_out = refs[:6]
    near_up, near_down, h1_v, g_v, df_v, f_v, da_v, _ = refs[6:]
    half = SEQ // 2
    mine = pl.ds(pl.multiple_of(where[2] * half, half), half)

    def norm(i):
        for part in range(4):
            at = slice(i * BLK + part * 64, i * BLK + part * 64 + 64)
            h1 = x[at, :].astype(f32) + (p0[at, :].astype(f32) + p1[at, :].astype(f32))
            h1_v[at, :] = h1
            normed, inv = norm_rows(h1)
            n2_out[at, :] = normed.astype(bf16)
            r2_out[at, :] = jnp.broadcast_to(inv, (64, 128))
            u2_out[at, :] = (normed * gain[...] + bias[...]).astype(bf16)
            yield

    def put(i, cols, m, du):
        m_out[rows_at(i), cols] = m.astype(bf16)
        du_out[rows_at(i), cols] = du.astype(bf16)

    unpack_units([more_up], [more_down], near_up, near_down)
    drain(norm(0))
    unit_blocks(
        u2_out,
        dy,
        [
            (up, down, [512] * (up.shape[1] // 512), da),
            (near_up, near_down, [BLK], None),
        ],
        g_v,
        df_v,
        f_v,
        da_v,
        put,
        lambda i: norm(i + 1) if i + 1 < NBLK else iter(()),
    )
    h1_out[...] = h1_v[mine, :]


def mlp_own(where, *args):
    full = ((SEQ, D), bf16)
    units = args[7].shape[1] + BLK
    return call(
        mlp_own_kernel,
        "mlp_own",
        where,
        [Near(a) for a in args],
        [((SEQ // 2, D), f32), full, ((SEQ, 128), f32), full, full, full],
        [((D, BLK), bf16), ((BLK, D), bf16), ((SEQ, D), f32), *unit_scratch(units, 512)],
        1,
        flops=1,
        near=6,
    )


def mlp_peer_kernel(where, u2, dy, m_in, du_in, *refs):
    ups, downs, refs = refs[:3], refs[3:6], refs[6:]
    wo_own_in, wo_peer_in, w_own_in, w_peer_in, ot_in, stat_in, qt_in, v_in, kt_in = refs[:9]
    m_mine, m_other, du_out, wo, w, ot, stat, qt, v, kt = refs[9:19]
    m_v, up, down, g_v, df_v, f_v, da_v, sems = refs[19:]
    moves = Moves(sems)
    for source, target in (
        (wo_own_in, wo.at[0]),
        (wo_peer_in, wo.at[1]),
        (ot_in, ot),
        (stat_in, stat),
        (qt_in, qt),
        (w_own_in, w.at[0]),
        (w_peer_in, w.at[1]),
        (v_in, v),
        (kt_in, kt),
    ):
        moves.store(source, target)

    def put(i, cols, m, du):
        at = rows_at(i)
        m_v[at, cols] = (m_in[at, cols].astype(f32) + m).astype(bf16)
        du_out[at, cols] = (du_in[at, cols].astype(f32) + du).astype(bf16)

    unpack_units(ups, downs, up, down)
    unit_blocks(u2, dy, [(up, down, [BLK] * 3, None)], g_v, df_v, f_v, da_v, put)
    split_halves(where[2], m_v, m_mine, m_other)
    moves.finish()


def split_halves(side, values, mine, other):
    half = SEQ // 2
    mine[...] = values[pl.ds(pl.multiple_of(side * half, half), half), :]
    other[...] = values[pl.ds(pl.multiple_of((1 - side) * half, half), half), :]


def mlp_peer(where, near, kept):
    kept_out = kept[4:]
    full = ((SEQ, D), bf16)
    half = ((SEQ // 2, D), bf16)
    units = 3 * BLK
    return call(
        mlp_peer_kernel,
        "mlp_peer",
        where,
        [Near(a) for a in near] + [*kept],
        [half, half, full, ((2, COLS, D), bf16), ((2, 3, D, COLS), bf16)]
        + [(a.shape, a.dtype) for a in kept_out],
        [full, ((D, units), bf16), ((units, D), bf16), *unit_scratch(units, BLK)],
        9,
        flops=1,
        near=10,
    )


def turn_kernel(where, *refs):
    own, sib, n2, r2, dy, gain, wo, ot, stat, qt = refs[:10]
    kv_own_in, units_near, w2_own_in, w2_peer_in, e_in = refs[10:15]
    dh_out, dot_v, stat_v, dkv_v, e_last = refs[15:20]
    kv, dh_v, low_v, w2, sems = refs[20:]
    side = where[2]
    moves = Moves(sems)
    got_kv = once([moves.load(kv_own_in, kv.at[0])] + peer_prefix(moves, units_near, kv.at[1]))
    got_w2 = once([moves.load(w2_own_in, w2.at[0]), moves.load(w2_peer_in, w2.at[1])])
    moves.store(e_in.at[:, TRI[-1] :], e_last)

    def norm(i):
        for part in range(4):
            at = slice(i * BLK + part * 64, i * BLK + part * 64 + 64)
            du = own[at, :].astype(f32) + sib[at, :].astype(f32)
            dh = dy[at, :].astype(f32) + norm_back(
                du, n2[at, :].astype(f32), r2[at, 0:1], gain[...]
            )
            dh_v[at, :] = dh
            low_v[at, :] = dh.astype(bf16)
            yield

    def grads(i, g):
        at = rows_at(i)
        do = dot_nt(low_v[at, :], wo[g])
        yield
        do_t = do.T
        yield
        for h in range(HEADS):
            scaled = do_t[head_rows(h)] * stat[g, h, PREFIX_ROWS : PREFIX_ROWS + 1, at]
            dot_v[g, head_rows(h), at] = scaled.astype(bf16)
            balance = jnp.sum(
                scaled * ot[g, head_rows(h), at].astype(f32), axis=0, keepdims=True
            )
            stat_v[g, h, PREFIX_ROWS:, at] = jnp.broadcast_to(balance, (8, BLK))
            yield

    def prefix(g, h):
        got_kv()
        pv = kv[g, PREFIX_ROWS:]
        pv = jnp.where(
            lax.broadcasted_iota(jnp.int32, pv.shape, 1) // HD == h, pv, jnp.zeros_like(pv)
        )
        ep = stat[g, h, :PREFIX_ROWS, :]
        dp = dot_nn(pv, dot_v[g])
        dpv = dot_nt(ep.astype(bf16), dot_v[g, head_rows(h), :])
        yield
        grad = ep * (dp - stat_v[g, h, PREFIX_ROWS : PREFIX_ROWS + 1, :])
        stat_v[g, h, :PREFIX_ROWS, :] = grad
        yield
        dpk = dot_nt(grad.astype(bf16), qt[g, head_rows(h), :])
        yield
        low = 2 * g * PREFIX_ROWS
        dkv_v[low : low + PREFIX_ROWS, head_rows(h)] = dpk * (1.0 / LOG2E)
        dkv_v[low + PREFIX_ROWS : low + 2 * PREFIX_ROWS, head_rows(h)] = dpv

    drain(norm(0))
    for i in range(NBLK):
        drain(grads(i, 0), grads(i, 1), *([norm(i + 1)] if i + 1 < NBLK else []))
    drain(*[prefix(g, h) for g in range(2) for h in range(HEADS)])
    got_w2()
    da = 0.0
    for n in range(4):
        grad = dkv_v[n * PREFIX_ROWS : (n + 1) * PREFIX_ROWS, :].astype(bf16)
        da = da + dot_nt(grad, w2[n // 2, :, (n % 2) * COLS : (n % 2 + 1) * COLS])
    dkv_v[4 * PREFIX_ROWS : 5 * PREFIX_ROWS, :] = da[:, :COLS]
    dkv_v[5 * PREFIX_ROWS :, :] = da[:, COLS:]
    half = SEQ // 2
    dh_out[...] = dh_v[pl.ds(pl.multiple_of(side * half, half), half), :]
    moves.finish()


def turn(where, near, small, e):
    return call(
        turn_kernel,
        "turn",
        where,
        [Near(a) for a in near] + [*small, e],
        [
            ((SEQ // 2, D), f32),
            ((2, COLS, SEQ), bf16),
            ((2, HEADS, PREFIX_ROWS + 8, SEQ), f32),
            ((6 * PREFIX_ROWS, COLS), f32),
            ((2, SEQ, LANES), bf16),
        ],
        [
            ((2, 2 * PREFIX_ROWS, COLS), bf16),
            ((SEQ, D), f32),
            ((SEQ, D), bf16),
            ((2, 2 * COLS, 2 * COLS), bf16),
        ],
        5,
        flops=6 * 10**9,
        near=5,
    )


def attend_back_kernel(where, *refs):
    do_t, qt, v, kt, e_last, stat, w, e_in, kv_own_in, units_near, x_in = refs[:11]
    mine_out, other_out, x_v, e, kv, dkt, dvt, du_v, ds_v, sems = refs[11:]
    slot, side = where[0], where[2]
    half = SEQ // 2
    moves = Moves(sems)
    kv_loads = [moves.load(kv_own_in, kv.at[0])] + peer_prefix(moves, units_near, kv.at[1])
    moves.store(x_in.at[pl.ds(pl.multiple_of(slot * SEQ + side * half, half), half)], x_v)

    def run(local):
        spans = [(i, 1) if local else (0, i + 1) for i in range(NBLK)]
        last = NBLK - 1
        parts = Moves(sems)
        parts.used = moves.used
        e_got = {}
        for i in reversed(range(last)):
            at = slice(TRI[i], TRI[i] + spans[i][1] * BLK)
            for g in range(2):
                e_got[i, g, 0] = once([parts.load(e_in.at[g, at], e.at[g, at])])

        def weights(i, g, h, c):
            if i == last:
                return e_last[g, rows_at(c), head_lanes(h)]
            return e[g, TRI[i] + c * BLK : TRI[i] + (c + 1) * BLK, head_lanes(h)]

        once(kv_loads)()
        dqs = {}

        def slopes(n, i, g, h, first, count):
            here = rows_at(i)
            do_h = do_t[g, :, here]
            do_h = jnp.where(
                lax.broadcasted_iota(jnp.int32, do_h.shape, 0) // HD == h, do_h, jnp.zeros_like(do_h)
            )
            balance = stat[g, h, PREFIX_ROWS : PREFIX_ROWS + 1, here]
            if (i, g, h) in e_got:
                e_got[i, g, h]()
            for c in range(count):
                dp = dot_nn(v[g, rows_at(first + c), :], do_h)
                e_low = weights(i, g, h, c)
                ds_v[n % 2, rows_at(c), :] = (e_low.astype(f32) * (dp - balance)).astype(bf16)
                yield

        def use(n, i, g, h, first, count):
            heads, here = head_rows(h), rows_at(i)
            pk_t = kv[g, :PREFIX_ROWS].astype(f32).T.astype(bf16)
            dq = dot_nn(pk_t[heads], stat[g, h, :PREFIX_ROWS, here].astype(bf16))
            for c in range(count):
                at = rows_at(first + c)
                e_low = weights(i, g, h, c)
                ds = ds_v[n % 2, rows_at(c), :]
                dv = dot_nt(do_t[g, heads, here], e_low)
                dk = dot_nt(qt[g, heads, here], ds)
                if local or i == last:
                    dvt[g, heads, at] = dv
                    dkt[g, heads, at] = dk
                else:
                    dvt[g, heads, at] += dv
                    dkt[g, heads, at] += dk
                dq = dq + dot_nn(kt[g, heads, at], ds)
                yield
            dqs[i, g, h] = dq

        def share(i):
            here = rows_at(i)
            grads = []
            for g in range(2):
                dq = jnp.concatenate([dqs.pop((i, g, h)) for h in range(HEADS)], axis=0)
                for value, scale in ((dq, SCALE), (dkt[g, :, here], 1.0 / LOG2E), (dvt[g, :, here], 1.0)):
                    grads.append((value.T * scale).astype(bf16))
                    yield
            for c in range(D // BLK):
                total = None
                for g in range(2):
                    for part in range(3):
                        term = dot_nt(grads[3 * g + part], w[g, part, rows_at(c), :])
                        total = term if total is None else total + term
                du_v[here, rows_at(c)] = total.astype(bf16)
                yield

        units = []
        for i in reversed(range(NBLK)):
            for g in range(2):
                for h in range(HEADS):
                    units.append((len(units), i, g, h, *spans[i]))
        tail = iter(())
        drain(slopes(*units[0]))
        for n, unit in enumerate(units):
            i, g, h = unit[1:4]
            ahead = [slopes(*units[n + 1])] if n + 1 < len(units) else []
            for _ in weave(*ahead, use(*unit)):
                next(tail, None)
            if g == 1 and h == HEADS - 1:
                drain(tail)
                tail = share(i)
        drain(tail)

    bucket = where[3]

    @pl.when(bucket == 0)
    def _():
        run(True)

    @pl.when(bucket != 0)
    def _():
        run(False)

    split_halves(side, du_v, mine_out, other_out)
    moves.finish()


def attend_back(where, near, e, kv_own, units_near, x):
    half = ((SEQ // 2, D), bf16)
    return call(
        attend_back_kernel,
        "attend_back",
        where,
        [Near(a) for a in near] + [e, kv_own, units_near, x],
        [half, half, half],
        [
            ((2, TRI[-1], LANES), bf16),
            ((2, 2 * PREFIX_ROWS, COLS), bf16),
            ((2, COLS, SEQ), f32),
            ((2, COLS, SEQ), f32),
            ((SEQ, D), bf16),
            ((2, SEQ, BLK), bf16),
        ],
        16,
        flops=16 * 10**9,
        near=3,
    )


def finish_kernel(where, own, sib, x, dh, gain, out, out_v, sems):
    moves = Moves(sems)
    size = 64
    for n in range(SEQ // 2 // size):
        at = slice(n * size, (n + 1) * size)
        normed, inv = norm_rows(x[at, :].astype(f32))
        du = own[at, :].astype(f32) + sib[at, :].astype(f32)
        out_v[at, :] = dh[at, :] + norm_back(du, normed, inv, gain[...])
        moves.store(out_v.at[at], out.at[at])
    moves.finish()


def finish(where, *args):
    wide = ((SEQ // 2, D), f32)
    return call(finish_kernel, "finish", where, [Near(a) for a in args], [wide], [wide], 8)[0]


def result_kernel(where, h1, own, sib, after, out, out_v, sems):
    moves = Moves(sems)
    size = 64
    for n in range(SEQ // 2 // size):
        at = slice(n * size, (n + 1) * size)
        out_v[at, :] = (h1[at, :] + (own[at, :].astype(f32) + sib[at, :].astype(f32))).astype(bf16)
        moves.store(out_v.at[at], out.at[at])
    moves.finish()


def result(where, h1, own, sib, after):
    half = ((SEQ // 2, D), bf16)
    return call(
        result_kernel, "result", where, [Near(h1), Near(own), Near(sib), Loose(after)], [half], [half], 8
    )[0]


def swap(values, axis, bit):
    size = lax.axis_size(axis)
    return lax.ppermute(values, axis, [(n, n ^ bit) for n in range(size)])


def after(values, *others):
    return lax.optimization_barrier((values, *others))[0]


def other_half(values, side):
    half = values.shape[0] // 2
    return lax.dynamic_slice_in_dim(values, (1 - side) * half, half, 0)


def on_device(
    inputs,
    buckets,
    ln1_gain,
    ln1_bias,
    w_qkv,
    w_out,
    ln2_gain,
    ln2_bias,
    w_up,
    w_down,
    prefix_embed,
    prefix_w1,
    prefix_b1,
    prefix_w2,
    prefix_b2,
    cotangent,
):
    prefix_count = prefix_embed.shape[0]
    width = prefix_w1.shape[1]
    member = lax.axis_index("tensor")
    place = lax.axis_index("batch") & 3
    side = member & 1
    slot = member // 2
    where = jnp.stack([slot, place, side, buckets[slot]]).astype(jnp.int32)
    w = w_qkv.transpose(1, 0, 2)
    w2_flat = prefix_w2.reshape(width, 2 * COLS)
    gain1, bias1 = ln1_gain.reshape(1, D), ln1_bias.reshape(1, D)
    gain2, bias2 = ln2_gain.reshape(1, D), ln2_bias.reshape(1, D)
    embed = jnp.pad(prefix_embed, ((0, PREFIX_ROWS - prefix_count), (0, 0)))

    def across(values):
        return swap(values, "tensor", 2)

    first_near = across(pack(w, w_out))
    hidden, kv_own, up_near, down_near, up_far, down_far = prefix_forward(
        embed,
        prefix_w1,
        prefix_b1.reshape(1, width),
        w2_flat,
        prefix_b2.reshape(1, 2 * COLS),
        w_up,
        w_down,
    )
    up_near = across(up_near)
    down_near = across(after(down_near, where))
    first_beside = swap(first_near, "batch", 1)
    first_above = swap(first_near, "batch", 2)
    *saved, x, u1, part, dy, down = attend(
        where,
        0,
        (after(inputs, first_near), gain1, bias1, w, w_out, kv_own, cotangent, w_down),
    )
    half = first_near.shape[0] // 2
    first_top = swap(after(first_above, u1)[:half], "batch", 1)
    first_bottom = swap(after(first_beside, u1)[half:], "batch", 2)
    first = (first_near, first_beside, first_above, first_top, first_bottom)
    up_sent = after(up_near, u1)
    up_far = across(after(up_far, u1))
    up_beside = swap(up_sent, "batch", 1)
    up_above = swap(up_sent, "batch", 2)
    da = cotangent_units(where, after(dy, first_beside, first_above), down)
    *saved, w_peer, wo_peer, part, up = attend(
        where,
        1,
        (*[Near(a) for a in (u1, *first, up_near, after(part, da, down_near))], w_up),
        saved,
    )
    part_sib = swap(after(part, up_beside, up_above, up_far), "tensor", 1)
    down_sent = after(down_near, part)
    down_beside = swap(down_sent, "batch", 1)
    down_above = swap(down_sent, "batch", 2)
    down_far = across(after(down_far, part))
    qt, kt, v, ot, e, stat = saved
    h1, n2, r2, u2, m, du = mlp_own(
        where, x, part, part_sib, gain2, bias2, dy, da, up, down, up_near, down_near
    )
    w2_peer = across(after(w2_flat, part))
    m_mine, m_other, du, wo_pair, w_pair, ot, stat, qt, v, kt = mlp_peer(
        where,
        (u2, dy, m, du, up_beside, up_above, up_far, down_beside, down_above, down_far),
        (w_out, wo_peer, w, w_peer, ot, stat, qt, v, kt),
    )
    du_sib = swap(after(du, w2_peer), "tensor", 1)
    m_sib = swap(m_other, "tensor", 1)
    dh, do_t, stat, dkv, e_last = turn(
        where,
        (du, du_sib, n2, r2, dy, gain2, wo_pair, ot, stat, qt),
        (kv_own, Loose(up_near), w2_flat, Loose(w2_peer)),
        e,
    )

    dkv_peer = across(dkv)
    output = result(where, h1, m_mine, m_sib, dkv)
    dkv_peer = after(dkv_peer, output)
    rows = 2 * PREFIX_ROWS
    sums = jnp.concatenate(
        [dkv[:rows] + dkv_peer[rows : 2 * rows], dkv[2 * rows :] + dkv_peer[2 * rows :]], axis=0
    )
    bits = [1 << n for n in reversed(range(lax.axis_size("batch").bit_length() - 1))]
    sums_away = swap(sums, "batch", bits[0])
    du1_mine, du1_other, x = attend_back(
        where,
        (after(do_t, sums), qt, v, kt, e_last, stat, w_pair),
        e,
        kv_own,
        Loose(up_near),
        inputs,
    )
    du1_sib = swap(after(du1_other, sums_away), "tensor", 1)
    sums = sums + after(sums_away, du1_mine)
    for bit in bits[1:-2]:
        sums = sums + swap(sums, "batch", bit)
    away = [swap(sums, "batch", pair) for pair in (1, 2, 3)]
    input_grad = finish(where, du1_mine, after(du1_sib, sums), x, dh, gain1)
    away = lax.optimization_barrier((*away, input_grad))
    sums = (sums + away[0]) + (away[1] + away[2])
    da = sums[rows:] + swap(sums[rows:], "tensor", 1)
    w2_grad, b2_grad, embed_grad, w1_grad, b1_grad = prefix_back(
        sums[:rows], da, hidden, embed, prefix_w1
    )
    return (
        output,
        input_grad,
        embed_grad[:prefix_count],
        w1_grad,
        b1_grad.reshape(width),
        w2_grad,
        b2_grad,
    )


def solution(mesh):
    placed = (
        P("batch", None),
        P("batch"),
        P(),
        P(),
        P(None, None, "tensor"),
        P("tensor", None),
        P(),
        P(),
        P(None, "tensor"),
        P("tensor", None),
        P(),
        P(),
        P(),
        P(None, None, "tensor"),
        P(None, "tensor"),
        P("batch", None),
    )
    return jax.shard_map(
        on_device,
        mesh=mesh,
        in_specs=placed,
        out_specs=(
            P(("batch", "tensor"), None),
            P(("batch", "tensor"), None),
            P(),
            P(),
            P(),
            P(None, None, "tensor"),
            P(None, "tensor"),
        ),
        check_vma=False,
    )
```

```python
import functools
import math

import jax
import jax.numpy as jnp
from jax import lax
from jax.experimental import pallas as pl
from jax.experimental.pallas import tpu as pltpu
from jax.sharding import PartitionSpec as P

D = 1024
HD = 64
SEQ = 1024
HEADS = 4
COLS = HEADS * HD
BLK = 256
NBLK = SEQ // BLK
HALF = NBLK // 2
LANES = HEADS * BLK
PREFIX_ROWS = 16
EXT = HD + 16
TRI = [BLK * i * (i + 1) // 2 for i in range(NBLK)]
E_ROWS = BLK * NBLK * (NBLK + 1) // 2
LOG2E = 1.4426950408889634
SCALE = 0.125
FAR = -1e30
MASKED = -1e9 * LOG2E
MIB = 1 << 20

f32 = jnp.float32
bf16 = jnp.bfloat16
precise = lax.Precision.HIGHEST


def dot_nn(a, b):
    return lax.dot_general(a, b, (((1,), (0,)), ((), ())), preferred_element_type=f32)


def dot_nt(a, b):
    return lax.dot_general(a, b, (((1,), (1,)), ((), ())), preferred_element_type=f32)


def exact(a, b, dims):
    return lax.dot_general(a, b, (dims, ((), ())), precision=precise, preferred_element_type=f32)


def norm_rows(values):
    average = jnp.mean(values, axis=-1, keepdims=True)
    centred = values - average
    inv = lax.rsqrt(jnp.mean(centred * centred, axis=-1, keepdims=True) + 1e-05)
    return centred * inv, inv


def norm_back(incoming, normed, inv, gain):
    scaled = incoming * gain
    return inv * (
        scaled
        - jnp.mean(scaled, axis=-1, keepdims=True)
        - normed * jnp.mean(scaled * normed, axis=-1, keepdims=True)
    )


def head_lanes(h):
    return slice(h * BLK, (h + 1) * BLK)


def head_rows(h):
    return slice(h * HD, (h + 1) * HD)


def head_blocks(cols):
    row_head = lax.broadcasted_iota(jnp.int32, cols.shape, 0) // HD
    return jnp.concatenate(
        [jnp.where(row_head == h, cols, jnp.zeros_like(cols)) for h in range(HEADS)], axis=1
    )


class Loose:
    def __init__(self, array):
        self.array = array


class Near:
    def __init__(self, array):
        self.array = array


def placed(a):
    if isinstance(a, Loose):
        return a.array
    if isinstance(a, Near):
        return pltpu.with_memory_space_constraint(a.array, pltpu.VMEM)
    return pltpu.with_memory_space_constraint(a, pltpu.HBM)


def hbm(*arrays):
    return [placed(a) for a in arrays]


def plain(arrays):
    return [a.array if isinstance(a, (Loose, Near)) else a for a in arrays]


def rows_at(i, count=1):
    return slice(i * BLK, (i + count) * BLK)


class Moves:
    def __init__(self, sems):
        self.sems = sems
        self.used = 0
        self.out = []
        self.halves = []

    def load(self, source, target):
        copy = pltpu.make_async_copy(source, target, self.sems.at[self.used])
        self.used += 1
        copy.start()
        return copy

    def store(self, source, target):
        self.out.append(self.load(source, target))

    def store_half(self, source, same, at, mine, other):
        sem = self.sems.at[self.used]
        self.used += 1
        here = pltpu.make_async_copy(source, mine.at[at], sem)
        there = pltpu.make_async_copy(source, other.at[at], sem)
        pl.when(same)(here.start)
        pl.when(jnp.logical_not(same))(there.start)
        self.halves.append((same, here, there))

    def finish(self):
        for copy in self.out:
            copy.wait()
        for same, here, there in self.halves:
            pl.when(same)(here.wait)
            pl.when(jnp.logical_not(same))(there.wait)


def once(copies):
    left = list(copies)

    def wait():
        while left:
            left.pop().wait()

    return wait


def weave(*tasks):
    live = list(tasks)
    while live:
        for task in list(live):
            if next(task, live) is live:
                live.remove(task)
        yield


def drain(*tasks):
    for _ in weave(*tasks):
        pass


ANY = pl.BlockSpec(memory_space=pl.ANY)
SMALL = pl.BlockSpec(memory_space=pltpu.SMEM)


def room(scratch):
    return sum(math.prod(shape) * jnp.dtype(kind).itemsize for shape, kind in scratch)


FULL = pl.BlockSpec(memory_space=pltpu.VMEM)


def call(kernel, name, where, args, outs, scratch, sems, aliases=None, flops=0, near=0):
    far = len(outs) - near
    return pl.pallas_call(
        kernel,
        in_specs=[SMALL] + [FULL if isinstance(a, Near) else ANY for a in args],
        out_specs=[ANY] * far + [FULL] * near,
        out_shape=[pltpu.HBM(shape, kind) for shape, kind in outs[:far]]
        + [pltpu.VMEM(shape, kind) for shape, kind in outs[far:]],
        scratch_shapes=[pltpu.VMEM(shape, kind) for shape, kind in scratch]
        + [pltpu.SemaphoreType.DMA((sems,))],
        input_output_aliases=aliases or {},
        compiler_params=pltpu.CompilerParams(
            vmem_limit_bytes=room(scratch) // MIB * MIB + 8 * MIB
        ),
        cost_estimate=pl.CostEstimate(
            flops=flops,
            transcendentals=0,
            bytes_accessed=sum(a.size * a.dtype.itemsize for a in plain(args)),
        ),
        name=name,
    )(where, *hbm(*args))


def unpack_first(place, pieces, w, wo):
    rows, thin = D // 4, COLS // 4
    near, beside, above, top, bottom = pieces
    for k in range(4):

        def rows_of(first, count):
            if k < 3:
                return (near, beside, above)[k][first : first + count, :]
            half = 2 * BLK
            return (top if first < half else bottom)[first % half : first % half + count, :]

        at = pl.ds(pl.multiple_of((place ^ k) * rows, rows), rows)
        for part in range(3):
            w[part, at, :] = rows_of(part * BLK, BLK)
        at = pl.ds(pl.multiple_of((place ^ k) * thin, thin), thin)
        for c in range(D // COLS):
            wo[at, rows_at(c)] = rows_of(3 * BLK + c * thin, thin)


def pack_pieces(moves, place, w, wo, out):
    rows, thin = D // 4, COLS // 4
    at = pl.ds(pl.multiple_of(place * rows, rows), rows)
    for part in range(3):
        moves.store(w.at[part, at], out.at[rows_at(part)])
    at = pl.ds(pl.multiple_of(place * thin, thin), thin)
    for c in range(D // COLS):
        moves.store(
            wo.at[at, c * COLS : (c + 1) * COLS],
            out.at[3 * BLK + c * thin : 3 * BLK + (c + 1) * thin],
        )


def pack_kernel(w, wo, out, sems):
    moves = Moves(sems)
    pack_pieces(moves, lax.axis_index("batch") & 3, w, wo, out)
    moves.finish()


def pack(w, wo):
    return pl.pallas_call(
        pack_kernel,
        in_specs=[ANY, ANY],
        out_specs=pl.BlockSpec(memory_space=pltpu.VMEM),
        out_shape=jax.ShapeDtypeStruct((4 * BLK, COLS), bf16),
        scratch_shapes=[pltpu.SemaphoreType.DMA((7,))],
        name="pack",
    )(*hbm(w, wo))


def prefix_kernel(embed, w1, b1, w2, b2, up, down, *refs):
    hidden_out, kv_out, up_near, down_near, up_far, down_far, sems = refs
    place = lax.axis_index("batch") & 3
    moves = Moves(sems)
    for bits, up_out, down_out in ((0, up_near, down_near), (3, up_far, down_far)):
        units = pl.ds(pl.multiple_of((place ^ bits) * BLK, BLK), BLK)
        moves.store(up.at[:, units], up_out.at[:D])
        for c in range(D // BLK):
            moves.store(down.at[units, rows_at(c)], down_out.at[rows_at(c)])
    hidden = jnp.tanh(dot_nn(embed[...], w1[...]) + b1[...])
    kv = exact(hidden, w2[...].astype(f32), ((1,), (0,))) + b2[...]
    real = lax.broadcasted_iota(jnp.int32, kv.shape, 0) < 10
    kv = jnp.where(real, kv, 0.0)
    hidden_out[...] = hidden
    kv = jnp.concatenate([kv[:, :COLS], kv[:, COLS:]], axis=0).astype(bf16)
    kv_out[...] = kv
    up_near[D:, :] = kv
    moves.finish()


def prefix_forward(embed, w1, b1, w2, b2, up, down):
    width = w1.shape[1]
    full = pl.BlockSpec(memory_space=pltpu.VMEM)
    return pl.pallas_call(
        prefix_kernel,
        in_specs=[full] * 5 + [ANY] * 2,
        out_specs=[full] * 6,
        out_shape=(
            pltpu.HBM((PREFIX_ROWS, width), f32),
            pltpu.HBM((2 * PREFIX_ROWS, COLS), bf16),
            jax.ShapeDtypeStruct((D + 2 * PREFIX_ROWS, BLK), bf16),
            jax.ShapeDtypeStruct((D, BLK), bf16),
            jax.ShapeDtypeStruct((D, BLK), bf16),
            jax.ShapeDtypeStruct((D, BLK), bf16),
        ),
        scratch_shapes=[pltpu.SemaphoreType.DMA((10,))],
        compiler_params=pltpu.CompilerParams(vmem_limit_bytes=24 * MIB),
        name="prefix_forward",
    )(*hbm(embed, w1, b1, w2, b2, up, down))


def peer_prefix(moves, units_near, kv):
    return [moves.load(units_near.at[D:], kv)]


def prefix_back_kernel(dkv, da, hidden, embed, w1, w2_out, b2_out, embed_out, w1_out, b1_out):
    wide = hidden[...]
    low = wide.astype(bf16)
    over_rows = (((0,), (0,)), ((), ()))
    for part in range(2):
        grad = dkv[part * PREFIX_ROWS : (part + 1) * PREFIX_ROWS, :]
        w2_out[:, part, :] = lax.dot_general(
            low, grad.astype(bf16), over_rows, preferred_element_type=f32
        )
        b2_out[part : part + 1, :] = jnp.sum(grad, axis=0, keepdims=True)
    pre = jnp.concatenate([da[:PREFIX_ROWS], da[PREFIX_ROWS:]], axis=1) * (1.0 - wide * wide)
    b1_out[...] = jnp.sum(pre, axis=0, keepdims=True)
    pre_low = pre.astype(bf16)
    w1_out[...] = lax.dot_general(embed[...], pre_low, over_rows, preferred_element_type=f32)
    embed_out[...] = dot_nt(pre_low, w1[...])


def prefix_back(dkv, da, hidden, embed, w1):
    width = w1.shape[1]
    return pl.pallas_call(
        prefix_back_kernel,
        out_shape=(
            pltpu.HBM((width, 2, COLS), f32),
            pltpu.HBM((2, COLS), f32),
            pltpu.HBM((PREFIX_ROWS, D), f32),
            pltpu.HBM((D, width), f32),
            pltpu.HBM((1, width), f32),
        ),
        compiler_params=pltpu.CompilerParams(vmem_limit_bytes=24 * MIB),
        name="prefix_back",
    )(dkv, da, *hbm(Near(hidden), Near(embed), Near(w1)))


def attend_kernel(peer, where, *refs):
    slot, place, bucket = where[0], where[1], where[3]
    if peer:
        u1_v, *pieces = refs[:6]
        units_near, part_v, up_in = refs[6:9]
        refs = refs[9:]
    else:
        x_in, gain_in, bias_in, w_in, wo_in, kv_in, dy_in, down_in = refs[:8]
        refs = refs[8:]
    e_out = refs[0]
    if peer:
        w_out, wo_out, qt_v, kt_v, v_v, ot_v, stat_v, mix_v, up_v = refs[1:10]
        w, wo, kv, k_v, vt_v, e_v, s_v, sems = refs[10:]
    else:
        qt_v, kt_v, v_v, ot_v, stat_v, rows_v, u1_v, mix_v, dy_v, down_v = refs[1:11]
        gain, bias, w, wo, kv, k_v, vt_v, e_v, s_v, sems = refs[11:]
    group = 1 if peer else 0
    moves = Moves(sems)
    if peer:
        unpack_first(place, pieces, w, wo)
        kv[...] = units_near[D:, :]
        got_w = got_wo = got_kv = once([])
        moves.store(up_in, up_v)
    else:
        got_norm = once([moves.load(gain_in, gain), moves.load(bias_in, bias)])
        first = pl.multiple_of(slot * SEQ, SEQ)
        rows = [moves.load(x_in.at[pl.ds(first, BLK)], rows_v.at[rows_at(0)])]
        got_w = once([moves.load(w_in, w)])
        got_kv = once([moves.load(kv_in, kv)])
        rows += [
            moves.load(x_in.at[pl.ds(first + i * BLK, BLK)], rows_v.at[rows_at(i)])
            for i in range(1, NBLK)
        ]
        got_wo = once([moves.load(wo_in, wo)])
        moves.store(dy_in.at[pl.ds(first, SEQ)], dy_v)
        moves.store(down_in, down_v)
    filler = jnp.where(
        lax.broadcasted_iota(jnp.int32, (EXT - HD, SEQ), 0) == 0, 1.0, 0.0
    ).astype(bf16)
    for h in range(HEADS):
        vt_v[h * EXT + HD : (h + 1) * EXT, :] = filler

    def project(i):
        if not peer:
            rows[i].wait()
            got_norm()
            for part in range(4):
                at = slice(i * BLK + part * 64, i * BLK + part * 64 + 64)
                normed, _ = norm_rows(rows_v[at, :].astype(f32))
                u1_v[at, :] = (normed * gain[...] + bias[...]).astype(bf16)
                yield
        u1 = u1_v[rows_at(i), :]
        got_w()
        if peer and i == 0:
            moves.store(w, w_out)
        keys = dot_nn(u1, w[1])
        yield
        qs = dot_nn(u1, w[0])
        k_v[rows_at(i), :] = keys.astype(bf16)
        kt_v[:, rows_at(i)] = keys.T.astype(bf16)
        yield
        values = dot_nn(u1, w[2])
        qt_v[:, rows_at(i)] = (qs * (SCALE * LOG2E)).T.astype(bf16)
        yield
        v_v[rows_at(i), :] = values.astype(bf16)
        values_t = values.T.astype(bf16)
        for h in range(HEADS):
            vt_v[h * EXT : h * EXT + HD, rows_at(i)] = values_t[head_rows(h)]
        yield

    tops = {}
    done = {}

    def scores(n, i, h, first, count):
        got_kv()
        qt = qt_v[:, rows_at(i)]
        q_h = jnp.where(
            lax.broadcasted_iota(jnp.int32, qt.shape, 0) // HD == h, qt, jnp.zeros_like(qt)
        )
        real = lax.broadcasted_iota(jnp.int32, (PREFIX_ROWS, BLK), 0) < 10
        prefix = jnp.where(real, dot_nn(kv[:PREFIX_ROWS], q_h), FAR)
        top = jnp.max(prefix, axis=0, keepdims=True)
        for c in range(count):
            block = dot_nn(k_v[rows_at(first + c), :], q_h)
            if c == count - 1:
                keep = lax.broadcasted_iota(jnp.int32, (BLK, BLK), 0) <= lax.broadcasted_iota(
                    jnp.int32, (BLK, BLK), 1
                )
                block = jnp.where(keep, block, MASKED)
            s_v[n % 2, rows_at(c), :] = block
            top = jnp.maximum(top, jnp.max(block, axis=0, keepdims=True))
            yield
        tops[n] = prefix, top

    def mix(n, i, h, first, count):
        prefix, top = tops.pop(n)
        ep = jnp.exp2(prefix - top)
        stat_v[h, :PREFIX_ROWS, rows_at(i)] = ep
        one = jnp.where(
            lax.broadcasted_iota(jnp.int32, (EXT - HD, PREFIX_ROWS), 0) == 0, 1.0, 0.0
        )
        pv_t = kv[PREFIX_ROWS:].astype(f32).T
        pv_ext = jnp.concatenate([pv_t[head_rows(h)], one], axis=0).astype(bf16)
        mixed = dot_nn(pv_ext, ep.astype(bf16))
        for c in range(count):
            e_low = jnp.exp2(s_v[n % 2, rows_at(c), :] - top).astype(bf16)
            e_v[TRI[i] + c * BLK : TRI[i] + (c + 1) * BLK, head_lanes(h)] = e_low
            mixed = mixed + dot_nn(vt_v[h * EXT : (h + 1) * EXT, rows_at(first + c)], e_low)
            yield
        e_at = slice(TRI[i], TRI[i] + count * BLK)
        moves.store(e_v.at[e_at, head_lanes(h)], e_out.at[e_at, head_lanes(h)])
        inv = 1.0 / mixed[HD : HD + 1]
        stat_v[h, PREFIX_ROWS:, rows_at(i)] = jnp.broadcast_to(inv, (8, BLK))
        done[n] = mixed[:HD] * inv

    def write(i, count):
        ot = jnp.concatenate([done.pop(i * HEADS + h) for h in range(HEADS)], axis=0)
        ot_v[:, rows_at(i)] = ot.astype(bf16)
        o = ot.T.astype(bf16)
        yield
        got_wo()
        if peer:
            if i == 0:
                moves.store(wo, wo_out)
        for c in range(D // BLK):
            part = dot_nn(o, wo[:, rows_at(c)])
            if peer:
                part = part + part_v[rows_at(i), rows_at(c)].astype(f32)
            mix_v[rows_at(i), rows_at(c)] = part.astype(bf16)
            yield

    def run(local):
        units = []
        for i in range(NBLK):
            for h in range(HEADS):
                units.append((len(units), i, h, *((i, 1) if local else (0, i + 1))))
        drain(project(0))
        side = None
        drain(scores(*units[0]))
        for n, unit in enumerate(units):
            i, h = unit[1:3]
            if h == 0:
                side = iter(())
                steps = []
                if i > 0:
                    steps.append(write(i - 1, units[n - 1][4]))
                if i + 1 < NBLK:
                    steps.append(project(i + 1))
                side = weave(*steps)
                if i + 2 == NBLK:
                    pass
            ahead = []
            if n + 1 < len(units):
                if h == HEADS - 1:
                    drain(side)
                ahead = [scores(*units[n + 1])]
            for _ in weave(*ahead, mix(*unit)):
                next(side, None)
                next(side, None)
        drain(side)
        drain(write(NBLK - 1, units[-1][4]))
        moves.finish()

    return run


def attend_main(peer, where, *refs):
    bucket = where[3]

    @pl.when(bucket == 0)
    def _():
        attend_kernel(peer, where, *refs)(True)

    @pl.when(bucket != 0)
    def _():
        attend_kernel(peer, where, *refs)(False)


def attend(where, group, args):
    peer = group == 1
    full = ((SEQ, D), bf16)
    kept = [
        ((COLS, SEQ), bf16),
        ((COLS, SEQ), bf16),
        ((SEQ, COLS), bf16),
        ((COLS, SEQ), bf16),
        ((HEADS, PREFIX_ROWS + 8, SEQ), f32),
    ]
    outs = [((E_ROWS, LANES), bf16)]
    if peer:
        outs += [((3, D, COLS), bf16), ((COLS, D), bf16), *kept, full, (args[-1].shape, bf16)]
        scratch = []
    else:
        outs += [*kept, full, full, full, full, (args[-1].shape, bf16)]
        scratch = [((1, D), f32), ((1, D), f32)]
    scratch += [
        ((3, D, COLS), bf16),
        ((COLS, D), bf16),
        ((2 * PREFIX_ROWS, COLS), bf16),
        ((SEQ, COLS), bf16),
        ((HEADS * EXT, SEQ), bf16),
        ((E_ROWS, LANES), bf16),
        ((2, SEQ, BLK), f32),
    ]
    return call(
        functools.partial(attend_main, peer),
        "attend_peer" if peer else "attend_own",
        where,
        args,
        outs,
        scratch,
        40,
        flops=10 * 10**9,
        near=7 if peer else 10,
    )


def unit_blocks(u2, dy, shards, g_v, df_v, f_v, da_v, put, side=None):
    k = 0.7978845608028654
    chunks, spans, start = [], [], 0
    for up, down, widths, known in shards:
        inner = 0
        for size in widths:
            chunks.append(
                (up, down, slice(inner, inner + size), slice(start + inner, start + inner + size), known)
            )
            inner += size
        spans.append((up, down, slice(start, start + inner)))
        start += inner
    last = NBLK * len(chunks)

    def products(n):
        i, c = divmod(n, len(chunks))
        up, down, units, _, known = chunks[c]
        at, size = rows_at(i), units.stop - units.start
        f_v[n % 2, :, :size] = dot_nn(u2[at, :], up[:, units])
        yield
        if known is None:
            da_v[n % 2, :, :size] = dot_nt(dy[at, :], down[units, :])
            yield

    def bend(n):
        i, c = divmod(n, len(chunks))
        _, _, inner, units, known = chunks[c]
        size = units.stop - units.start
        for part in range(4):
            at = slice(part * 64, (part + 1) * 64)
            f = f_v[n % 2, at, :size]
            if known is None:
                da = da_v[n % 2, at, :size]
            else:
                da = known[i * BLK + part * 64 : i * BLK + part * 64 + 64, inner].astype(f32)
            square = f * f
            t = jnp.tanh(f * (k + (k * 0.044715) * square))
            half = 0.5 * t + 0.5
            g = f * half
            slope = half + g * (1.0 - half) * (2 * k + (6 * k * 0.044715) * square)
            g_v[i % 2, at, units] = g.astype(bf16)
            df_v[i % 2, at, units] = (da * slope).astype(bf16)
            yield

    def close(i):
        for part in range(D // WIDE):
            cols = slice(part * WIDE, (part + 1) * WIDE)
            m = sum(dot_nn(g_v[i % 2, :, span], down[:, cols]) for _, down, span in spans)
            yield
            du = sum(dot_nt(df_v[i % 2, :, span], up[cols, :]) for up, _, span in spans)
            put(i, cols, m, du)
            yield

    side = side or (lambda i: iter(()))
    drain(products(0))
    for n in range(last):
        i, c = divmod(n, len(chunks))
        if c == 0:
            extra = side(i)
        if c == len(chunks) - 1:
            drain(extra)
        for _ in weave(*([products(n + 1)] if n + 1 < last else []), bend(n)):
            next(extra, None)
        if c == len(chunks) - 1:
            drain(close(i))


def cotangent_units_kernel(where, dy, down, out, sems):
    for i in range(NBLK):
        for c in range(down.shape[0] // WIDE):
            units = slice(c * WIDE, (c + 1) * WIDE)
            out[rows_at(i), units] = dot_nt(dy[rows_at(i), :], down[units, :]).astype(bf16)


def cotangent_units(where, dy, down):
    return call(
        cotangent_units_kernel,
        "cotangent_units",
        where,
        [Near(dy), Near(down)],
        [((SEQ, down.shape[0]), bf16)],
        [],
        1,
        flops=2 * 10**9,
        near=1,
    )[0]


WIDE = 512


def unit_scratch(units, widest):
    return [
        ((2, BLK, units), bf16),
        ((2, BLK, units), bf16),
        ((2, BLK, widest), f32),
        ((2, BLK, widest), f32),
    ]


def unpack_units(ups, downs, up, down):
    for k, (up_piece, down_piece) in enumerate(zip(ups, downs)):
        up[:, rows_at(k)] = up_piece[:D, :]
        for c in range(D // BLK):
            down[rows_at(k), rows_at(c)] = down_piece[rows_at(c), :]


def mlp_own_kernel(
    where, x, p0, p1, gain, bias, dy, da, up, down, more_up, more_down, *refs
):
    h1_out, n2_out, r2_out, u2_out, m_out, du_out = refs[:6]
    near_up, near_down, h1_v, g_v, df_v, f_v, da_v, _ = refs[6:]
    half = SEQ // 2
    mine = pl.ds(pl.multiple_of(where[2] * half, half), half)

    def norm(i):
        for part in range(4):
            at = slice(i * BLK + part * 64, i * BLK + part * 64 + 64)
            h1 = x[at, :].astype(f32) + (p0[at, :].astype(f32) + p1[at, :].astype(f32))
            h1_v[at, :] = h1
            normed, inv = norm_rows(h1)
            n2_out[at, :] = normed.astype(bf16)
            r2_out[at, :] = jnp.broadcast_to(inv, (64, 128))
            u2_out[at, :] = (normed * gain[...] + bias[...]).astype(bf16)
            yield

    def put(i, cols, m, du):
        m_out[rows_at(i), cols] = m.astype(bf16)
        du_out[rows_at(i), cols] = du.astype(bf16)

    unpack_units([more_up], [more_down], near_up, near_down)
    drain(norm(0))
    unit_blocks(
        u2_out,
        dy,
        [
            (up, down, [512] * (up.shape[1] // 512), da),
            (near_up, near_down, [BLK], None),
        ],
        g_v,
        df_v,
        f_v,
        da_v,
        put,
        lambda i: norm(i + 1) if i + 1 < NBLK else iter(()),
    )
    h1_out[...] = h1_v[mine, :]


def mlp_own(where, *args):
    full = ((SEQ, D), bf16)
    units = args[7].shape[1] + BLK
    return call(
        mlp_own_kernel,
        "mlp_own",
        where,
        [Near(a) for a in args],
        [((SEQ // 2, D), f32), full, ((SEQ, 128), f32), full, full, full],
        [((D, BLK), bf16), ((BLK, D), bf16), ((SEQ, D), f32), *unit_scratch(units, 512)],
        1,
        flops=1,
        near=6,
    )


def mlp_peer_kernel(where, u2, dy, m_in, du_in, *refs):
    ups, downs, refs = refs[:3], refs[3:6], refs[6:]
    wo_own_in, wo_peer_in, m_mine, m_other, du_out, wo = refs[:6]
    m_v, up, down, g_v, df_v, f_v, da_v, sems = refs[6:]
    moves = Moves(sems)
    for source, target in (
        (wo_own_in, wo.at[0]),
        (wo_peer_in, wo.at[1]),
    ):
        moves.store(source, target)

    def put(i, cols, m, du):
        at = rows_at(i)
        m_v[at, cols] = (m_in[at, cols].astype(f32) + m).astype(bf16)
        du_out[at, cols] = (du_in[at, cols].astype(f32) + du).astype(bf16)

    unpack_units(ups, downs, up, down)
    unit_blocks(u2, dy, [(up, down, [2 * BLK, BLK], None)], g_v, df_v, f_v, da_v, put)
    split_halves(where[2], m_v, m_mine, m_other)
    moves.finish()


def split_halves(side, values, mine, other):
    half = SEQ // 2
    mine[...] = values[pl.ds(pl.multiple_of(side * half, half), half), :]
    other[...] = values[pl.ds(pl.multiple_of((1 - side) * half, half), half), :]


def mlp_peer(where, near, kept):
    full = ((SEQ, D), bf16)
    half = ((SEQ // 2, D), bf16)
    units = 3 * BLK
    return call(
        mlp_peer_kernel,
        "mlp_peer",
        where,
        [Near(a) for a in near] + [*kept],
        [half, half, full, ((2, COLS, D), bf16)],
        [full, ((D, units), bf16), ((units, D), bf16), *unit_scratch(units, 2 * BLK)],
        2,
        flops=1,
        near=4,
    )


def turn_kernel(where, *refs):
    own, sib, n2, r2, dy, gain, wo = refs[:7]
    ot, stat, qt = refs[7:9], refs[9:11], refs[11:13]
    kv_own_in, units_near, w2_own_in, w2_peer_in = refs[13:17]
    e_in = refs[17:19]
    dh_out, dot_v, stat_v, dkv_v, e_last = refs[19:24]
    kv, dh_v, low_v, w2, sems = refs[24:]
    side = where[2]
    moves = Moves(sems)
    got_kv = once([moves.load(kv_own_in, kv.at[0])] + peer_prefix(moves, units_near, kv.at[1]))
    got_w2 = once([moves.load(w2_own_in, w2.at[0]), moves.load(w2_peer_in, w2.at[1])])
    for g in range(2):
        moves.store(e_in[g].at[TRI[-1] :], e_last.at[g])

    def norm(i):
        for part in range(4):
            at = slice(i * BLK + part * 64, i * BLK + part * 64 + 64)
            du = own[at, :].astype(f32) + sib[at, :].astype(f32)
            dh = dy[at, :].astype(f32) + norm_back(
                du, n2[at, :].astype(f32), r2[at, 0:1], gain[...]
            )
            dh_v[at, :] = dh
            low_v[at, :] = dh.astype(bf16)
            yield

    def grads(i, g):
        at = rows_at(i)
        do = dot_nt(low_v[at, :], wo[g])
        yield
        do_t = do.T
        yield
        for h in range(HEADS):
            scaled = do_t[head_rows(h)] * stat[g][h, PREFIX_ROWS : PREFIX_ROWS + 1, at]
            dot_v[g, head_rows(h), at] = scaled.astype(bf16)
            balance = jnp.sum(
                scaled * ot[g][head_rows(h), at].astype(f32), axis=0, keepdims=True
            )
            stat_v[g, h, PREFIX_ROWS:, at] = jnp.broadcast_to(balance, (8, BLK))
            yield

    def prefix(g, h):
        got_kv()
        pv = kv[g, PREFIX_ROWS:]
        pv = jnp.where(
            lax.broadcasted_iota(jnp.int32, pv.shape, 1) // HD == h, pv, jnp.zeros_like(pv)
        )
        ep = stat[g][h, :PREFIX_ROWS, :]
        dp = dot_nn(pv, dot_v[g])
        dpv = dot_nt(ep.astype(bf16), dot_v[g, head_rows(h), :])
        yield
        grad = ep * (dp - stat_v[g, h, PREFIX_ROWS : PREFIX_ROWS + 1, :])
        stat_v[g, h, :PREFIX_ROWS, :] = grad
        yield
        dpk = dot_nt(grad.astype(bf16), qt[g][head_rows(h), :])
        yield
        low = 2 * g * PREFIX_ROWS
        dkv_v[low : low + PREFIX_ROWS, head_rows(h)] = dpk * (1.0 / LOG2E)
        dkv_v[low + PREFIX_ROWS : low + 2 * PREFIX_ROWS, head_rows(h)] = dpv

    drain(norm(0))
    for i in range(NBLK):
        drain(grads(i, 0), grads(i, 1), *([norm(i + 1)] if i + 1 < NBLK else []))
    drain(*[prefix(g, h) for g in range(2) for h in range(HEADS)])
    got_w2()
    da = 0.0
    for n in range(4):
        grad = dkv_v[n * PREFIX_ROWS : (n + 1) * PREFIX_ROWS, :].astype(bf16)
        da = da + dot_nt(grad, w2[n // 2, :, (n % 2) * COLS : (n % 2 + 1) * COLS])
    dkv_v[4 * PREFIX_ROWS : 5 * PREFIX_ROWS, :] = da[:, :COLS]
    dkv_v[5 * PREFIX_ROWS :, :] = da[:, COLS:]
    half = SEQ // 2
    dh_out[...] = dh_v[pl.ds(pl.multiple_of(side * half, half), half), :]
    moves.finish()


def turn(where, near, small, es):
    return call(
        turn_kernel,
        "turn",
        where,
        [Near(a) for a in near] + [*small, *es],
        [
            ((SEQ // 2, D), f32),
            ((2, COLS, SEQ), bf16),
            ((2, HEADS, PREFIX_ROWS + 8, SEQ), f32),
            ((6 * PREFIX_ROWS, COLS), f32),
            ((2, SEQ, LANES), bf16),
        ],
        [
            ((2, 2 * PREFIX_ROWS, COLS), bf16),
            ((SEQ, D), f32),
            ((SEQ, D), bf16),
            ((2, 2 * COLS, 2 * COLS), bf16),
        ],
        6,
        flops=6 * 10**9,
        near=5,
    )


def attend_back_kernel(where, *refs):
    do_t, e_last, stat = refs[:3]
    qt, v, kt, e_in = refs[3:5], refs[5:7], refs[7:9], refs[9:11]
    kv_own_in, units_near, x_in, w_own_in, w_peer_in = refs[11:16]
    mine_out, other_out, x_v, e, kv, dkt, dvt, du_v, ds_v, w, sems = refs[16:]
    slot, side = where[0], where[2]
    half = SEQ // 2
    moves = Moves(sems)
    kv_loads = [moves.load(kv_own_in, kv.at[0])] + peer_prefix(moves, units_near, kv.at[1])
    w_loads = [moves.load(w_own_in, w.at[0]), moves.load(w_peer_in, w.at[1])]
    moves.store(x_in.at[pl.ds(pl.multiple_of(slot * SEQ + side * half, half), half)], x_v)

    def run(local):
        got_w = once(w_loads)
        spans = [(i, 1) if local else (0, i + 1) for i in range(NBLK)]
        last = NBLK - 1
        parts = Moves(sems)
        parts.used = moves.used
        e_got = {}
        for i in reversed(range(last)):
            at = slice(TRI[i], TRI[i] + spans[i][1] * BLK)
            for g in range(2):
                e_got[i, g, 0] = once([parts.load(e_in[g].at[at], e.at[g, at])])

        def weights(i, g, h, c):
            if i == last:
                return e_last[g, rows_at(c), head_lanes(h)]
            return e[g, TRI[i] + c * BLK : TRI[i] + (c + 1) * BLK, head_lanes(h)]

        once(kv_loads)()
        dqs = {}

        def slopes(n, i, g, h, first, count):
            here = rows_at(i)
            do_h = do_t[g, :, here]
            do_h = jnp.where(
                lax.broadcasted_iota(jnp.int32, do_h.shape, 0) // HD == h, do_h, jnp.zeros_like(do_h)
            )
            balance = stat[g, h, PREFIX_ROWS : PREFIX_ROWS + 1, here]
            if (i, g, h) in e_got:
                e_got[i, g, h]()
            for c in range(count):
                dp = dot_nn(v[g][rows_at(first + c), :], do_h)
                e_low = weights(i, g, h, c)
                ds_v[n % 2, rows_at(c), :] = (e_low.astype(f32) * (dp - balance)).astype(bf16)
                yield

        def use(n, i, g, h, first, count):
            heads, here = head_rows(h), rows_at(i)
            pk_t = kv[g, :PREFIX_ROWS].astype(f32).T.astype(bf16)
            dq = dot_nn(pk_t[heads], stat[g, h, :PREFIX_ROWS, here].astype(bf16))
            for c in range(count):
                at = rows_at(first + c)
                e_low = weights(i, g, h, c)
                ds = ds_v[n % 2, rows_at(c), :]
                dv = dot_nt(do_t[g, heads, here], e_low)
                dk = dot_nt(qt[g][heads, here], ds)
                if local or i == last:
                    dvt[g, heads, at] = dv
                    dkt[g, heads, at] = dk
                else:
                    dvt[g, heads, at] += dv
                    dkt[g, heads, at] += dk
                dq = dq + dot_nn(kt[g][heads, at], ds)
                yield
            dqs[i, g, h] = dq

        def share(i):
            here = rows_at(i)
            grads = []
            for g in range(2):
                dq = jnp.concatenate([dqs.pop((i, g, h)) for h in range(HEADS)], axis=0)
                for value, scale in ((dq, SCALE), (dkt[g, :, here], 1.0 / LOG2E), (dvt[g, :, here], 1.0)):
                    grads.append((value.T * scale).astype(bf16))
                    yield
            got_w()
            for c in range(D // BLK):
                total = None
                for g in range(2):
                    for part in range(3):
                        term = dot_nt(grads[3 * g + part], w[g, part, rows_at(c), :])
                        total = term if total is None else total + term
                du_v[here, rows_at(c)] = total.astype(bf16)
                yield

        units = []
        for i in reversed(range(NBLK)):
            for g in range(2):
                for h in range(HEADS):
                    units.append((len(units), i, g, h, *spans[i]))
        tail = iter(())
        drain(slopes(*units[0]))
        for n, unit in enumerate(units):
            i, g, h = unit[1:4]
            ahead = [slopes(*units[n + 1])] if n + 1 < len(units) else []
            for _ in weave(*ahead, use(*unit)):
                next(tail, None)
            if g == 1 and h == HEADS - 1:
                drain(tail)
                tail = share(i)
        drain(tail)

    bucket = where[3]

    @pl.when(bucket == 0)
    def _():
        run(True)

    @pl.when(bucket != 0)
    def _():
        run(False)

    split_halves(side, du_v, mine_out, other_out)
    moves.finish()


def attend_back(where, near, es, kv_own, units_near, x, w_own, w_peer):
    half = ((SEQ // 2, D), bf16)
    return call(
        attend_back_kernel,
        "attend_back",
        where,
        [Near(a) for a in near] + [*es, kv_own, units_near, x, w_own, w_peer],
        [half, half, half],
        [
            ((2, TRI[-1], LANES), bf16),
            ((2, 2 * PREFIX_ROWS, COLS), bf16),
            ((2, COLS, SEQ), f32),
            ((2, COLS, SEQ), f32),
            ((SEQ, D), bf16),
            ((2, SEQ, BLK), bf16),
            ((2, 3, D, COLS), bf16),
        ],
        18,
        flops=16 * 10**9,
        near=3,
    )


def finish_kernel(where, own, sib, x, dh, gain, out, out_v, sems):
    moves = Moves(sems)
    size = 64
    for n in range(SEQ // 2 // size):
        at = slice(n * size, (n + 1) * size)
        normed, inv = norm_rows(x[at, :].astype(f32))
        du = own[at, :].astype(f32) + sib[at, :].astype(f32)
        out_v[at, :] = dh[at, :] + norm_back(du, normed, inv, gain[...])
        moves.store(out_v.at[at], out.at[at])
    moves.finish()


def finish(where, *args):
    wide = ((SEQ // 2, D), f32)
    return call(finish_kernel, "finish", where, [Near(a) for a in args], [wide], [wide], 8)[0]


def result_kernel(where, h1, own, sib, after, out, out_v, sems):
    moves = Moves(sems)
    size = 64
    for n in range(SEQ // 2 // size):
        at = slice(n * size, (n + 1) * size)
        out_v[at, :] = (h1[at, :] + (own[at, :].astype(f32) + sib[at, :].astype(f32))).astype(bf16)
        moves.store(out_v.at[at], out.at[at])
    moves.finish()


def result(where, h1, own, sib, after):
    half = ((SEQ // 2, D), bf16)
    return call(
        result_kernel, "result", where, [Near(h1), Near(own), Near(sib), Loose(after)], [half], [half], 8
    )[0]


def swap(values, axis, bit):
    size = lax.axis_size(axis)
    return lax.ppermute(values, axis, [(n, n ^ bit) for n in range(size)])


def after(values, *others):
    return lax.optimization_barrier((values, *others))[0]


def other_half(values, side):
    half = values.shape[0] // 2
    return lax.dynamic_slice_in_dim(values, (1 - side) * half, half, 0)


def on_device(
    inputs,
    buckets,
    ln1_gain,
    ln1_bias,
    w_qkv,
    w_out,
    ln2_gain,
    ln2_bias,
    w_up,
    w_down,
    prefix_embed,
    prefix_w1,
    prefix_b1,
    prefix_w2,
    prefix_b2,
    cotangent,
):
    prefix_count = prefix_embed.shape[0]
    width = prefix_w1.shape[1]
    member = lax.axis_index("tensor")
    place = lax.axis_index("batch") & 3
    side = member & 1
    slot = member // 2
    w = w_qkv.transpose(1, 0, 2)
    w2_flat = prefix_w2.reshape(width, 2 * COLS)
    gain1, bias1 = ln1_gain.reshape(1, D), ln1_bias.reshape(1, D)
    gain2, bias2 = ln2_gain.reshape(1, D), ln2_bias.reshape(1, D)
    embed = jnp.pad(prefix_embed, ((0, PREFIX_ROWS - prefix_count), (0, 0)))

    def across(values):
        return swap(values, "tensor", 2)

    first_near = across(pack(w, w_out))
    hidden, kv_own, up_near, down_near, up_far, down_far = prefix_forward(
        embed,
        prefix_w1,
        prefix_b1.reshape(1, width),
        w2_flat,
        prefix_b2.reshape(1, 2 * COLS),
        w_up,
        w_down,
    )
    where = jnp.stack([slot, place, side, after(buckets, kv_own)[slot]]).astype(jnp.int32)
    up_near = across(up_near)
    down_near = across(after(down_near, first_near))
    first_beside = swap(first_near, "batch", 1)
    first_above = swap(first_near, "batch", 2)
    e0, qt0, kt0, v0, ot0, stat0, x, u1, part, dy, down = attend(
        where,
        0,
        (after(inputs, first_near), gain1, bias1, w, w_out, kv_own, cotangent, w_down),
    )
    half = first_near.shape[0] // 2
    first_top = swap(after(first_above, u1)[:half], "batch", 1)
    first_bottom = swap(after(first_beside, u1)[half:], "batch", 2)
    first = (first_near, first_beside, first_above, first_top, first_bottom)
    up_sent = after(up_near, u1)
    up_far = across(after(up_far, u1))
    up_beside = swap(up_sent, "batch", 1)
    up_above = swap(up_sent, "batch", 2)
    da = cotangent_units(where, after(dy, first_beside, first_above), down)
    e1, w_peer, wo_peer, qt1, kt1, v1, ot1, stat1, part, up = attend(
        where,
        1,
        (*[Near(a) for a in (u1, *first, up_near, after(part, da, down_near))], w_up),
    )
    part_sib = swap(after(part, up_beside, up_above, up_far), "tensor", 1)
    down_sent = after(down_near, part)
    down_beside = swap(down_sent, "batch", 1)
    down_above = swap(down_sent, "batch", 2)
    down_far = across(after(down_far, part))
    h1, n2, r2, u2, m, du = mlp_own(
        where, x, part, part_sib, gain2, bias2, dy, da, up, down, up_near, down_near
    )
    w2_peer = across(after(w2_flat, part))
    m_mine, m_other, du, wo_pair = mlp_peer(
        where,
        (u2, dy, m, du, up_beside, up_above, up_far, down_beside, down_above, down_far),
        (w_out, wo_peer),
    )
    du_sib = swap(after(du, w2_peer), "tensor", 1)
    m_sib = swap(m_other, "tensor", 1)
    dh, do_t, stat, dkv, e_last = turn(
        where,
        (du, du_sib, n2, r2, dy, gain2, wo_pair, ot0, ot1, stat0, stat1, qt0, qt1),
        (kv_own, Loose(up_near), w2_flat, Loose(w2_peer)),
        (e0, e1),
    )

    dkv_peer = across(dkv)
    output = result(where, h1, m_mine, m_sib, dkv)
    dkv_peer = after(dkv_peer, output)
    rows = 2 * PREFIX_ROWS
    sums = jnp.concatenate(
        [dkv[:rows] + dkv_peer[rows : 2 * rows], dkv[2 * rows :] + dkv_peer[2 * rows :]], axis=0
    )
    bits = [1 << n for n in reversed(range(lax.axis_size("batch").bit_length() - 1))]
    sums_away = swap(sums, "batch", bits[0])
    du1_mine, du1_other, x = attend_back(
        where,
        (after(do_t, sums), e_last, stat, qt0, qt1, v0, v1, kt0, kt1),
        (e0, e1),
        kv_own,
        Loose(up_near),
        inputs,
        w,
        w_peer,
    )
    du1_sib = swap(after(du1_other, sums_away), "tensor", 1)
    sums = sums + after(sums_away, du1_mine)
    for bit in bits[1:-2]:
        sums = sums + swap(sums, "batch", bit)
    away = [swap(sums, "batch", pair) for pair in (1, 2, 3)]
    input_grad = finish(where, du1_mine, after(du1_sib, sums), x, dh, gain1)
    away = lax.optimization_barrier((*away, input_grad))
    sums = (sums + away[0]) + (away[1] + away[2])
    da = sums[rows:] + swap(sums[rows:], "tensor", 1)
    w2_grad, b2_grad, embed_grad, w1_grad, b1_grad = prefix_back(
        sums[:rows], da, hidden, embed, prefix_w1
    )
    return (
        output,
        input_grad,
        embed_grad[:prefix_count],
        w1_grad,
        b1_grad.reshape(width),
        w2_grad,
        b2_grad,
    )


def solution(mesh):
    placed = (
        P("batch", None),
        P("batch"),
        P(),
        P(),
        P(None, None, "tensor"),
        P("tensor", None),
        P(),
        P(),
        P(None, "tensor"),
        P("tensor", None),
        P(),
        P(),
        P(),
        P(None, None, "tensor"),
        P(None, "tensor"),
        P("batch", None),
    )
    return jax.shard_map(
        on_device,
        mesh=mesh,
        in_specs=placed,
        out_specs=(
            P(("batch", "tensor"), None),
            P(("batch", "tensor"), None),
            P(),
            P(),
            P(),
            P(None, None, "tensor"),
            P(None, "tensor"),
        ),
        check_vma=False,
    )
```
